512 devices in a mesh: tm: 16 (over x, y), node: 32 (over z, core).
Axes of the slice: x: 4, y: 4, z: 16, core: 2. Of those that a mesh axis runs over, the one named last changes fastest.
Arguments:
- message: bfloat16 [131072, 512], P(('tm', 'node')), may hold values from -6 to 6
- dest_mem: bfloat16 [131072, 512], P(('tm', 'node')), may hold values from -6 to 6
- nbr_rows: bfloat16 [786432, 512], P(('tm', 'node')), may hold values from -6 to 6
- emb_grad: bfloat16 [131072, 512], P(('tm', 'node')), may hold values from -6 to 6
- event_time: int32 [131072], P(('tm', 'node')), may hold values from 1000 to 1999
- nbr_time: int32 [131072, 6], P(('tm', 'node')), may hold values from 0 to 999
- nbr_count: int32 [131072], P(('tm', 'node')), may hold values from 1 to 6
- source_id: int32 [131072], P(('tm', 'node')), may hold values from 0 to 1023
- dest_local: int32 [131072], P(('tm', 'node')), may hold values from 0 to 31
- read_owner: int32 [786432, 1], P(('tm', 'node')), may hold values from 0 to 15; in each aligned block of 1536 rows (0 to 1535, 1536 to 3071, ...) at most 192 rows name the same one
- read_row: int32 [786432], P(('tm', 'node')), may hold values from 0 to 31
- w_in: bfloat16 [512, 1536], P('node'), may hold values from -0.25 to 0.25
- w_hid: bfloat16 [512, 1536], P('node'), may hold values from -0.25 to 0.25
- w_query: bfloat16 [512, 512], P('node'), may hold values from -0.25 to 0.25
- w_keyval: bfloat16 [512, 1024], P('node'), may hold values from -0.25 to 0.25
- w_out: bfloat16 [512, 512], P('node'), may hold values from -0.25 to 0.25
Outputs:
- version_grad: float32 [16384, 512], P(('tm', 'node'))
- node_grad: float32 [16, 1024, 512], P('tm', 'node')
The draws below stay inside these ranges and needn't reach their ends.
Inputs may be any that keep to these rules, and one draw needn't show every extreme that they name: `read_owner`: no owner group is named by more than 192 of the reads of one device.
All inputs are finite; a program needn't handle non-finite values.
Results may differ from the reference program's by a relative error of at most 0.015.
Values may be sent and summed in bfloat16 or wider, within the bound.
A program may use at most 64 MiB of HBM per device.

```python
import math
import jax
import jax.numpy as jnp
import numpy as np
from jax import lax

D = 512
HEADS = 2
NBR = 6
EV_DEV = 256
NODE_DEV = 32
VER_DEV = 32
NODES = 1024
EVENTS = 131072
READS_DEV = 1536
READS = 786432
VERSIONS = 16384
CAP = 192
N_TM = 16
N_NODE = 32


def touch_ends(result, stream_key, least, largest):
    spot = [jax.random.randint(jax.random.fold_in(stream_key, axis), (), 0, length) for axis, length in enumerate(result.shape)]
    main_axis = result.shape.index(max(result.shape))
    next_to = spot[:main_axis] + [(spot[main_axis] + 1) % result.shape[main_axis]] + spot[main_axis + 1:]
    return result.at[tuple(spot)].set(least).at[tuple(next_to)].set(largest)


def level_of(rng, extent, cuts, low, high):
    factor_of = 1.0
    for position, blocks in cuts:
        draws = jax.random.uniform(jax.random.fold_in(jax.random.fold_in(rng, 6), position), (blocks,), jnp.float32, low / len(cuts), high / len(cuts))
        factor_of = factor_of * jnp.repeat(jnp.exp(draws), extent[position] // blocks).reshape((-1,) + (1,) * (len(extent) - 1 - position))
    return factor_of


def rank_table(amount, lean):
    loads = [(1 << 20) // math.isqrt(rank ** lean) + 1 for rank in range(1, amount + 1)]
    width = 1 + sum(loads) // (1 << 30)
    return np.cumsum(np.array([max(1, weight // width) for weight in loads]))


def ranked_ids(own_key, dims, number_of, skew):
    table = rank_table(number_of, skew)
    lot = jax.random.randint(jax.random.fold_in(own_key, 1), dims, 0, int(table[number_of - 1]))
    grade = jnp.searchsorted(jnp.asarray(table, jnp.int32), lot, side="right")
    return jax.random.permutation(jax.random.fold_in(own_key, 2), number_of)[grade].astype(jnp.int32)


def deal_out(rng, own, number, rows, count, top, reach, slope):
    sequence = jax.random.permutation(rng, count)
    crowded, ordinary = load_shares(count, rows * top, reach, slope, True), load_shares(count, rows * top, reach, slope, False)
    places = jnp.arange(count)

    def named(tallies, rotation):
        used = int((tallies > 0).sum())
        fixed = max(1, used // 4)
        passed = fixed + (places - fixed + rotation * (used - fixed)) % max(1, count - fixed)
        return jnp.zeros((count,), jnp.int32).at[sequence[jnp.where(places < fixed, places, passed)]].set(jnp.asarray(tallies, jnp.int32))

    tallies = jnp.where(number % 4 == 0, named(crowded, number // 4), named(ordinary, number - number // 4 - 1))
    mixed = jax.random.permutation(jax.random.fold_in(own, 3), count)
    donor, receiver = mixed[0:count // 2 * 2:2], mixed[1:count // 2 * 2:2]
    margin = jnp.minimum(tallies[donor] - 1, reach - tallies[receiver]) // 2
    margin = jnp.where((donor == sequence[0]) | (receiver == sequence[0]) | (tallies[receiver] == 0), 0, jnp.maximum(margin, 0))
    passed = jax.random.randint(jax.random.fold_in(own, 4), (count // 2,), 0, 1 << 20) % (margin + 1)
    tallies = tallies.at[donor].add(-passed).at[receiver].add(passed)
    items = jnp.searchsorted(jnp.cumsum(tallies), jnp.arange(rows * top), side="right").astype(jnp.int32)
    grid = items.reshape(top, rows).T
    grid = grid[jax.random.permutation(jax.random.fold_in(own, 1), rows)]
    rotation = jax.random.randint(jax.random.fold_in(own, 2), (rows, 1), 0, top)
    return jnp.take_along_axis(grid, (jnp.arange(top)[None, :] + rotation) % top, axis=1)


def load_shares(amount, total, most, skew, full):
    portions = [(1 << 20) // math.isqrt(standing ** skew) + 1 for standing in range(1, amount + 1)]
    largest = most if full else min(most, max(-(-total // amount), total * portions[0] // sum(portions)))
    least = 1 if total - largest >= amount - 1 else 0
    holding, surplus = [largest] + [least] * (amount - 1), total - largest - least * (amount - 1)
    while surplus > 0:
        candidates = [i for i in range(1, amount) if holding[i] < largest] or [i for i in range(1, amount) if holding[i] < most]
        mass, remaining = sum([portions[i] for i in candidates]), surplus
        for i in candidates:
            extra = min(most - holding[i], max(1, remaining * portions[i] // mass), surplus)
            holding[i] = holding[i] + extra
            surplus = surplus - extra
    return np.array(holding)


def gaussian(key, dims, scale, reach, cuts=(), kind=jnp.bfloat16):
    gain = level_of(key, dims, cuts, -0.22, 0.18) if cuts else 1.0
    drawn = jax.random.normal(key, dims, jnp.float32) * scale * gain
    return jnp.minimum(jnp.maximum(drawn, -reach), reach).astype(kind)


def setup_inputs(seed: int = 0) -> dict:
    arg_keys = jax.random.split(jax.random.key(seed), 17)
    message = gaussian(arg_keys[0], (EVENTS, D), 1.0, 6.0, ((0, 512),))
    dest_mem = gaussian(arg_keys[1], (EVENTS, D), 1.0, 6.0, ((0, 512),))
    nbr_rows = gaussian(arg_keys[2], (READS, D), 1.0, 6.0, ((0, 512),))
    emb_grad = gaussian(arg_keys[3], (EVENTS, D), 1.0, 6.0, ((0, 512),))
    event_time = touch_ends(jax.random.randint(arg_keys[4], (EVENTS,), 1000, 2000), jax.random.fold_in(arg_keys[4], 1), 1000, 1999).astype(jnp.int32)
    nbr_time = touch_ends(jax.random.randint(arg_keys[5], (EVENTS, NBR), 0, 1000), jax.random.fold_in(arg_keys[5], 1), 0, 999).astype(jnp.int32)
    nbr_count = touch_ends(jax.random.randint(arg_keys[6], (EVENTS,), 1, NBR + 1), jax.random.fold_in(arg_keys[6], 1), 1, NBR).astype(jnp.int32)
    source_id = touch_ends(ranked_ids(arg_keys[7], (EVENTS,), NODES, 2), jax.random.fold_in(arg_keys[7], 3), 0, NODES - 1).astype(jnp.int32)
    dest_local = touch_ends(jax.random.randint(arg_keys[8], (EVENTS,), 0, NODE_DEV), jax.random.fold_in(arg_keys[8], 1), 0, NODE_DEV - 1).astype(jnp.int32)
    read_owner_keys = jax.random.split(jax.random.fold_in(arg_keys[9], 1), READS // READS_DEV)
    read_owner_turns = jax.random.permutation(jax.random.fold_in(arg_keys[9], 3), READS // READS_DEV)
    read_owner = jax.vmap(lambda own, number: deal_out(jax.random.fold_in(arg_keys[9], 2), own, number, READS_DEV, N_TM, 1, CAP, 2))(read_owner_keys, read_owner_turns).reshape((READS, 1))
    read_row = touch_ends(jax.random.randint(arg_keys[10], (READS,), 0, VER_DEV), jax.random.fold_in(arg_keys[10], 1), 0, VER_DEV - 1).astype(jnp.int32)
    w_in = gaussian(arg_keys[11], (D, 3 * D), D ** -0.5, 0.25, ((0, 32),))
    w_hid = gaussian(arg_keys[12], (D, 3 * D), D ** -0.5, 0.25, ((0, 32),))
    w_query = gaussian(arg_keys[13], (D, D), D ** -0.5, 0.25, ((0, 32),))
    w_keyval = gaussian(arg_keys[14], (D, 2 * D), D ** -0.5, 0.25, ((0, 32),))
    w_out = gaussian(arg_keys[15], (D, D), D ** -0.5, 0.25, ((0, 32),))
    return {"message": message, "dest_mem": dest_mem, "nbr_rows": nbr_rows, "emb_grad": emb_grad, "event_time": event_time, "nbr_time": nbr_time, "nbr_count": nbr_count, "source_id": source_id, "dest_local": dest_local, "read_owner": read_owner, "read_row": read_row, "w_in": w_in, "w_hid": w_hid, "w_query": w_query, "w_keyval": w_keyval, "w_out": w_out}


def embed_events(message, dest_mem, key_in, slot_mask, weights):
    w_in, w_hid, w_query, w_keyval, w_out = weights
    features = message.shape[1]
    events = message.shape[0]
    neighbours = key_in.shape[1]
    head_size = features // HEADS
    gate_in = jnp.dot(message, w_in, preferred_element_type=jnp.float32)
    gate_hid = jnp.dot(dest_mem, w_hid, preferred_element_type=jnp.float32)
    reset_gate = jax.nn.sigmoid(gate_in[:, :features] + gate_hid[:, :features])
    update_gate = jax.nn.sigmoid(gate_in[:, features:2 * features] + gate_hid[:, features:2 * features])
    candidate = jnp.tanh(gate_in[:, 2 * features:] + reset_gate * gate_hid[:, 2 * features:])
    memory = ((1.0 - update_gate) * candidate + update_gate * dest_mem.astype(jnp.float32)).astype(jnp.bfloat16)
    queries = jnp.dot(memory, w_query, preferred_element_type=jnp.float32).astype(jnp.bfloat16)
    queries = queries.reshape(events, HEADS, head_size)
    keyval = jnp.dot(key_in.reshape(events * neighbours, features), w_keyval, preferred_element_type=jnp.float32)
    keyval = keyval.astype(jnp.bfloat16).reshape(events, neighbours, 2, HEADS, head_size)
    score_scale = 1.0 / math.sqrt(head_size)
    scores = jnp.einsum('eah,ejah->eaj', queries.astype(jnp.float32), keyval[:, :, 0].astype(jnp.float32)) * score_scale
    weight_raw = jnp.exp(scores) * slot_mask[:, None, :]
    attn_weights = (weight_raw / lax.optimization_barrier(jnp.sum(weight_raw, axis=2, keepdims=True))).astype(jnp.bfloat16)
    attended = jnp.einsum('eaj,ejah->eah', attn_weights.astype(jnp.float32), keyval[:, :, 1].astype(jnp.float32))
    attended = attended.astype(jnp.bfloat16).reshape(events, features)
    return jnp.dot(attended, w_out, preferred_element_type=jnp.float32) + memory.astype(jnp.float32)

def backward(message, dest_mem, nbr_rows, emb_grad, event_time, nbr_time, nbr_count, weights):
    events = message.shape[0]
    features = message.shape[1]
    neighbours = nbr_time.shape[1]
    frequency = jnp.exp(jnp.arange(features, dtype=jnp.float32) * (-9.0 * math.log(10.0) / features))
    time_gap = (event_time[:, None] - nbr_time).astype(jnp.float32)
    time_code = jnp.cos(time_gap[:, :, None] * frequency[None, None, :])
    key_in = (nbr_rows.reshape(events, neighbours, features).astype(jnp.float32) + time_code).astype(jnp.bfloat16)
    slot_mask = (jnp.arange(neighbours, dtype=jnp.int32)[None, :] < nbr_count[:, None]).astype(jnp.float32)

    def local_embed(msg_part, dest_part, key_part):
        return embed_events(msg_part, dest_part, key_part, slot_mask, weights)
    _, pullback = jax.vjp(local_embed, message, dest_mem, key_in)
    grad_message, grad_dest, grad_key = pullback(emb_grad.astype(jnp.float32))
    return (grad_message, grad_dest, grad_key.reshape(events * neighbours, features))

def reference(message, dest_mem, nbr_rows, emb_grad, event_time, nbr_time, nbr_count, source_id, dest_local, read_owner, read_row, w_in, w_hid, w_query, w_keyval, w_out):
    weights = (w_in, w_hid, w_query, w_keyval, w_out)
    devices = N_TM * N_NODE
    blocks = (message.reshape(devices, EV_DEV, D), dest_mem.reshape(devices, EV_DEV, D), nbr_rows.reshape(devices, READS_DEV, D), emb_grad.reshape(devices, EV_DEV, D), event_time.reshape(devices, EV_DEV), nbr_time.reshape(devices, EV_DEV, NBR), nbr_count.reshape(devices, EV_DEV))

    def per_device(block):
        return backward(block[0], block[1], block[2], block[3], block[4], block[5], block[6], weights)
    grad_message, grad_dest, grad_read = lax.map(per_device, blocks)
    grad_read = grad_read.reshape(READS, D)
    read_device = jnp.arange(READS, dtype=jnp.int32) // READS_DEV
    version_ids = (read_owner[:, 0] * N_NODE + read_device % N_NODE) * VER_DEV + read_row
    version_grad = jax.ops.segment_sum(grad_read.astype(jnp.float32), version_ids, VERSIONS)
    event_device = jnp.arange(EVENTS, dtype=jnp.int32) // EV_DEV
    group_of = event_device // N_NODE
    source_ids = group_of * NODES + source_id
    dest_ids = group_of * NODES + event_device % N_NODE * NODE_DEV + dest_local
    node_ids = jnp.concatenate([source_ids, dest_ids]).astype(jnp.int32)
    both_grads = jnp.concatenate([grad_message.reshape(EVENTS, D), grad_dest.reshape(EVENTS, D)]).astype(jnp.float32)
    node_grad = jax.ops.segment_sum(both_grads, node_ids, N_TM * NODES).reshape(N_TM, NODES, D)
    return (version_grad, node_grad)
```

```python
import functools
import math

import jax
import jax.numpy as jnp
from jax import lax
from jax.experimental import pallas as pl
from jax.experimental.pallas import tpu as pltpu
from jax.sharding import PartitionSpec as P

D = 512
HEAD = 256
SLOTS = 6
EV = 256
READS = EV * SLOTS
OWN = 32
CA = 512
CB = 768
F32 = jnp.float32
BF16 = jnp.bfloat16
MESH = pl.DeviceIdType.MESH
FAR = ((5, 6, 7, 8), (9, 10, 11, 12), (1, 2, 3, 4), (13, 14, 15, 0))


def nn(a, b):
    return lax.dot_general(a, b, (((1,), (0,)), ((), ())), preferred_element_type=F32)


def nt(a, b):
    return lax.dot_general(a, b, (((1,), (1,)), ((), ())), preferred_element_type=F32)


def sigmoid(v):
    return 0.5 * jnp.tanh(0.5 * v) + 0.5


def cos_wide(angle):
    half = 0.5 * angle
    turns = jnp.floor(half * (1.0 / math.pi) + 0.5)
    s = (half - turns * 3.140625) - turns * (math.pi - 3.140625)
    q = s * s
    p = q * (-1.0 / 39916800.0) + (1.0 / 362880.0)
    p = p * q + (-1.0 / 5040.0)
    p = p * q + (1.0 / 120.0)
    p = p * q + (-1.0 / 6.0)
    p = p * q + 1.0
    sine = p * s
    return 1.0 - 2.0 * (sine * sine)


def cos_small(angle):
    q = angle * angle
    return 1.0 + q * (q * (1.0 / 24.0) - 0.5)


def kernel(
    msg, dst, nbr, emb, ev_time, nb_time, nb_count, src_id, dst_loc, owner, vrow,
    w_in, w_hid, w_q, w_kv, w_out,
    ver_out, node_out,
    wa, wb, rbuf, keys, gkb, qk, gv, ctx, gates, gmem, gin, gcand, gmsg, tcol, tpack, gwp, scp, wtp,
    vpart, vbuf, npart, nsib, nsend, nrecv, dpart,
    loc_sem, s1_send, s1_recv, r1_send, r2_send, piece_sem, sib_send, sib_recv,
    v_send, v_recv, nd_send, nd_recv, ring_send, ring_recv,
):
    tm = lax.axis_index("tm")
    node = lax.axis_index("node")
    x, y = tm // 4, tm % 4
    z, c = node // 2, node % 2
    other = 1 - c
    sibling = (tm, z * 2 + other)
    zq, zy = z // 4, z % 4

    def pick(p, q):
        return jnp.where(c == 0, p, q)

    a, b = pick(x, y), pick(y, x)

    def tm_of(aa, bb):
        return pick(aa * 4 + bb, bb * 4 + aa)

    a_left, a_right, a_far = (a + 3) % 4, (a + 1) % 4, (a + 2) % 4
    b_left, b_right, b_far = (b + 3) % 4, (b + 1) % 4, (b + 2) % 4
    dev_a_left, dev_a_right = (tm_of(a_left, b), node), (tm_of(a_right, b), node)
    dev_b_left, dev_b_right = (tm_of(a, b_left), node), (tm_of(a, b_right), node)

    bufs = ((wa, CA), (wb, CB))

    def share(ph, q):
        buf, width = bufs[ph]
        return buf.at[q, y, c, :, pl.ds(pl.multiple_of(x * width, 128), width)]

    blocks = (((w_kv, 0), (w_in, 0)), ((w_kv, CA), (w_in, CB)), ((w_out, 0), (w_hid, 0)), ((w_q, 0), (w_hid, CB)))
    for k, pair in enumerate(blocks):
        @pl.when(jnp.logical_and(zy == y, x == k))
        def _(pair=pair):
            for ph, (ref, at) in enumerate(pair):
                pltpu.make_async_copy(
                    ref.at[:, pl.ds(at, bufs[ph][1])], share(ph, zq), loc_sem.at[ph]
                ).start()

    barrier = pltpu.get_barrier_semaphore()

    def greet(k, carry):
        pl.semaphore_signal(barrier, inc=1, device_id=(tm, (node + 2 * k) % 32), device_id_type=MESH)
        pl.semaphore_signal(barrier, inc=1, device_id=((tm + k) % 16, node), device_id_type=MESH)
        return carry

    lax.fori_loop(1, 16, greet, 0)
    pl.semaphore_signal(barrier, inc=1, device_id=sibling, device_id_type=MESH)

    pl.semaphore_wait(barrier, 31)

    @pl.when(zy == y)
    def _():
        for ph in range(2):
            def send(k, carry, ph=ph):
                pltpu.make_async_remote_copy(
                    src_ref=share(ph, zq), dst_ref=share(ph, zq),
                    send_sem=s1_send.at[ph], recv_sem=s1_recv.at[ph, zq],
                    device_id=(tm, ((z + k) % 16) * 2 + c), device_id_type=MESH,
                ).start()
                return carry
            pltpu.make_async_copy(share(ph, zq), share(ph, zq), loc_sem.at[ph]).wait()
            lax.fori_loop(1, 16, send, 0)

    def stage1_wait(ph):
        for q in range(4):
            @pl.when(4 * q + y != z)
            def _(q=q):
                pltpu.make_async_copy(share(ph, q), share(ph, q), s1_recv.at[ph, q]).wait()

    def piece(ph, aa, bb, part=None):
        buf, width = bufs[ph]
        xx, yy = pick(aa, bb), pick(bb, aa)
        rows = pl.ds(0, 4) if part is None else pl.ds(2 * part, 2)
        return buf.at[rows, yy, c, :, pl.ds(pl.multiple_of(xx * width, 128), width)]

    def send_piece(ph, aa, bb, device, send_sem, part=None, slot=0):
        ref = piece(ph, aa, bb, part)
        pltpu.make_async_remote_copy(
            src_ref=ref, dst_ref=ref, send_sem=send_sem.at[ph],
            recv_sem=piece_sem.at[ph, aa * 4 + bb, slot],
            device_id=device, device_id_type=MESH,
        ).start()

    def wait_piece(ph, aa, bb, part=None, slot=0):
        ref = piece(ph, aa, bb, part)
        pltpu.make_async_copy(ref, ref, piece_sem.at[ph, aa * 4 + bb, slot]).wait()

    def to_sibling(ph, aa, bb):
        ref = piece(ph, aa, bb)
        pltpu.make_async_remote_copy(
            src_ref=ref, dst_ref=ref, send_sem=sib_send.at[ph], recv_sem=sib_recv.at[ph],
            device_id=sibling, device_id_type=MESH,
        ).start()

    def second_ring(ph, aa):
        send_piece(ph, aa, b, dev_b_left, r2_send)
        send_piece(ph, aa, b, dev_b_right, r2_send)
        to_sibling(ph, aa, b)

    def step0(ph):
        stage1_wait(ph)
        send_piece(ph, a, b, dev_a_left, r1_send)
        send_piece(ph, a, b, dev_a_right, r1_send)
        second_ring(ph, a)

    def step1(ph):
        wait_piece(ph, a_left, b)
        send_piece(ph, a_left, b, dev_a_right, r1_send, 0, 0)
        second_ring(ph, a_left)
        wait_piece(ph, a_right, b)
        send_piece(ph, a_right, b, dev_a_left, r1_send, 1, 1)
        second_ring(ph, a_right)

    def step2(ph):
        wait_piece(ph, a_far, b, 0, 0)
        wait_piece(ph, a_far, b, 1, 1)
        second_ring(ph, a_far)

    def step3(ph):
        for aa in (a, a_left, a_right, a_far):
            wait_piece(ph, aa, b_left)
            send_piece(ph, aa, b_left, dev_b_right, r2_send, 0, 0)
            to_sibling(ph, aa, b_left)
            wait_piece(ph, aa, b_right)
            send_piece(ph, aa, b_right, dev_b_left, r2_send, 1, 1)
            to_sibling(ph, aa, b_right)

    def step4(ph):
        for aa in (a, a_left, a_right, a_far):
            wait_piece(ph, aa, b_far, 0, 0)
            wait_piece(ph, aa, b_far, 1, 1)
            to_sibling(ph, aa, b_far)

    def all_here(ph):
        ref = bufs[ph][0].at[:, :, other]
        pltpu.make_async_copy(ref, ref, sib_recv.at[ph]).wait()

    def widen(i, carry):
        at = pl.ds(pl.multiple_of(i * 64, 64), 64)
        for t in range(4):
            rbuf[t, at, :] = nbr[at, t * 128 : (t + 1) * 128].astype(F32)
        return carry

    lax.fori_loop(0, READS // 64, widen, 0)
    tpack[0:6, :] = (ev_time[...] - nb_time[...]).astype(F32)
    tpack[6:7, :] = nb_count[...].astype(F32)
    tpack[7:8, :] = jnp.zeros((1, EV), F32)
    tcol[...] = jnp.transpose(tpack[...])
    lanes = lax.broadcasted_iota(jnp.int32, (1, D), 1).astype(F32)
    freq = jnp.exp(lanes * (-9.0 * math.log(10.0) / D))

    def make_keys(i, carry):
        at = pl.ds(pl.multiple_of(i * 16, 16), 16)
        gaps = tcol[at, :]
        for j in range(SLOTS):
            gap = gaps[:, j : j + 1]
            for t, cosine in enumerate((cos_wide, cos_wide, cos_small, cos_small)):
                cut = slice(t * 128, (t + 1) * 128)
                rows = rbuf[t, pl.ds(i * (16 * SLOTS) + j, 16, stride=SLOTS), :]
                keys[j, at, cut] = rows + cosine(gap * freq[:, cut])
        return carry

    lax.fori_loop(0, EV // 16, make_keys, 0)

    step0(0)
    step0(1)
    step1(0)
    step2(0)
    step1(1)
    step2(1)
    step3(0)
    step4(0)
    step3(1)

    all_here(0)

    def wide(ref, start, width):
        return ref[:, :, :, :, pl.ds(start, width)].reshape(D, width)

    gatt = nt(emb[...], wide(wa, 1024, 512)).astype(BF16)
    for h in range(2):
        gv[h] = nt(gatt[:, h * HEAD : (h + 1) * HEAD], wide(wa, 512 + h * HEAD, HEAD))

    lane16 = lax.broadcasted_iota(jnp.int32, (16, 128), 1)

    def row_dots(vec, out):
        def block(i, carry):
            at = pl.ds(pl.multiple_of(i * 16, 16), 16)
            acc = jnp.zeros((16, 128), F32)
            v0, v1 = vec[0, at, :], vec[1, at, :]
            for j in range(SLOTS):
                key = keys[j, at, :]
                for h, v in enumerate((v0, v1)):
                    prod = key * v
                    part = (prod[:, 0:128] + prod[:, 128:256]) + (prod[:, 256:384] + prod[:, 384:512])
                    acc = jnp.where(lane16 == h * SLOTS + j, jnp.sum(part, axis=1, keepdims=True), acc)
            out[at, :] = acc
            return carry
        lax.fori_loop(0, EV // 16, block, 0)

    row_dots(gv, gwp)

    step4(1)
    all_here(1)

    def gate(k):
        return (nn(msg[...], wide(wb, k * D, D)), nn(dst[...], wide(wb, 1536 + k * D, D)))

    gi, gh = gate(0)
    reset = sigmoid(gi + gh)
    gates[0] = reset
    gi, gh = gate(2)
    gates[3] = gh
    gates[2] = jnp.tanh(gi + gates[0] * gh)
    gi, gh = gate(1)
    update = sigmoid(gi + gh)
    gates[1] = update
    memory = ((1.0 - update) * gates[2] + update * dst[...].astype(F32)).astype(BF16)
    quer = nn(memory, wide(wa, 1536, 512)).astype(BF16)
    for h in range(2):
        qk[h] = nt(quer[:, h * HEAD : (h + 1) * HEAD], wide(wa, h * HEAD, HEAD))

    row_dots(qk, scp)

    lane = lax.broadcasted_iota(jnp.int32, (EV, 128), 1)
    slot = jnp.where(lane >= SLOTS, lane - SLOTS, lane).astype(F32)
    head0, head1 = lane < SLOTS, jnp.logical_and(lane >= SLOTS, lane < 2 * SLOTS)
    live = jnp.logical_and(lane < 2 * SLOTS, slot < tcol[:, 6:7])
    raw = jnp.where(live, jnp.exp(scp[...] * (1.0 / 16.0)), 0.0)

    def per_head(v):
        s0 = jnp.sum(jnp.where(head0, v, 0.0), axis=1, keepdims=True)
        s1 = jnp.sum(jnp.where(head1, v, 0.0), axis=1, keepdims=True)
        return jnp.where(head0, s0, s1)

    weight = raw / per_head(raw)
    gw = gwp[...]
    wtp[...] = weight
    scp[...] = weight * (gw - per_head(weight * gw)) * (1.0 / 16.0)

    def spread(i, carry):
        at = pl.ds(pl.multiple_of(i * 16, 16), 16)
        sc, wt = scp[at, :], wtp[at, :]
        for lo in (0, 256):
            cut = slice(lo, lo + 256)
            q0, q1, g0, g1 = qk[0, at, cut], qk[1, at, cut], gv[0, at, cut], gv[1, at, cut]
            c0 = jnp.zeros((16, 256), F32)
            c1 = jnp.zeros((16, 256), F32)
            for j in range(SLOTS):
                s0, s1 = sc[:, j : j + 1], sc[:, SLOTS + j : SLOTS + j + 1]
                w0, w1 = wt[:, j : j + 1], wt[:, SLOTS + j : SLOTS + j + 1]
                key = keys[j, at, cut]
                c0 = c0 + s0 * key
                c1 = c1 + s1 * key
                for half in range(0, 256, 128):
                    hs = slice(half, half + 128)
                    rbuf[(lo + half) // 128, pl.ds(i * (16 * SLOTS) + j, 16, stride=SLOTS), :] = (
                        (s0 * q0[:, hs] + s1 * q1[:, hs]) + (w0 * g0[:, hs] + w1 * g1[:, hs])
                    )
            ctx[0, at, cut] = c0.astype(BF16)
            ctx[1, at, cut] = c1.astype(BF16)
        return carry

    lax.fori_loop(0, EV // 16, spread, 0)

    def narrow(i, carry):
        at = pl.ds(pl.multiple_of(i * 64, 64), 64)
        for t in range(4):
            gkb[at, t * 128 : (t + 1) * 128] = rbuf[t, at, :].astype(BF16)
        return carry

    lax.fori_loop(0, READS // 64, narrow, 0)

    vid = owner[...] * OWN + vrow[...]
    for m in range(2):
        hot = (lax.broadcasted_iota(jnp.int32, (256, READS), 0) + 256 * m == vid).astype(F32).astype(BF16)
        sums = nn(hot, gkb[...]).astype(BF16)
        vpart[pl.ds(8 * m, 8)] = sums.reshape(8, OWN, D)

    def send_versions(k, carry):
        to = (tm + k) % 16
        pltpu.make_async_remote_copy(
            src_ref=vpart.at[to], dst_ref=vbuf.at[k - 1],
            send_sem=v_send, recv_sem=v_recv,
            device_id=(to, node), device_id_type=MESH,
        ).start()
        return carry

    lax.fori_loop(1, 16, send_versions, 0)

    gq = [nn(ctx[h], wide(wa, h * HEAD, HEAD)).astype(BF16) for h in range(2)]
    gmem[...] = emb[...].astype(F32) + (
        nt(gq[0], wide(wa, 1536, HEAD)) + nt(gq[1], wide(wa, 1536 + HEAD, HEAD))
    )

    def gru(i, carry):
        at = pl.ds(pl.multiple_of(i * 16, 16), 16)
        gm = gmem[at, :]
        r, u, cand, hc = gates[0, at, :], gates[1, at, :], gates[2, at, :], gates[3, at, :]
        gu = gm * (dst[at, :].astype(F32) - cand)
        gc = gm * (1.0 - u) * (1.0 - cand * cand)
        gin[at, 0:512] = (gc * hc * (r * (1.0 - r))).astype(BF16)
        gin[at, 512:1024] = (gu * (u * (1.0 - u))).astype(BF16)
        gin[at, 1024:1536] = gc.astype(BF16)
        gcand[at, :] = (gc * r).astype(BF16)
        gmem[at, :] = gm * u
        return carry

    lax.fori_loop(0, EV // 16, gru, 0)

    gmsg[...] = nt(gin[...], wide(wb, 0, 1536)).astype(BF16)

    def part_copy(g):
        ref_from, ref_to = npart.at[g, other], nsib.at[g]
        return pltpu.make_async_remote_copy(
            src_ref=ref_from, dst_ref=ref_to, send_sem=nd_send.at[g], recv_sem=nd_recv.at[g],
            device_id=sibling, device_id_type=MESH,
        )

    for g, offsets in enumerate(FAR):
        base = ((z + offsets[0]) % 16) * 64
        wanted = (lax.broadcasted_iota(jnp.int32, (256, EV), 0) + base) & 1023
        hot = (wanted == src_id[...]).astype(F32).astype(BF16)
        sums = nn(hot, gmsg[...]).astype(BF16).reshape(4, 2, OWN, D)
        npart[g, 0] = sums[:, 0]
        npart[g, 1] = sums[:, 1]
        part_copy(g).start()

    def mine(rel):
        for g, offsets in enumerate(FAR):
            if rel in offsets:
                k = offsets.index(rel)
                return npart[g, c, k].astype(F32) + nsib[g, k].astype(F32)

    def hop(way, s):
        to = (z + 15) % 16 if way == 0 else (z + 1) % 16
        return pltpu.make_async_remote_copy(
            src_ref=nsend.at[way, s], dst_ref=nrecv.at[way, s],
            send_sem=ring_send.at[way, s], recv_sem=ring_recv.at[way, s],
            device_id=(tm, to * 2 + c), device_id_type=MESH,
        )

    part_copy(0).wait()
    nsend[0, 0] = mine(8).astype(BF16)
    hop(0, 0).start()
    nsend[1, 0] = mine(7).astype(BF16)
    hop(1, 0).start()

    gdst = (nt(gin[:, 0:1024], wide(wb, 1536, 1024)) + nt(gcand[...], wide(wb, 2560, 512))) + gmem[...]
    hot = (lax.broadcasted_iota(jnp.int32, (OWN, EV), 0) == dst_loc[...]).astype(F32).astype(BF16)
    dpart[...] = nn(hot, gdst.astype(BF16))

    for g in range(1, 4):
        part_copy(g).wait()

    for s in range(1, 8):
        hop(0, s - 1).wait_recv()
        nsend[0, s] = (mine(8 + s) + nrecv[0, s - 1].astype(F32)).astype(BF16)
        hop(0, s).start()
        if s < 7:
            hop(1, s - 1).wait_recv()
            nsend[1, s] = (mine(7 - s) + nrecv[1, s - 1].astype(F32)).astype(BF16)
            hop(1, s).start()
        if s == 4:
            pltpu.make_async_copy(vbuf, vbuf, v_recv).wait()
            total = vpart[tm].astype(F32)
            for k in range(15):
                total = total + vbuf[k].astype(F32)
            ver_out[...] = total
    hop(0, 7).wait_recv()
    hop(1, 6).wait_recv()
    node_out[...] = (mine(0) + dpart[...]) + (nrecv[0, 7].astype(F32) + nrecv[1, 6].astype(F32))

    for s in range(8):
        hop(0, s).wait_send()
        if s < 7:
            hop(1, s).wait_send()
    pltpu.make_async_copy(vbuf, vbuf, v_send).wait()
    for ph, (buf, width) in enumerate(bufs):
        ref = buf.at[:, :, c]
        pltpu.make_async_copy(ref, ref, sib_send.at[ph]).wait()
        ref = buf.at[:, 0:3, c, :, 0:width]
        pltpu.make_async_copy(ref, ref, r1_send.at[ph]).wait()
        ref = buf.at[:, 0:3, c]
        pltpu.make_async_copy(ref, ref, r2_send.at[ph]).wait()

    @pl.when(zy == y)
    def _():
        ref = wa.at[:, 0, c, :, 0:1920]
        pltpu.make_async_copy(ref, ref, s1_send.at[0]).wait()
        ref = wb.at[0, 0:3, :, :, 0:1920]
        pltpu.make_async_copy(ref, ref, s1_send.at[1]).wait()


def body(
    message, dest_mem, nbr_rows, emb_grad, event_time, nbr_time, nbr_count, source_id, dest_local,
    read_owner, read_row, w_in, w_hid, w_query, w_keyval, w_out,
):
    vmem = pl.BlockSpec(memory_space=pltpu.VMEM)
    hbm = pl.BlockSpec(memory_space=pl.ANY)
    dma = pltpu.SemaphoreType.DMA
    scratch = [
        pltpu.VMEM((4, 4, 2, 16, 2048), BF16),
        pltpu.VMEM((4, 4, 2, 16, 3072), BF16),
        pltpu.VMEM((4, READS, 128), F32),
        pltpu.VMEM((SLOTS, EV, D), F32),
        pltpu.VMEM((READS, D), BF16),
        pltpu.VMEM((2, EV, D), F32),
        pltpu.VMEM((2, EV, D), F32),
        pltpu.VMEM((2, EV, D), BF16),
        pltpu.VMEM((4, EV, D), F32),
        pltpu.VMEM((EV, D), F32),
        pltpu.VMEM((EV, 3 * D), BF16),
        pltpu.VMEM((EV, D), BF16),
        pltpu.VMEM((EV, D), BF16),
        pltpu.VMEM((EV, 8), F32),
        pltpu.VMEM((8, EV), F32),
        pltpu.VMEM((EV, 128), F32),
        pltpu.VMEM((EV, 128), F32),
        pltpu.VMEM((EV, 128), F32),
        pltpu.VMEM((16, OWN, D), BF16),
        pltpu.VMEM((15, OWN, D), BF16),
        pltpu.VMEM((4, 2, 4, OWN, D), BF16),
        pltpu.VMEM((4, 4, OWN, D), BF16),
        pltpu.VMEM((2, 8, OWN, D), BF16),
        pltpu.VMEM((2, 8, OWN, D), BF16),
        pltpu.VMEM((OWN, D), F32),
        dma((2,)),
        dma((2,)),
        dma((2, 4)),
        dma((2,)),
        dma((2,)),
        dma((2, 16, 2)),
        dma((2,)),
        dma((2,)),
        dma,
        dma,
        dma((4,)),
        dma((4,)),
        dma((2, 8)),
        dma((2, 8)),
    ]
    version_grad, node_grad = pl.pallas_call(
        kernel,
        out_shape=(jax.ShapeDtypeStruct((OWN, D), F32), jax.ShapeDtypeStruct((OWN, D), F32)),
        in_specs=[vmem] * 11 + [hbm] * 5,
        out_specs=(vmem, vmem),
        scratch_shapes=scratch,
        compiler_params=pltpu.CompilerParams(
            collective_id=0, has_side_effects=True, vmem_limit_bytes=56 * 1024 * 1024
        ),
        cost_estimate=pl.CostEstimate(
            flops=4_000_000_000, bytes_accessed=8_000_000, transcendentals=1_000_000
        ),
    )(
        message, dest_mem, nbr_rows, emb_grad,
        event_time.reshape(1, EV), nbr_time.T, nbr_count.reshape(1, EV),
        source_id.reshape(1, EV), dest_local.reshape(1, EV),
        read_owner.reshape(1, READS), read_row.reshape(1, READS),
        w_in, w_hid, w_query, w_keyval, w_out,
    )
    return version_grad, node_grad[None]


def solution(mesh):
    both = P(("tm", "node"))
    in_specs = (
        (P(("tm", "node"), None),) * 4
        + (both, P(("tm", "node"), None), both, both, both, P(("tm", "node"), None), both)
        + (P("node", None),) * 5
    )
    out_specs = (P(("tm", "node"), None), P("tm", "node", None))
    return jax.shard_map(body, mesh=mesh, in_specs=in_specs, out_specs=out_specs, check_vma=False)
```

```python
import math

import jax
import jax.numpy as jnp
from jax import lax
from jax.experimental import pallas as pl
from jax.experimental.pallas import tpu as pltpu
from jax.sharding import PartitionSpec as P

D = 512
HEAD = 256
SLOTS = 6
EV = 256
READS = EV * SLOTS
OWN = 32
CA = 512
CB = 768
F32 = jnp.float32
BF16 = jnp.bfloat16
MESH = pl.DeviceIdType.MESH
FAR = ((5, 6, 7, 8), (9, 10, 11, 12), (1, 2, 3, 4), (13, 14, 15, 0))


def nn(a, b):
    return lax.dot_general(a, b, (((1,), (0,)), ((), ())), preferred_element_type=F32)


def nt(a, b):
    return lax.dot_general(a, b, (((1,), (1,)), ((), ())), preferred_element_type=F32)


def sigmoid(v):
    return 0.5 * jnp.tanh(0.5 * v) + 0.5


def cos_wide(angle):
    half = 0.5 * angle
    turns = jnp.floor(half * (1.0 / math.pi) + 0.5)
    s = (half - turns * 3.140625) - turns * (math.pi - 3.140625)
    q = s * s
    p = q * (-1.0 / 39916800.0) + (1.0 / 362880.0)
    p = p * q + (-1.0 / 5040.0)
    p = p * q + (1.0 / 120.0)
    p = p * q + (-1.0 / 6.0)
    p = p * q + 1.0
    sine = p * s
    return 1.0 - 2.0 * (sine * sine)


def cos_small(angle):
    q = angle * angle
    return 1.0 + q * (q * (1.0 / 24.0) - 0.5)


def kernel(
    msg, dst, nbr, emb, ev_time, nb_time, nb_count, src_id, dst_loc, owner, vrow,
    w_in, w_hid, w_q, w_kv, w_out,
    ver_out, node_out,
    wa, wb, rbuf, keys, gkb, qk, gv, ctx, gates, mem, gmem, gin, gcand, gmsg, tcol, tpack, gwp, scp, wtp,
    vpart, vbuf, npart, nsib, nsend, nrecv, dpart,
    loc_sem, s1_send, s1_recv, r1_send, r2_send, piece_sem, sib_send, sib_recv,
    v_send, v_recv, nd_send, nd_recv, ring_send, ring_recv,
):
    tm = lax.axis_index("tm")
    node = lax.axis_index("node")
    x, y = tm // 4, tm % 4
    z, c = node // 2, node % 2
    other = 1 - c
    sibling = (tm, z * 2 + other)
    zq, zy = z // 4, z % 4

    def pick(p, q):
        return jnp.where(c == 0, p, q)

    a, b = pick(x, y), pick(y, x)

    def tm_of(aa, bb):
        return pick(aa * 4 + bb, bb * 4 + aa)

    a_left, a_right, a_far = (a + 3) % 4, (a + 1) % 4, (a + 2) % 4
    b_left, b_right, b_far = (b + 3) % 4, (b + 1) % 4, (b + 2) % 4
    dev_a_left, dev_a_right = (tm_of(a_left, b), node), (tm_of(a_right, b), node)
    dev_b_left, dev_b_right = (tm_of(a, b_left), node), (tm_of(a, b_right), node)

    bufs = ((wa, CA), (wb, CB))

    def share(ph, q):
        buf, width = bufs[ph]
        return buf.at[q, y, c, :, pl.ds(pl.multiple_of(x * width, 128), width)]

    blocks = (((w_kv, 0), (w_in, 0)), ((w_kv, CA), (w_in, CB)), ((w_out, 0), (w_hid, 0)), ((w_q, 0), (w_hid, CB)))
    for k, pair in enumerate(blocks):
        @pl.when(jnp.logical_and(zy == y, x == k))
        def _(pair=pair):
            for ph, (ref, at) in enumerate(pair):
                pltpu.make_async_copy(
                    ref.at[:, pl.ds(at, bufs[ph][1])], share(ph, zq), loc_sem.at[ph]
                ).start()

    barrier = pltpu.get_barrier_semaphore()

    def greet(k, carry):
        pl.semaphore_signal(barrier, inc=1, device_id=(tm, (node + 2 * k) % 32), device_id_type=MESH)
        pl.semaphore_signal(barrier, inc=1, device_id=((tm + k) % 16, node), device_id_type=MESH)
        return carry

    lax.fori_loop(1, 16, greet, 0)
    pl.semaphore_signal(barrier, inc=1, device_id=sibling, device_id_type=MESH)

    pl.semaphore_wait(barrier, 31)

    @pl.when(zy == y)
    def _():
        for ph in range(2):
            def send(k, carry, ph=ph):
                pltpu.make_async_remote_copy(
                    src_ref=share(ph, zq), dst_ref=share(ph, zq),
                    send_sem=s1_send.at[ph], recv_sem=s1_recv.at[ph, zq],
                    device_id=(tm, ((z + k) % 16) * 2 + c), device_id_type=MESH,
                ).start()
                return carry
            pltpu.make_async_copy(share(ph, zq), share(ph, zq), loc_sem.at[ph]).wait()
            lax.fori_loop(1, 16, send, 0)

    def stage1_wait(ph):
        for q in range(4):
            @pl.when(4 * q + y != z)
            def _(q=q):
                pltpu.make_async_copy(share(ph, q), share(ph, q), s1_recv.at[ph, q]).wait()

    def piece(ph, aa, bb, part=None):
        buf, width = bufs[ph]
        xx, yy = pick(aa, bb), pick(bb, aa)
        rows = pl.ds(0, 4) if part is None else pl.ds(2 * part, 2)
        return buf.at[rows, yy, c, :, pl.ds(pl.multiple_of(xx * width, 128), width)]

    def send_piece(ph, aa, bb, device, send_sem, part=None, slot=0):
        ref = piece(ph, aa, bb, part)
        pltpu.make_async_remote_copy(
            src_ref=ref, dst_ref=ref, send_sem=send_sem.at[ph],
            recv_sem=piece_sem.at[ph, aa * 4 + bb, slot],
            device_id=device, device_id_type=MESH,
        ).start()

    def wait_piece(ph, aa, bb, part=None, slot=0):
        ref = piece(ph, aa, bb, part)
        pltpu.make_async_copy(ref, ref, piece_sem.at[ph, aa * 4 + bb, slot]).wait()

    def to_sibling(ph, aa, bb):
        ref = piece(ph, aa, bb)
        pltpu.make_async_remote_copy(
            src_ref=ref, dst_ref=ref, send_sem=sib_send.at[ph], recv_sem=sib_recv.at[ph],
            device_id=sibling, device_id_type=MESH,
        ).start()

    def second_ring(ph, aa):
        send_piece(ph, aa, b, dev_b_left, r2_send)
        send_piece(ph, aa, b, dev_b_right, r2_send)
        to_sibling(ph, aa, b)

    def step0(ph):
        stage1_wait(ph)
        send_piece(ph, a, b, dev_a_left, r1_send)
        send_piece(ph, a, b, dev_a_right, r1_send)
        second_ring(ph, a)

    def step1(ph):
        wait_piece(ph, a_left, b)
        send_piece(ph, a_left, b, dev_a_right, r1_send, 0, 0)
        second_ring(ph, a_left)
        wait_piece(ph, a_right, b)
        send_piece(ph, a_right, b, dev_a_left, r1_send, 1, 1)
        second_ring(ph, a_right)

    def step2(ph):
        wait_piece(ph, a_far, b, 0, 0)
        wait_piece(ph, a_far, b, 1, 1)
        second_ring(ph, a_far)

    def step3(ph):
        for aa in (a, a_left, a_right, a_far):
            wait_piece(ph, aa, b_left)
            send_piece(ph, aa, b_left, dev_b_right, r2_send, 0, 0)
            to_sibling(ph, aa, b_left)
            wait_piece(ph, aa, b_right)
            send_piece(ph, aa, b_right, dev_b_left, r2_send, 1, 1)
            to_sibling(ph, aa, b_right)

    def step4(ph):
        for aa in (a, a_left, a_right, a_far):
            wait_piece(ph, aa, b_far, 0, 0)
            wait_piece(ph, aa, b_far, 1, 1)
            to_sibling(ph, aa, b_far)

    def all_here(ph):
        ref = bufs[ph][0].at[:, :, other]
        pltpu.make_async_copy(ref, ref, sib_recv.at[ph]).wait()

    def widen(i, carry):
        at = pl.ds(pl.multiple_of(i * 64, 64), 64)
        for t in range(4):
            rbuf[t, at, :] = nbr[at, t * 128 : (t + 1) * 128].astype(F32)
        return carry

    lax.fori_loop(0, READS // 64, widen, 0)
    tpack[0:6, :] = (ev_time[...] - nb_time[...]).astype(F32)
    tpack[6:7, :] = nb_count[...].astype(F32)
    tpack[7:8, :] = jnp.zeros((1, EV), F32)
    tcol[...] = jnp.transpose(tpack[...])
    lanes = lax.broadcasted_iota(jnp.int32, (1, D), 1).astype(F32)
    freq = jnp.exp(lanes * (-9.0 * math.log(10.0) / D))

    def make_keys(i, carry):
        at = pl.ds(pl.multiple_of(i * 16, 16), 16)
        gaps = tcol[at, :]
        for j in range(SLOTS):
            gap = gaps[:, j : j + 1]
            for t, cosine in enumerate((cos_wide, cos_wide, cos_small, cos_small)):
                cut = slice(t * 128, (t + 1) * 128)
                rows = rbuf[t, pl.ds(i * (16 * SLOTS) + j, 16, stride=SLOTS), :]
                keys[j, at, cut] = rows + cosine(gap * freq[:, cut])
        return carry

    lax.fori_loop(0, EV // 16, make_keys, 0)

    step0(1)
    step0(0)
    step1(1)
    step2(1)
    step1(0)
    step2(0)
    step3(1)
    step4(1)
    step3(0)

    def wide(ref, start, width):
        return ref[:, :, :, :, pl.ds(start, width)].reshape(D, width)

    all_here(1)

    def gate(k):
        return (nn(msg[...], wide(wb, k * D, D)), nn(dst[...], wide(wb, 1536 + k * D, D)))

    gi, gh = gate(0)
    gates[0] = sigmoid(gi + gh)
    gi, gh = gate(2)
    gates[3] = gh
    gates[2] = jnp.tanh(gi + gates[0] * gh)
    gi, gh = gate(1)
    update = sigmoid(gi + gh)
    gates[1] = update
    mem[...] = ((1.0 - update) * gates[2] + update * dst[...].astype(F32)).astype(BF16)

    step4(0)
    all_here(0)

    gatt = nt(emb[...], wide(wa, 1024, 512)).astype(BF16)
    for h in range(2):
        gv[h] = nt(gatt[:, h * HEAD : (h + 1) * HEAD], wide(wa, 512 + h * HEAD, HEAD))

    lane16 = lax.broadcasted_iota(jnp.int32, (16, 128), 1)

    def row_dots(vec, out):
        def block(i, carry):
            at = pl.ds(pl.multiple_of(i * 16, 16), 16)
            acc = jnp.zeros((16, 128), F32)
            v0, v1 = vec[0, at, :], vec[1, at, :]
            for j in range(SLOTS):
                key = keys[j, at, :]
                for h, v in enumerate((v0, v1)):
                    prod = key * v
                    part = (prod[:, 0:128] + prod[:, 128:256]) + (prod[:, 256:384] + prod[:, 384:512])
                    acc = jnp.where(lane16 == h * SLOTS + j, jnp.sum(part, axis=1, keepdims=True), acc)
            out[at, :] = acc
            return carry
        lax.fori_loop(0, EV // 16, block, 0)

    row_dots(gv, gwp)

    quer = nn(mem[...], wide(wa, 1536, 512)).astype(BF16)
    for h in range(2):
        qk[h] = nt(quer[:, h * HEAD : (h + 1) * HEAD], wide(wa, h * HEAD, HEAD))

    row_dots(qk, scp)

    lane = lax.broadcasted_iota(jnp.int32, (EV, 128), 1)
    slot = jnp.where(lane >= SLOTS, lane - SLOTS, lane).astype(F32)
    head0, head1 = lane < SLOTS, jnp.logical_and(lane >= SLOTS, lane < 2 * SLOTS)
    live = jnp.logical_and(lane < 2 * SLOTS, slot < tcol[:, 6:7])
    raw = jnp.where(live, jnp.exp(scp[...] * (1.0 / 16.0)), 0.0)

    def per_head(v):
        s0 = jnp.sum(jnp.where(head0, v, 0.0), axis=1, keepdims=True)
        s1 = jnp.sum(jnp.where(head1, v, 0.0), axis=1, keepdims=True)
        return jnp.where(head0, s0, s1)

    weight = raw / per_head(raw)
    gw = gwp[...]
    wtp[...] = weight
    scp[...] = weight * (gw - per_head(weight * gw)) * (1.0 / 16.0)

    def gather_slots(i, carry):
        at = pl.ds(pl.multiple_of(i * 16, 16), 16)
        sc = scp[at, :]
        c0 = jnp.zeros((16, D), F32)
        c1 = jnp.zeros((16, D), F32)
        for j in range(SLOTS):
            key = keys[j, at, :]
            c0 = c0 + sc[:, j : j + 1] * key
            c1 = c1 + sc[:, SLOTS + j : SLOTS + j + 1] * key
        ctx[0, at, :] = c0.astype(BF16)
        ctx[1, at, :] = c1.astype(BF16)
        return carry

    lax.fori_loop(0, EV // 16, gather_slots, 0)
    gq = [nn(ctx[h], wide(wa, h * HEAD, HEAD)).astype(BF16) for h in range(2)]
    gmem[...] = emb[...].astype(F32) + (
        nt(gq[0], wide(wa, 1536, HEAD)) + nt(gq[1], wide(wa, 1536 + HEAD, HEAD))
    )

    def gru(i, carry):
        at = pl.ds(pl.multiple_of(i * 16, 16), 16)
        gm = gmem[at, :]
        r, u, cand, hc = gates[0, at, :], gates[1, at, :], gates[2, at, :], gates[3, at, :]
        gu = gm * (dst[at, :].astype(F32) - cand)
        gc = gm * (1.0 - u) * (1.0 - cand * cand)
        gin[at, 0:512] = (gc * hc * (r * (1.0 - r))).astype(BF16)
        gin[at, 512:1024] = (gu * (u * (1.0 - u))).astype(BF16)
        gin[at, 1024:1536] = gc.astype(BF16)
        gcand[at, :] = (gc * r).astype(BF16)
        gmem[at, :] = gm * u
        return carry

    lax.fori_loop(0, EV // 16, gru, 0)

    gmsg[...] = nt(gin[...], wide(wb, 0, 1536)).astype(BF16)

    def part_copy(g):
        return pltpu.make_async_remote_copy(
            src_ref=npart.at[g, other], dst_ref=nsib.at[g], send_sem=nd_send.at[g], recv_sem=nd_recv.at[g],
            device_id=sibling, device_id_type=MESH,
        )

    for g, offsets in enumerate(FAR):
        base = ((z + offsets[0]) % 16) * 64
        wanted = (lax.broadcasted_iota(jnp.int32, (256, EV), 0) + base) & 1023
        hot = (wanted == src_id[...]).astype(F32).astype(BF16)
        sums = nn(hot, gmsg[...]).astype(BF16).reshape(4, 2, OWN, D)
        npart[g, 0] = sums[:, 0]
        npart[g, 1] = sums[:, 1]
        part_copy(g).start()

    def mine(rel):
        for g, offsets in enumerate(FAR):
            if rel in offsets:
                k = offsets.index(rel)
                return npart[g, c, k].astype(F32) + nsib[g, k].astype(F32)

    chains = (((8, 9, 10, 11), -1, -5), ((7, 6, 5), 1, 5), ((12, 13, 14, 15), -1, -1), ((4, 3, 2, 1), 1, 1))

    def hop(way, s):
        steps, near, last = chains[way]
        to = (z + (last if s == len(steps) - 1 else near) + 16) % 16
        return pltpu.make_async_remote_copy(
            src_ref=nsend.at[way, s], dst_ref=nrecv.at[way, s],
            send_sem=ring_send.at[way, s], recv_sem=ring_recv.at[way, s],
            device_id=(tm, to * 2 + c), device_id_type=MESH,
        )

    def chain_step(way, s):
        total = mine(chains[way][0][s])
        if s > 0:
            hop(way, s - 1).wait_recv()
            total = total + nrecv[way, s - 1].astype(F32)
        nsend[way, s] = total.astype(BF16)
        hop(way, s).start()

    def chain_steps(s):
        for way in range(4):
            if s < len(chains[way][0]):
                chain_step(way, s)

    def spread(i, carry):
        at = pl.ds(pl.multiple_of(i * 16, 16), 16)
        sc, wt = scp[at, :], wtp[at, :]
        for j in range(SLOTS):
            s0, s1 = sc[:, j : j + 1], sc[:, SLOTS + j : SLOTS + j + 1]
            w0, w1 = wt[:, j : j + 1], wt[:, SLOTS + j : SLOTS + j + 1]
            for t in range(4):
                cut = slice(t * 128, (t + 1) * 128)
                rbuf[t, pl.ds(i * (16 * SLOTS) + j, 16, stride=SLOTS), :] = (
                    (s0 * qk[0, at, cut] + s1 * qk[1, at, cut]) + (w0 * gv[0, at, cut] + w1 * gv[1, at, cut])
                )
        return carry

    def narrow(i, carry):
        at = pl.ds(pl.multiple_of(i * 64, 64), 64)
        for t in range(4):
            gkb[at, t * 128 : (t + 1) * 128] = rbuf[t, at, :].astype(BF16)
        return carry

    def version_sums(m):
        ids = []
        for k in range(READS // 128):
            vid = owner[:, k * 128 : (k + 1) * 128] * OWN + vrow[k : k + 1, :]
            ids.append((lax.broadcasted_iota(jnp.int32, (256, 128), 0) + 256 * m == vid).astype(F32).astype(BF16))
        sums = nn(jnp.concatenate(ids, axis=1), gkb[...]).astype(BF16)
        vpart[pl.ds(8 * m, 8)] = sums.reshape(8, OWN, D)
        for t in range(8 * m, 8 * m + 8):
            @pl.when(tm != t)
            def _(t=t):
                pltpu.make_async_remote_copy(
                    src_ref=vpart.at[t], dst_ref=vbuf.at[(t - tm + 15) % 16],
                    send_sem=v_send, recv_sem=v_recv,
                    device_id=(t, node), device_id_type=MESH,
                ).start()

    lax.fori_loop(0, EV // 32, spread, 0)
    for g in range(3):
        part_copy(g).wait()
    chain_steps(0)
    lax.fori_loop(EV // 32, EV // 16, spread, 0)
    part_copy(3).wait()
    chain_steps(1)
    lax.fori_loop(0, READS // 64, narrow, 0)
    version_sums(0)
    chain_steps(2)
    version_sums(1)
    chain_steps(3)

    gdst = (nt(gin[:, 0:1024], wide(wb, 1536, 1024)) + nt(gcand[...], wide(wb, 2560, 512))) + gmem[...]
    hot = (lax.broadcasted_iota(jnp.int32, (OWN, EV), 0) == dst_loc[...]).astype(F32).astype(BF16)
    dpart[...] = mine(0) + nn(hot, gdst.astype(BF16))

    ends = [(way, len(chains[way][0]) - 1) for way in range(4)]
    for way, s in ends:
        hop(way, s).wait_recv()
    node_out[...] = dpart[...] + (
        (nrecv[0, 3].astype(F32) + nrecv[1, 2].astype(F32)) + (nrecv[2, 3].astype(F32) + nrecv[3, 3].astype(F32))
    )
    pltpu.make_async_copy(vbuf, vbuf, v_recv).wait()
    total = vpart[tm].astype(F32)
    for k in range(15):
        total = total + vbuf[k].astype(F32)
    ver_out[...] = total

    for way in range(4):
        for s in range(len(chains[way][0])):
            hop(way, s).wait_send()
    pltpu.make_async_copy(vbuf, vbuf, v_send).wait()
    for ph, (buf, width) in enumerate(bufs):
        ref = buf.at[:, :, c]
        pltpu.make_async_copy(ref, ref, sib_send.at[ph]).wait()
        ref = buf.at[:, 0:3, c, :, 0:width]
        pltpu.make_async_copy(ref, ref, r1_send.at[ph]).wait()
        ref = buf.at[:, 0:3, c]
        pltpu.make_async_copy(ref, ref, r2_send.at[ph]).wait()

    @pl.when(zy == y)
    def _():
        ref = wa.at[:, 0, c, :, 0:1920]
        pltpu.make_async_copy(ref, ref, s1_send.at[0]).wait()
        ref = wb.at[0, 0:3, :, :, 0:1920]
        pltpu.make_async_copy(ref, ref, s1_send.at[1]).wait()


def hand_out(ver_in, node_in, ver_out, node_out, sems):
    copies = [
        pltpu.make_async_copy(ver_in, ver_out, sems.at[0]),
        pltpu.make_async_copy(node_in, node_out, sems.at[1]),
    ]
    for copy in copies:
        copy.start()
    for copy in copies:
        copy.wait()


def body(
    message, dest_mem, nbr_rows, emb_grad, event_time, nbr_time, nbr_count, source_id, dest_local,
    read_owner, read_row, w_in, w_hid, w_query, w_keyval, w_out,
):
    vmem = pl.BlockSpec(memory_space=pltpu.VMEM)
    hbm = pl.BlockSpec(memory_space=pl.ANY)
    dma = pltpu.SemaphoreType.DMA
    scratch = [
        pltpu.VMEM((4, 4, 2, 16, 2048), BF16),
        pltpu.VMEM((4, 4, 2, 16, 3072), BF16),
        pltpu.VMEM((4, READS, 128), F32),
        pltpu.VMEM((SLOTS, EV, D), F32),
        pltpu.VMEM((READS, D), BF16),
        pltpu.VMEM((2, EV, D), F32),
        pltpu.VMEM((2, EV, D), F32),
        pltpu.VMEM((2, EV, D), BF16),
        pltpu.VMEM((4, EV, D), F32),
        pltpu.VMEM((EV, D), BF16),
        pltpu.VMEM((EV, D), F32),
        pltpu.VMEM((EV, 3 * D), BF16),
        pltpu.VMEM((EV, D), BF16),
        pltpu.VMEM((EV, D), BF16),
        pltpu.VMEM((EV, 8), F32),
        pltpu.VMEM((8, EV), F32),
        pltpu.VMEM((EV, 128), F32),
        pltpu.VMEM((EV, 128), F32),
        pltpu.VMEM((EV, 128), F32),
        pltpu.VMEM((16, OWN, D), BF16),
        pltpu.VMEM((15, OWN, D), BF16),
        pltpu.VMEM((4, 2, 4, OWN, D), BF16),
        pltpu.VMEM((4, 4, OWN, D), BF16),
        pltpu.VMEM((4, 4, OWN, D), BF16),
        pltpu.VMEM((4, 4, OWN, D), BF16),
        pltpu.VMEM((OWN, D), F32),
        dma((2,)),
        dma((2,)),
        dma((2, 4)),
        dma((2,)),
        dma((2,)),
        dma((2, 16, 2)),
        dma((2,)),
        dma((2,)),
        dma,
        dma,
        dma((4,)),
        dma((4,)),
        dma((4, 4)),
        dma((4, 4)),
    ]
    version_grad, node_grad = pl.pallas_call(
        kernel,
        out_shape=(jax.ShapeDtypeStruct((OWN, D), F32), jax.ShapeDtypeStruct((OWN, D), F32)),
        in_specs=[vmem] * 11 + [hbm] * 5,
        out_specs=(vmem, vmem),
        scratch_shapes=scratch,
        compiler_params=pltpu.CompilerParams(
            collective_id=0, has_side_effects=True, vmem_limit_bytes=56 * 1024 * 1024
        ),
        cost_estimate=pl.CostEstimate(
            flops=4_000_000_000, bytes_accessed=8_000_000, transcendentals=1_000_000
        ),
    )(
        message, dest_mem, nbr_rows, emb_grad,
        event_time.reshape(1, EV), nbr_time.T, nbr_count.reshape(1, EV),
        source_id.reshape(1, EV), dest_local.reshape(1, EV),
        read_owner.reshape(1, READS), read_row.reshape(READS // 128, 128),
        w_in, w_hid, w_query, w_keyval, w_out,
    )
    version_grad, node_grad = pl.pallas_call(
        hand_out,
        out_shape=(jax.ShapeDtypeStruct((OWN, D), F32), jax.ShapeDtypeStruct((OWN, D), F32)),
        in_specs=[hbm] * 2,
        out_specs=(hbm, hbm),
        scratch_shapes=[dma((2,))],
        compiler_params=pltpu.CompilerParams(vmem_limit_bytes=60 * 1024 * 1024),
    )(version_grad, node_grad)
    return version_grad, node_grad[None]


def solution(mesh):
    both = P(("tm", "node"))
    in_specs = (
        (P(("tm", "node"), None),) * 4
        + (both, P(("tm", "node"), None), both, both, both, P(("tm", "node"), None), both)
        + (P("node", None),) * 5
    )
    out_specs = (P(("tm", "node"), None), P("tm", "node", None))
    return jax.shard_map(body, mesh=mesh, in_specs=in_specs, out_specs=out_specs, check_vma=False)
```

```python
import math

import jax
import jax.numpy as jnp
from jax import lax
from jax.experimental import pallas as pl
from jax.experimental.pallas import tpu as pltpu
from jax.sharding import PartitionSpec as P

D = 512
HEAD = 256
SLOTS = 6
EV = 256
READS = EV * SLOTS
OWN = 32
CA = 512
CB = 768
F32 = jnp.float32
BF16 = jnp.bfloat16
MESH = pl.DeviceIdType.MESH
FAR = ((5, 6, 7, 8), (9, 10, 11, 12), (1, 2, 3, 4), (13, 14, 15, 0))


def nn(a, b):
    return lax.dot_general(a, b, (((1,), (0,)), ((), ())), preferred_element_type=F32)


def nt(a, b):
    return lax.dot_general(a, b, (((1,), (1,)), ((), ())), preferred_element_type=F32)


def sigmoid(v):
    return 0.5 * jnp.tanh(0.5 * v) + 0.5


def cos_wide(angle):
    half = 0.5 * angle
    turns = jnp.floor(half * (1.0 / math.pi) + 0.5)
    s = (half - turns * 3.140625) - turns * (math.pi - 3.140625)
    q = s * s
    p = q * (-1.0 / 39916800.0) + (1.0 / 362880.0)
    p = p * q + (-1.0 / 5040.0)
    p = p * q + (1.0 / 120.0)
    p = p * q + (-1.0 / 6.0)
    p = p * q + 1.0
    sine = p * s
    return 1.0 - 2.0 * (sine * sine)


def cos_small(angle):
    q = angle * angle
    return 1.0 + q * (q * (1.0 / 24.0) - 0.5)


def gather_kernel(
    nbr, ev_time, nb_time, nb_count, w_in, w_hid, w_q, w_kv, w_out,
    wa, wb, keys, tcol,
    rbuf, tpack,
    loc_sem, s1_send, s1_recv, r1_send, r2_send, piece_sem, sib_send, sib_recv,
):
    tm = lax.axis_index("tm")
    node = lax.axis_index("node")
    x, y = tm // 4, tm % 4
    z, c = node // 2, node % 2
    other = 1 - c
    sibling = (tm, z * 2 + other)
    zq, zy = z // 4, z % 4

    def pick(p, q):
        return jnp.where(c == 0, p, q)

    a, b = pick(x, y), pick(y, x)

    def tm_of(aa, bb):
        return pick(aa * 4 + bb, bb * 4 + aa)

    a_left, a_right, a_far = (a + 3) % 4, (a + 1) % 4, (a + 2) % 4
    b_left, b_right, b_far = (b + 3) % 4, (b + 1) % 4, (b + 2) % 4
    dev_a_left, dev_a_right = (tm_of(a_left, b), node), (tm_of(a_right, b), node)
    dev_b_left, dev_b_right = (tm_of(a, b_left), node), (tm_of(a, b_right), node)

    bufs = ((wa, CA), (wb, CB))

    def share(ph, q):
        buf, width = bufs[ph]
        return buf.at[q, y, c, :, pl.ds(pl.multiple_of(x * width, 128), width)]

    blocks = (((w_kv, 0), (w_in, 0)), ((w_kv, CA), (w_in, CB)), ((w_out, 0), (w_hid, 0)), ((w_q, 0), (w_hid, CB)))
    for k, pair in enumerate(blocks):
        @pl.when(jnp.logical_and(zy == y, x == k))
        def _(pair=pair):
            for ph, (ref, at) in enumerate(pair):
                pltpu.make_async_copy(
                    ref.at[:, pl.ds(at, bufs[ph][1])], share(ph, zq), loc_sem.at[ph]
                ).start()

    barrier = pltpu.get_barrier_semaphore()

    def greet(k, carry):
        pl.semaphore_signal(barrier, inc=1, device_id=(tm, (node + 2 * k) % 32), device_id_type=MESH)
        pl.semaphore_signal(barrier, inc=1, device_id=((tm + k) % 16, node), device_id_type=MESH)
        return carry

    lax.fori_loop(1, 16, greet, 0)
    pl.semaphore_signal(barrier, inc=1, device_id=sibling, device_id_type=MESH)

    pl.semaphore_wait(barrier, 31)

    @pl.when(zy == y)
    def _():
        for ph in range(2):
            def send(k, carry, ph=ph):
                pltpu.make_async_remote_copy(
                    src_ref=share(ph, zq), dst_ref=share(ph, zq),
                    send_sem=s1_send.at[ph], recv_sem=s1_recv.at[ph, zq],
                    device_id=(tm, ((z + k) % 16) * 2 + c), device_id_type=MESH,
                ).start()
                return carry
            pltpu.make_async_copy(share(ph, zq), share(ph, zq), loc_sem.at[ph]).wait()
            lax.fori_loop(1, 16, send, 0)

    def stage1_wait(ph):
        for q in range(4):
            @pl.when(4 * q + y != z)
            def _(q=q):
                pltpu.make_async_copy(share(ph, q), share(ph, q), s1_recv.at[ph, q]).wait()

    def piece(ph, aa, bb, part=None):
        buf, width = bufs[ph]
        xx, yy = pick(aa, bb), pick(bb, aa)
        rows = pl.ds(0, 4) if part is None else pl.ds(2 * part, 2)
        return buf.at[rows, yy, c, :, pl.ds(pl.multiple_of(xx * width, 128), width)]

    def send_piece(ph, aa, bb, device, send_sem, part=None, slot=0):
        ref = piece(ph, aa, bb, part)
        pltpu.make_async_remote_copy(
            src_ref=ref, dst_ref=ref, send_sem=send_sem.at[ph],
            recv_sem=piece_sem.at[ph, aa * 4 + bb, slot],
            device_id=device, device_id_type=MESH,
        ).start()

    def wait_piece(ph, aa, bb, part=None, slot=0):
        ref = piece(ph, aa, bb, part)
        pltpu.make_async_copy(ref, ref, piece_sem.at[ph, aa * 4 + bb, slot]).wait()

    def to_sibling(ph, aa, bb):
        ref = piece(ph, aa, bb)
        pltpu.make_async_remote_copy(
            src_ref=ref, dst_ref=ref, send_sem=sib_send.at[ph], recv_sem=sib_recv.at[ph],
            device_id=sibling, device_id_type=MESH,
        ).start()

    def second_ring(ph, aa):
        send_piece(ph, aa, b, dev_b_left, r2_send)
        send_piece(ph, aa, b, dev_b_right, r2_send)
        to_sibling(ph, aa, b)

    def step0(ph):
        stage1_wait(ph)
        send_piece(ph, a, b, dev_a_left, r1_send)
        send_piece(ph, a, b, dev_a_right, r1_send)
        second_ring(ph, a)

    def step1(ph):
        wait_piece(ph, a_left, b)
        send_piece(ph, a_left, b, dev_a_right, r1_send, 0, 0)
        second_ring(ph, a_left)
        wait_piece(ph, a_right, b)
        send_piece(ph, a_right, b, dev_a_left, r1_send, 1, 1)
        second_ring(ph, a_right)

    def step2(ph):
        wait_piece(ph, a_far, b, 0, 0)
        wait_piece(ph, a_far, b, 1, 1)
        second_ring(ph, a_far)

    def step3(ph):
        for aa in (a, a_left, a_right, a_far):
            wait_piece(ph, aa, b_left)
            send_piece(ph, aa, b_left, dev_b_right, r2_send, 0, 0)
            to_sibling(ph, aa, b_left)
            wait_piece(ph, aa, b_right)
            send_piece(ph, aa, b_right, dev_b_left, r2_send, 1, 1)
            to_sibling(ph, aa, b_right)

    def step4(ph):
        for aa in (a, a_left, a_right, a_far):
            wait_piece(ph, aa, b_far, 0, 0)
            wait_piece(ph, aa, b_far, 1, 1)
            to_sibling(ph, aa, b_far)

    def all_here(ph):
        ref = bufs[ph][0].at[:, :, other]
        pltpu.make_async_copy(ref, ref, sib_recv.at[ph]).wait()

    def widen(i, carry):
        at = pl.ds(pl.multiple_of(i * 64, 64), 64)
        for t in range(4):
            rbuf[t, at, :] = nbr[at, t * 128 : (t + 1) * 128].astype(F32)
        return carry

    lax.fori_loop(0, READS // 64, widen, 0)
    tpack[0:6, :] = (ev_time[...] - nb_time[...]).astype(F32)
    tpack[6:7, :] = nb_count[...].astype(F32)
    tpack[7:8, :] = jnp.zeros((1, EV), F32)
    tcol[...] = jnp.transpose(tpack[...])
    lanes = lax.broadcasted_iota(jnp.int32, (1, D), 1).astype(F32)
    freq = jnp.exp(lanes * (-9.0 * math.log(10.0) / D))

    def make_keys(i, carry):
        at = pl.ds(pl.multiple_of(i * 16, 16), 16)
        gaps = tcol[at, :]
        for j in range(SLOTS):
            gap = gaps[:, j : j + 1]
            for t, cosine in enumerate((cos_wide, cos_wide, cos_small, cos_small)):
                cut = slice(t * 128, (t + 1) * 128)
                rows = rbuf[t, pl.ds(i * (16 * SLOTS) + j, 16, stride=SLOTS), :]
                keys[j, at, cut] = rows + cosine(gap * freq[:, cut])
        return carry

    lax.fori_loop(0, EV // 16, make_keys, 0)

    step0(1)
    step0(0)
    step1(1)
    step2(1)
    step1(0)
    step2(0)
    step3(1)
    step4(1)
    step3(0)
    step4(0)
    all_here(1)
    all_here(0)

    for ph, (buf, width) in enumerate(bufs):
        ref = buf.at[:, :, c]
        pltpu.make_async_copy(ref, ref, sib_send.at[ph]).wait()
        ref = buf.at[:, 0:3, c, :, 0:width]
        pltpu.make_async_copy(ref, ref, r1_send.at[ph]).wait()
        ref = buf.at[:, 0:3, c]
        pltpu.make_async_copy(ref, ref, r2_send.at[ph]).wait()

    @pl.when(zy == y)
    def _():
        ref = wa.at[:, 0, c, :, 0:1920]
        pltpu.make_async_copy(ref, ref, s1_send.at[0]).wait()
        ref = wb.at[0, 0:3, :, :, 0:1920]
        pltpu.make_async_copy(ref, ref, s1_send.at[1]).wait()


def math_kernel(
    msg, dst, emb, wa, wb, keys, tcol, src_id, dst_loc, owner, vrow,
    vpart, npart, dpart,
    rbuf, gkb, qk, gv, ctx, gates, mem, gmem, gin, gcand, gmsg, gwp, scp, wtp,
):
    z = lax.axis_index("node") // 2

    def wide(ref, start, width):
        return ref[:, :, :, :, pl.ds(start, width)].reshape(D, width)

    def gate(k):
        return (nn(msg[...], wide(wb, k * D, D)), nn(dst[...], wide(wb, 1536 + k * D, D)))

    gi, gh = gate(0)
    gates[0] = sigmoid(gi + gh)
    gi, gh = gate(2)
    gates[3] = gh
    gates[2] = jnp.tanh(gi + gates[0] * gh)
    gi, gh = gate(1)
    update = sigmoid(gi + gh)
    gates[1] = update
    mem[...] = ((1.0 - update) * gates[2] + update * dst[...].astype(F32)).astype(BF16)

    gatt = nt(emb[...], wide(wa, 1024, 512)).astype(BF16)
    for h in range(2):
        gv[h] = nt(gatt[:, h * HEAD : (h + 1) * HEAD], wide(wa, 512 + h * HEAD, HEAD))

    lane16 = lax.broadcasted_iota(jnp.int32, (16, 128), 1)

    def row_dots(vec, out):
        def block(i, carry):
            at = pl.ds(pl.multiple_of(i * 16, 16), 16)
            acc = jnp.zeros((16, 128), F32)
            v0, v1 = vec[0, at, :], vec[1, at, :]
            for j in range(SLOTS):
                key = keys[j, at, :]
                for h, v in enumerate((v0, v1)):
                    prod = key * v
                    part = (prod[:, 0:128] + prod[:, 128:256]) + (prod[:, 256:384] + prod[:, 384:512])
                    acc = jnp.where(lane16 == h * SLOTS + j, jnp.sum(part, axis=1, keepdims=True), acc)
            out[at, :] = acc
            return carry
        lax.fori_loop(0, EV // 16, block, 0)

    row_dots(gv, gwp)

    quer = nn(mem[...], wide(wa, 1536, 512)).astype(BF16)
    for h in range(2):
        qk[h] = nt(quer[:, h * HEAD : (h + 1) * HEAD], wide(wa, h * HEAD, HEAD))

    row_dots(qk, scp)

    lane = lax.broadcasted_iota(jnp.int32, (EV, 128), 1)
    slot = jnp.where(lane >= SLOTS, lane - SLOTS, lane).astype(F32)
    head0, head1 = lane < SLOTS, jnp.logical_and(lane >= SLOTS, lane < 2 * SLOTS)
    live = jnp.logical_and(lane < 2 * SLOTS, slot < tcol[:, 6:7])
    raw = jnp.where(live, jnp.exp(scp[...] * (1.0 / 16.0)), 0.0)

    def per_head(v):
        s0 = jnp.sum(jnp.where(head0, v, 0.0), axis=1, keepdims=True)
        s1 = jnp.sum(jnp.where(head1, v, 0.0), axis=1, keepdims=True)
        return jnp.where(head0, s0, s1)

    weight = raw / per_head(raw)
    gw = gwp[...]
    wtp[...] = weight
    scp[...] = weight * (gw - per_head(weight * gw)) * (1.0 / 16.0)

    def gather_slots(i, carry):
        at = pl.ds(pl.multiple_of(i * 16, 16), 16)
        sc = scp[at, :]
        c0 = jnp.zeros((16, D), F32)
        c1 = jnp.zeros((16, D), F32)
        for j in range(SLOTS):
            key = keys[j, at, :]
            c0 = c0 + sc[:, j : j + 1] * key
            c1 = c1 + sc[:, SLOTS + j : SLOTS + j + 1] * key
        ctx[0, at, :] = c0.astype(BF16)
        ctx[1, at, :] = c1.astype(BF16)
        return carry

    lax.fori_loop(0, EV // 16, gather_slots, 0)
    gq = [nn(ctx[h], wide(wa, h * HEAD, HEAD)).astype(BF16) for h in range(2)]
    gmem[...] = emb[...].astype(F32) + (
        nt(gq[0], wide(wa, 1536, HEAD)) + nt(gq[1], wide(wa, 1536 + HEAD, HEAD))
    )

    def gru(i, carry):
        at = pl.ds(pl.multiple_of(i * 16, 16), 16)
        gm = gmem[at, :]
        r, u, cand, hc = gates[0, at, :], gates[1, at, :], gates[2, at, :], gates[3, at, :]
        gu = gm * (dst[at, :].astype(F32) - cand)
        gc = gm * (1.0 - u) * (1.0 - cand * cand)
        gin[at, 0:512] = (gc * hc * (r * (1.0 - r))).astype(BF16)
        gin[at, 512:1024] = (gu * (u * (1.0 - u))).astype(BF16)
        gin[at, 1024:1536] = gc.astype(BF16)
        gcand[at, :] = (gc * r).astype(BF16)
        gmem[at, :] = gm * u
        return carry

    lax.fori_loop(0, EV // 16, gru, 0)

    gmsg[...] = nt(gin[...], wide(wb, 0, 1536)).astype(BF16)

    for g, offsets in enumerate(FAR):
        base = ((z + offsets[0]) % 16) * 64
        wanted = (lax.broadcasted_iota(jnp.int32, (256, EV), 0) + base) & 1023
        hot = (wanted == src_id[...]).astype(F32).astype(BF16)
        sums = nn(hot, gmsg[...]).astype(BF16).reshape(4, 2, OWN, D)
        npart[g, 0] = sums[:, 0]
        npart[g, 1] = sums[:, 1]

    def spread(i, carry):
        at = pl.ds(pl.multiple_of(i * 16, 16), 16)
        sc, wt = scp[at, :], wtp[at, :]
        for j in range(SLOTS):
            s0, s1 = sc[:, j : j + 1], sc[:, SLOTS + j : SLOTS + j + 1]
            w0, w1 = wt[:, j : j + 1], wt[:, SLOTS + j : SLOTS + j + 1]
            for t in range(4):
                cut = slice(t * 128, (t + 1) * 128)
                rbuf[t, pl.ds(i * (16 * SLOTS) + j, 16, stride=SLOTS), :] = (
                    (s0 * qk[0, at, cut] + s1 * qk[1, at, cut]) + (w0 * gv[0, at, cut] + w1 * gv[1, at, cut])
                )
        return carry

    def narrow(i, carry):
        at = pl.ds(pl.multiple_of(i * 64, 64), 64)
        for t in range(4):
            gkb[at, t * 128 : (t + 1) * 128] = rbuf[t, at, :].astype(BF16)
        return carry

    def version_sums(m):
        ids = []
        for k in range(READS // 128):
            vid = owner[:, k * 128 : (k + 1) * 128] * OWN + vrow[k : k + 1, :]
            ids.append((lax.broadcasted_iota(jnp.int32, (256, 128), 0) + 256 * m == vid).astype(F32).astype(BF16))
        sums = nn(jnp.concatenate(ids, axis=1), gkb[...]).astype(BF16)
        vpart[pl.ds(8 * m, 8)] = sums.reshape(8, OWN, D)

    lax.fori_loop(0, EV // 16, spread, 0)
    lax.fori_loop(0, READS // 64, narrow, 0)
    version_sums(0)
    version_sums(1)
    gdst = (nt(gin[:, 0:1024], wide(wb, 1536, 1024)) + nt(gcand[...], wide(wb, 2560, 512))) + gmem[...]
    hot = (lax.broadcasted_iota(jnp.int32, (OWN, EV), 0) == dst_loc[...]).astype(F32).astype(BF16)
    dpart[...] = nn(hot, gdst.astype(BF16))


def sums_kernel(
    vpart, npart, dpart,
    ver_out, node_out,
    vbuf, nsib, nsend, nrecv,
    v_send, v_recv, nd_send, nd_recv, ring_send, ring_recv,
):
    tm = lax.axis_index("tm")
    node = lax.axis_index("node")
    z, c = node // 2, node % 2
    other = 1 - c
    sibling = (tm, z * 2 + other)

    barrier = pltpu.get_barrier_semaphore()

    def greet(k, carry):
        pl.semaphore_signal(barrier, inc=1, device_id=(tm, (node + 2 * k) % 32), device_id_type=MESH)
        pl.semaphore_signal(barrier, inc=1, device_id=((tm + k) % 16, node), device_id_type=MESH)
        return carry

    lax.fori_loop(1, 16, greet, 0)
    pl.semaphore_signal(barrier, inc=1, device_id=sibling, device_id_type=MESH)
    pl.semaphore_wait(barrier, 31)

    def part_copy(g):
        return pltpu.make_async_remote_copy(
            src_ref=npart.at[g, other], dst_ref=nsib.at[g], send_sem=nd_send.at[g], recv_sem=nd_recv.at[g],
            device_id=sibling, device_id_type=MESH,
        )

    def mine(rel):
        for g, offsets in enumerate(FAR):
            if rel in offsets:
                k = offsets.index(rel)
                return npart[g, c, k].astype(F32) + nsib[g, k].astype(F32)

    chains = (((8, 9, 10, 11), -1, -5), ((7, 6, 5), 1, 5), ((12, 13, 14, 15), -1, -1), ((4, 3, 2, 1), 1, 1))

    def hop(way, s):
        steps, near, last = chains[way]
        to = (z + (last if s == len(steps) - 1 else near) + 16) % 16
        return pltpu.make_async_remote_copy(
            src_ref=nsend.at[way, s], dst_ref=nrecv.at[way, s],
            send_sem=ring_send.at[way, s], recv_sem=ring_recv.at[way, s],
            device_id=(tm, to * 2 + c), device_id_type=MESH,
        )

    def chain_step(way, s):
        total = mine(chains[way][0][s])
        if s > 0:
            hop(way, s - 1).wait_recv()
            total = total + nrecv[way, s - 1].astype(F32)
        nsend[way, s] = total.astype(BF16)
        hop(way, s).start()

    def chain_steps(s):
        for way in range(4):
            if s < len(chains[way][0]):
                chain_step(way, s)

    def send_versions(k, carry):
        to = (tm + k) % 16
        pltpu.make_async_remote_copy(
            src_ref=vpart.at[to], dst_ref=vbuf.at[k - 1],
            send_sem=v_send, recv_sem=v_recv,
            device_id=(to, node), device_id_type=MESH,
        ).start()
        return carry

    for g in range(4):
        part_copy(g).start()
    lax.fori_loop(1, 16, send_versions, 0)
    for g in range(3):
        part_copy(g).wait()
    chain_steps(0)
    part_copy(3).wait()
    for s in range(1, 4):
        chain_steps(s)

    ends = [(way, len(chains[way][0]) - 1) for way in range(4)]
    for way, s in ends:
        hop(way, s).wait_recv()
    node_out[...] = (mine(0) + dpart[...]) + (
        (nrecv[0, 3].astype(F32) + nrecv[1, 2].astype(F32)) + (nrecv[2, 3].astype(F32) + nrecv[3, 3].astype(F32))
    )
    pltpu.make_async_copy(vbuf, vbuf, v_recv).wait()
    total = vpart[tm].astype(F32)
    for k in range(15):
        total = total + vbuf[k].astype(F32)
    ver_out[...] = total

    for way in range(4):
        for s in range(len(chains[way][0])):
            hop(way, s).wait_send()
    pltpu.make_async_copy(vbuf, vbuf, v_send).wait()


def body(
    message, dest_mem, nbr_rows, emb_grad, event_time, nbr_time, nbr_count, source_id, dest_local,
    read_owner, read_row, w_in, w_hid, w_query, w_keyval, w_out,
):
    vmem = pl.BlockSpec(memory_space=pltpu.VMEM)
    hbm = pl.BlockSpec(memory_space=pl.ANY)
    dma = pltpu.SemaphoreType.DMA
    shape = jax.ShapeDtypeStruct
    wa, wb, keys, tcol = pl.pallas_call(
        gather_kernel,
        out_shape=(
            shape((4, 4, 2, 16, 2048), BF16), shape((4, 4, 2, 16, 3072), BF16),
            shape((SLOTS, EV, D), F32), shape((EV, 8), F32),
        ),
        in_specs=[vmem] * 4 + [hbm] * 5,
        out_specs=(vmem,) * 4,
        scratch_shapes=[
            pltpu.VMEM((4, READS, 128), F32),
            pltpu.VMEM((8, EV), F32),
            dma((2,)), dma((2,)), dma((2, 4)), dma((2,)), dma((2,)), dma((2, 16, 2)), dma((2,)), dma((2,)),
        ],
        compiler_params=pltpu.CompilerParams(
            collective_id=0, has_side_effects=True, vmem_limit_bytes=24 * 1024 * 1024
        ),
        cost_estimate=pl.CostEstimate(flops=20_000_000, bytes_accessed=8_000_000, transcendentals=0),
    )(
        nbr_rows, event_time.reshape(1, EV), nbr_time.T, nbr_count.reshape(1, EV),
        w_in, w_hid, w_query, w_keyval, w_out,
    )
    vpart, npart, dpart = pl.pallas_call(
        math_kernel,
        out_shape=(shape((16, OWN, D), BF16), shape((4, 2, 4, OWN, D), BF16), shape((OWN, D), F32)),
        in_specs=[vmem] * 11,
        out_specs=(vmem,) * 3,
        scratch_shapes=[
            pltpu.VMEM((4, READS, 128), F32),
            pltpu.VMEM((READS, D), BF16),
            pltpu.VMEM((2, EV, D), F32),
            pltpu.VMEM((2, EV, D), F32),
            pltpu.VMEM((2, EV, D), BF16),
            pltpu.VMEM((4, EV, D), F32),
            pltpu.VMEM((EV, D), BF16),
            pltpu.VMEM((EV, D), F32),
            pltpu.VMEM((EV, 3 * D), BF16),
            pltpu.VMEM((EV, D), BF16),
            pltpu.VMEM((EV, D), BF16),
            pltpu.VMEM((EV, 128), F32),
            pltpu.VMEM((EV, 128), F32),
            pltpu.VMEM((EV, 128), F32),
        ],
        compiler_params=pltpu.CompilerParams(vmem_limit_bytes=40 * 1024 * 1024),
        cost_estimate=pl.CostEstimate(
            flops=4_000_000_000, bytes_accessed=8_000_000, transcendentals=1_000_000
        ),
    )(
        message, dest_mem, emb_grad, wa, wb, keys, tcol,
        source_id.reshape(1, EV), dest_local.reshape(1, EV),
        read_owner.reshape(1, READS), read_row.reshape(READS // 128, 128),
    )
    version_grad, node_grad = pl.pallas_call(
        sums_kernel,
        out_shape=(shape((OWN, D), F32), shape((OWN, D), F32)),
        in_specs=[vmem] * 3,
        out_specs=(vmem,) * 2,
        scratch_shapes=[
            pltpu.VMEM((15, OWN, D), BF16),
            pltpu.VMEM((4, 4, OWN, D), BF16),
            pltpu.VMEM((4, 4, OWN, D), BF16),
            pltpu.VMEM((4, 4, OWN, D), BF16),
            dma, dma, dma((4,)), dma((4,)), dma((4, 4)), dma((4, 4)),
        ],
        compiler_params=pltpu.CompilerParams(
            collective_id=1, has_side_effects=True, vmem_limit_bytes=24 * 1024 * 1024
        ),
        cost_estimate=pl.CostEstimate(flops=10_000_000, bytes_accessed=2_000_000, transcendentals=0),
    )(vpart, npart, dpart)
    return version_grad, node_grad[None]


def solution(mesh):
    both = P(("tm", "node"))
    in_specs = (
        (P(("tm", "node"), None),) * 4
        + (both, P(("tm", "node"), None), both, both, both, P(("tm", "node"), None), both)
        + (P("node", None),) * 5
    )
    out_specs = (P(("tm", "node"), None), P("tm", "node", None))
    return jax.shard_map(body, mesh=mesh, in_specs=in_specs, out_specs=out_specs, check_vma=False)
```

```python
import math

import jax
import jax.numpy as jnp
from jax import lax
from jax.experimental import pallas as pl
from jax.experimental.pallas import tpu as pltpu
from jax.sharding import PartitionSpec as P

D = 512
HEAD = 256
SLOTS = 6
EV = 256
READS = EV * SLOTS
OWN = 32
CA = 512
CB = 768
F32 = jnp.float32
BF16 = jnp.bfloat16
MESH = pl.DeviceIdType.MESH
FAR = ((5, 6, 7, 8), (9, 10, 11, 12), (1, 2, 3, 4), (13, 14, 15, 0))


def nn(a, b):
    return lax.dot_general(a, b, (((1,), (0,)), ((), ())), preferred_element_type=F32)


def nt(a, b):
    return lax.dot_general(a, b, (((1,), (1,)), ((), ())), preferred_element_type=F32)


def sigmoid(v):
    return 0.5 * jnp.tanh(0.5 * v) + 0.5


def cos_wide(angle):
    half = 0.5 * angle
    turns = jnp.floor(half * (1.0 / math.pi) + 0.5)
    s = (half - turns * 3.140625) - turns * (math.pi - 3.140625)
    q = s * s
    p = q * (-1.0 / 39916800.0) + (1.0 / 362880.0)
    p = p * q + (-1.0 / 5040.0)
    p = p * q + (1.0 / 120.0)
    p = p * q + (-1.0 / 6.0)
    p = p * q + 1.0
    sine = p * s
    return 1.0 - 2.0 * (sine * sine)


def cos_small(angle):
    q = angle * angle
    return 1.0 + q * (q * (1.0 / 24.0) - 0.5)


def kernel(
    msg, dst, nbr, emb, ev_time, nb_time, nb_count, src_id, dst_loc, owner, vrow,
    w_in, w_hid, w_q, w_kv, w_out,
    ver_out, node_out,
    wa, wb, rbuf, keys, gkb, qk, gv, ctx, gates, mem, gmem, gin, gcand, gmsg, tcol, tpack, gwp, scp, wtp,
    vpart, vbuf, npart, nsib, nsend, nrecv, dpart,
    loc_sem, s1_send, s1_recv, r1_send, r2_send, piece_sem, sib_send, sib_recv,
    v_send, v_recv, nd_send, nd_recv, ring_send, ring_recv,
):
    tm = lax.axis_index("tm")
    node = lax.axis_index("node")
    x, y = tm // 4, tm % 4
    z, c = node // 2, node % 2
    other = 1 - c
    sibling = (tm, z * 2 + other)
    zq, zy = z // 4, z % 4

    def pick(p, q):
        return jnp.where(c == 0, p, q)

    a, b = pick(x, y), pick(y, x)

    def tm_of(aa, bb):
        return pick(aa * 4 + bb, bb * 4 + aa)

    a_left, a_right, a_far = (a + 3) % 4, (a + 1) % 4, (a + 2) % 4
    b_left, b_right, b_far = (b + 3) % 4, (b + 1) % 4, (b + 2) % 4
    dev_a_left, dev_a_right = (tm_of(a_left, b), node), (tm_of(a_right, b), node)
    dev_b_left, dev_b_right = (tm_of(a, b_left), node), (tm_of(a, b_right), node)

    bufs = ((wa, CA), (wb, CB))

    def share(ph, q):
        buf, width = bufs[ph]
        return buf.at[q, y, c, :, pl.ds(pl.multiple_of(x * width, 128), width)]

    blocks = (((w_kv, 0), (w_in, 0)), ((w_kv, CA), (w_in, CB)), ((w_out, 0), (w_hid, 0)), ((w_q, 0), (w_hid, CB)))
    for k, pair in enumerate(blocks):
        @pl.when(jnp.logical_and(zy == y, x == k))
        def _(pair=pair):
            for ph, (ref, at) in enumerate(pair):
                pltpu.make_async_copy(
                    ref.at[:, pl.ds(at, bufs[ph][1])], share(ph, zq), loc_sem.at[ph]
                ).start()

    barrier = pltpu.get_barrier_semaphore()

    def greet(k, carry):
        pl.semaphore_signal(barrier, inc=1, device_id=(tm, (node + 2 * k) % 32), device_id_type=MESH)
        pl.semaphore_signal(barrier, inc=1, device_id=((tm + k) % 16, node), device_id_type=MESH)
        return carry

    lax.fori_loop(1, 16, greet, 0)
    pl.semaphore_signal(barrier, inc=1, device_id=sibling, device_id_type=MESH)

    pl.semaphore_wait(barrier, 31)

    @pl.when(zy == y)
    def _():
        for ph in range(2):
            def send(i, carry, ph=ph):
                k = jnp.where(i % 2 == 0, 8 - i // 2, 8 + (i + 1) // 2)
                pltpu.make_async_remote_copy(
                    src_ref=share(ph, zq), dst_ref=share(ph, zq),
                    send_sem=s1_send.at[ph], recv_sem=s1_recv.at[ph, zq],
                    device_id=(tm, ((z + k) % 16) * 2 + c), device_id_type=MESH,
                ).start()
                return carry
            pltpu.make_async_copy(share(ph, zq), share(ph, zq), loc_sem.at[ph]).wait()
            lax.fori_loop(0, 15, send, 0)

    def stage1_wait(ph):
        for q in range(4):
            @pl.when(4 * q + y != z)
            def _(q=q):
                pltpu.make_async_copy(share(ph, q), share(ph, q), s1_recv.at[ph, q]).wait()

    def piece(ph, aa, bb, part=None):
        buf, width = bufs[ph]
        xx, yy = pick(aa, bb), pick(bb, aa)
        rows = pl.ds(0, 4) if part is None else pl.ds(2 * part, 2)
        return buf.at[rows, yy, c, :, pl.ds(pl.multiple_of(xx * width, 128), width)]

    def send_piece(ph, aa, bb, device, send_sem, part=None, slot=0):
        ref = piece(ph, aa, bb, part)
        pltpu.make_async_remote_copy(
            src_ref=ref, dst_ref=ref, send_sem=send_sem.at[ph],
            recv_sem=piece_sem.at[ph, aa * 4 + bb, slot],
            device_id=device, device_id_type=MESH,
        ).start()

    def wait_piece(ph, aa, bb, part=None, slot=0):
        ref = piece(ph, aa, bb, part)
        pltpu.make_async_copy(ref, ref, piece_sem.at[ph, aa * 4 + bb, slot]).wait()

    def to_sibling(ph, bb):
        buf, width = bufs[ph]

        def send(ref):
            pltpu.make_async_remote_copy(
                src_ref=ref, dst_ref=ref, send_sem=sib_send.at[ph], recv_sem=sib_recv.at[ph],
                device_id=sibling, device_id_type=MESH,
            ).start()

        @pl.when(c == 0)
        def _():
            send(buf.at[:, bb, 0])

        @pl.when(c == 1)
        def _():
            send(buf.at[:, :, 1, :, pl.ds(pl.multiple_of(bb * width, 128), width)])

    def second_ring(ph, aa):
        send_piece(ph, aa, b, dev_b_left, r2_send)
        send_piece(ph, aa, b, dev_b_right, r2_send)

    def step0(ph):
        stage1_wait(ph)
        send_piece(ph, a, b, dev_a_left, r1_send)
        send_piece(ph, a, b, dev_a_right, r1_send)
        second_ring(ph, a)

    def step1(ph):
        wait_piece(ph, a_left, b)
        send_piece(ph, a_left, b, dev_a_right, r1_send, 0, 0)
        second_ring(ph, a_left)
        wait_piece(ph, a_right, b)
        send_piece(ph, a_right, b, dev_a_left, r1_send, 1, 1)
        second_ring(ph, a_right)

    def step2(ph):
        wait_piece(ph, a_far, b, 0, 0)
        wait_piece(ph, a_far, b, 1, 1)
        second_ring(ph, a_far)
        to_sibling(ph, b)

    def step3(ph):
        for aa in (a, a_left, a_right, a_far):
            wait_piece(ph, aa, b_left)
            send_piece(ph, aa, b_left, dev_b_right, r2_send, 0, 0)
            wait_piece(ph, aa, b_right)
            send_piece(ph, aa, b_right, dev_b_left, r2_send, 1, 1)
        to_sibling(ph, b_left)
        to_sibling(ph, b_right)

    def step4(ph):
        for aa in (a, a_left, a_right, a_far):
            wait_piece(ph, aa, b_far, 0, 0)
            wait_piece(ph, aa, b_far, 1, 1)
        to_sibling(ph, b_far)

    def all_here(ph):
        ref = bufs[ph][0].at[:, :, other]
        pltpu.make_async_copy(ref, ref, sib_recv.at[ph]).wait()

    def widen(i, carry):
        at = pl.ds(pl.multiple_of(i * 64, 64), 64)
        for t in range(4):
            rbuf[t, at, :] = nbr[at, t * 128 : (t + 1) * 128].astype(F32)
        return carry

    lax.fori_loop(0, READS // 64, widen, 0)
    tpack[0:6, :] = (ev_time[...] - nb_time[...]).astype(F32)
    tpack[6:7, :] = nb_count[...].astype(F32)
    tpack[7:8, :] = jnp.zeros((1, EV), F32)
    tcol[...] = jnp.transpose(tpack[...])
    lanes = lax.broadcasted_iota(jnp.int32, (1, D), 1).astype(F32)
    freq = jnp.exp(lanes * (-9.0 * math.log(10.0) / D))

    def make_keys(i, carry):
        at = pl.ds(pl.multiple_of(i * 16, 16), 16)
        gaps = tcol[at, :]
        for j in range(SLOTS):
            gap = gaps[:, j : j + 1]
            for t, cosine in enumerate((cos_wide, cos_wide, cos_small, cos_small)):
                cut = slice(t * 128, (t + 1) * 128)
                rows = rbuf[t, pl.ds(i * (16 * SLOTS) + j, 16, stride=SLOTS), :]
                keys[j, at, cut] = rows + cosine(gap * freq[:, cut])
        return carry

    lax.fori_loop(0, EV // 16, make_keys, 0)

    step0(1)
    step0(0)
    step1(1)
    step2(1)
    step1(0)
    step2(0)
    step3(1)
    step4(1)
    step3(0)

    def wide(ref, start, width):
        return ref[:, :, :, :, pl.ds(start, width)].reshape(D, width)

    all_here(1)

    def gate(k):
        return (nn(msg[...], wide(wb, k * D, D)), nn(dst[...], wide(wb, 1536 + k * D, D)))

    gi, gh = gate(0)
    gates[0] = sigmoid(gi + gh)
    gi, gh = gate(2)
    gates[3] = gh
    gates[2] = jnp.tanh(gi + gates[0] * gh)
    gi, gh = gate(1)
    update = sigmoid(gi + gh)
    gates[1] = update
    mem[...] = ((1.0 - update) * gates[2] + update * dst[...].astype(F32)).astype(BF16)

    step4(0)
    all_here(0)

    gatt = nt(emb[...], wide(wa, 1024, 512)).astype(BF16)
    for h in range(2):
        gv[h] = nt(gatt[:, h * HEAD : (h + 1) * HEAD], wide(wa, 512 + h * HEAD, HEAD))

    lane16 = lax.broadcasted_iota(jnp.int32, (16, 128), 1)

    def row_dots(vec, out):
        def block(i, carry):
            at = pl.ds(pl.multiple_of(i * 16, 16), 16)
            acc = jnp.zeros((16, 128), F32)
            v0, v1 = vec[0, at, :], vec[1, at, :]
            for j in range(SLOTS):
                key = keys[j, at, :]
                for h, v in enumerate((v0, v1)):
                    prod = key * v
                    part = (prod[:, 0:128] + prod[:, 128:256]) + (prod[:, 256:384] + prod[:, 384:512])
                    acc = jnp.where(lane16 == h * SLOTS + j, jnp.sum(part, axis=1, keepdims=True), acc)
            out[at, :] = acc
            return carry
        lax.fori_loop(0, EV // 16, block, 0)

    row_dots(gv, gwp)

    quer = nn(mem[...], wide(wa, 1536, 512)).astype(BF16)
    for h in range(2):
        qk[h] = nt(quer[:, h * HEAD : (h + 1) * HEAD], wide(wa, h * HEAD, HEAD))

    row_dots(qk, scp)

    lane = lax.broadcasted_iota(jnp.int32, (EV, 128), 1)
    slot = jnp.where(lane >= SLOTS, lane - SLOTS, lane).astype(F32)
    head0, head1 = lane < SLOTS, jnp.logical_and(lane >= SLOTS, lane < 2 * SLOTS)
    live = jnp.logical_and(lane < 2 * SLOTS, slot < tcol[:, 6:7])
    raw = jnp.where(live, jnp.exp(scp[...] * (1.0 / 16.0)), 0.0)

    def per_head(v):
        s0 = jnp.sum(jnp.where(head0, v, 0.0), axis=1, keepdims=True)
        s1 = jnp.sum(jnp.where(head1, v, 0.0), axis=1, keepdims=True)
        return jnp.where(head0, s0, s1)

    weight = raw / per_head(raw)
    gw = gwp[...]
    wtp[...] = weight
    scp[...] = weight * (gw - per_head(weight * gw)) * (1.0 / 16.0)

    def gather_slots(i, carry):
        at = pl.ds(pl.multiple_of(i * 16, 16), 16)
        sc = scp[at, :]
        c0 = jnp.zeros((16, D), F32)
        c1 = jnp.zeros((16, D), F32)
        for j in range(SLOTS):
            key = keys[j, at, :]
            c0 = c0 + sc[:, j : j + 1] * key
            c1 = c1 + sc[:, SLOTS + j : SLOTS + j + 1] * key
        ctx[0, at, :] = c0.astype(BF16)
        ctx[1, at, :] = c1.astype(BF16)
        return carry

    lax.fori_loop(0, EV // 16, gather_slots, 0)
    gq = [nn(ctx[h], wide(wa, h * HEAD, HEAD)).astype(BF16) for h in range(2)]
    gmem[...] = emb[...].astype(F32) + (
        nt(gq[0], wide(wa, 1536, HEAD)) + nt(gq[1], wide(wa, 1536 + HEAD, HEAD))
    )

    def gru(i, carry):
        at = pl.ds(pl.multiple_of(i * 16, 16), 16)
        gm = gmem[at, :]
        r, u, cand, hc = gates[0, at, :], gates[1, at, :], gates[2, at, :], gates[3, at, :]
        gu = gm * (dst[at, :].astype(F32) - cand)
        gc = gm * (1.0 - u) * (1.0 - cand * cand)
        gin[at, 0:512] = (gc * hc * (r * (1.0 - r))).astype(BF16)
        gin[at, 512:1024] = (gu * (u * (1.0 - u))).astype(BF16)
        gin[at, 1024:1536] = gc.astype(BF16)
        gcand[at, :] = (gc * r).astype(BF16)
        gmem[at, :] = gm * u
        return carry

    lax.fori_loop(0, EV // 16, gru, 0)

    gmsg[...] = nt(gin[...], wide(wb, 0, 1536)).astype(BF16)

    def part_copy(g):
        return pltpu.make_async_remote_copy(
            src_ref=npart.at[g, other], dst_ref=nsib.at[g], send_sem=nd_send.at[g], recv_sem=nd_recv.at[g],
            device_id=sibling, device_id_type=MESH,
        )

    for g, offsets in enumerate(FAR):
        base = ((z + offsets[0]) % 16) * 64
        wanted = (lax.broadcasted_iota(jnp.int32, (256, EV), 0) + base) & 1023
        hot = (wanted == src_id[...]).astype(F32).astype(BF16)
        sums = nn(hot, gmsg[...]).astype(BF16).reshape(4, 2, OWN, D)
        npart[g, 0] = sums[:, 0]
        npart[g, 1] = sums[:, 1]
        part_copy(g).start()

    def mine(rel):
        for g, offsets in enumerate(FAR):
            if rel in offsets:
                k = offsets.index(rel)
                return npart[g, c, k].astype(F32) + nsib[g, k].astype(F32)

    chains = (((8, 9, 10, 11), -1, -5), ((7, 6, 5), 1, 5), ((12, 13, 14, 15), -1, -1), ((4, 3, 2, 1), 1, 1))

    def hop(way, s):
        steps, near, last = chains[way]
        to = (z + (last if s == len(steps) - 1 else near) + 16) % 16
        return pltpu.make_async_remote_copy(
            src_ref=nsend.at[way, s], dst_ref=nrecv.at[way, s],
            send_sem=ring_send.at[way, s], recv_sem=ring_recv.at[way, s],
            device_id=(tm, to * 2 + c), device_id_type=MESH,
        )

    def chain_step(way, s):
        total = mine(chains[way][0][s])
        if s > 0:
            hop(way, s - 1).wait_recv()
            total = total + nrecv[way, s - 1].astype(F32)
        nsend[way, s] = total.astype(BF16)
        hop(way, s).start()

    def chain_steps(s):
        for way in range(4):
            if s < len(chains[way][0]):
                chain_step(way, s)

    def spread(i, carry):
        at = pl.ds(pl.multiple_of(i * 16, 16), 16)
        sc, wt = scp[at, :], wtp[at, :]
        for j in range(SLOTS):
            s0, s1 = sc[:, j : j + 1], sc[:, SLOTS + j : SLOTS + j + 1]
            w0, w1 = wt[:, j : j + 1], wt[:, SLOTS + j : SLOTS + j + 1]
            for t in range(4):
                cut = slice(t * 128, (t + 1) * 128)
                rbuf[t, pl.ds(i * (16 * SLOTS) + j, 16, stride=SLOTS), :] = (
                    (s0 * qk[0, at, cut] + s1 * qk[1, at, cut]) + (w0 * gv[0, at, cut] + w1 * gv[1, at, cut])
                )
        return carry

    def narrow(i, carry):
        at = pl.ds(pl.multiple_of(i * 64, 64), 64)
        for t in range(4):
            gkb[at, t * 128 : (t + 1) * 128] = rbuf[t, at, :].astype(BF16)
        return carry

    def version_sums(m):
        ids = []
        for k in range(READS // 128):
            vid = owner[:, k * 128 : (k + 1) * 128] * OWN + vrow[k : k + 1, :]
            ids.append((lax.broadcasted_iota(jnp.int32, (256, 128), 0) + 256 * m == vid).astype(F32).astype(BF16))
        sums = nn(jnp.concatenate(ids, axis=1), gkb[...]).astype(BF16)
        vpart[pl.ds(8 * m, 8)] = sums.reshape(8, OWN, D)
        for t in range(8 * m, 8 * m + 8):
            @pl.when(tm != t)
            def _(t=t):
                pltpu.make_async_remote_copy(
                    src_ref=vpart.at[t], dst_ref=vbuf.at[(t - tm + 15) % 16],
                    send_sem=v_send, recv_sem=v_recv,
                    device_id=(t, node), device_id_type=MESH,
                ).start()

    lax.fori_loop(0, EV // 32, spread, 0)
    for g in range(3):
        part_copy(g).wait()
    chain_steps(0)
    lax.fori_loop(EV // 32, EV // 16, spread, 0)
    part_copy(3).wait()
    chain_steps(1)
    lax.fori_loop(0, READS // 64, narrow, 0)
    version_sums(0)
    chain_steps(2)
    version_sums(1)
    chain_steps(3)

    gdst = (nt(gin[:, 0:1024], wide(wb, 1536, 1024)) + nt(gcand[...], wide(wb, 2560, 512))) + gmem[...]
    hot = (lax.broadcasted_iota(jnp.int32, (OWN, EV), 0) == dst_loc[...]).astype(F32).astype(BF16)
    dpart[...] = mine(0) + nn(hot, gdst.astype(BF16))

    ends = [(way, len(chains[way][0]) - 1) for way in range(4)]
    for way, s in ends:
        hop(way, s).wait_recv()
    node_out[...] = dpart[...] + (
        (nrecv[0, 3].astype(F32) + nrecv[1, 2].astype(F32)) + (nrecv[2, 3].astype(F32) + nrecv[3, 3].astype(F32))
    )
    pltpu.make_async_copy(vbuf, vbuf, v_recv).wait()
    total = vpart[tm].astype(F32)
    for k in range(15):
        total = total + vbuf[k].astype(F32)
    ver_out[...] = total

    for way in range(4):
        for s in range(len(chains[way][0])):
            hop(way, s).wait_send()
    pltpu.make_async_copy(vbuf, vbuf, v_send).wait()
    for ph, (buf, width) in enumerate(bufs):
        ref = buf.at[:, :, c]
        pltpu.make_async_copy(ref, ref, sib_send.at[ph]).wait()
        ref = buf.at[:, 0:3, c, :, 0:width]
        pltpu.make_async_copy(ref, ref, r1_send.at[ph]).wait()
        ref = buf.at[:, 0:3, c]
        pltpu.make_async_copy(ref, ref, r2_send.at[ph]).wait()

    @pl.when(zy == y)
    def _():
        ref = wa.at[:, 0, c, :, 0:1920]
        pltpu.make_async_copy(ref, ref, s1_send.at[0]).wait()
        ref = wb.at[0, 0:3, :, :, 0:1920]
        pltpu.make_async_copy(ref, ref, s1_send.at[1]).wait()


def hand_out(ver_in, node_in, ver_out, node_out):
    ver_out[...] = ver_in[...]
    node_out[...] = node_in[...]


def body(
    message, dest_mem, nbr_rows, emb_grad, event_time, nbr_time, nbr_count, source_id, dest_local,
    read_owner, read_row, w_in, w_hid, w_query, w_keyval, w_out,
):
    vmem = pl.BlockSpec(memory_space=pltpu.VMEM)
    hbm = pl.BlockSpec(memory_space=pl.ANY)
    dma = pltpu.SemaphoreType.DMA
    scratch = [
        pltpu.VMEM((4, 4, 2, 16, 2048), BF16),
        pltpu.VMEM((4, 4, 2, 16, 3072), BF16),
        pltpu.VMEM((4, READS, 128), F32),
        pltpu.VMEM((SLOTS, EV, D), F32),
        pltpu.VMEM((READS, D), BF16),
        pltpu.VMEM((2, EV, D), F32),
        pltpu.VMEM((2, EV, D), F32),
        pltpu.VMEM((2, EV, D), BF16),
        pltpu.VMEM((4, EV, D), F32),
        pltpu.VMEM((EV, D), BF16),
        pltpu.VMEM((EV, D), F32),
        pltpu.VMEM((EV, 3 * D), BF16),
        pltpu.VMEM((EV, D), BF16),
        pltpu.VMEM((EV, D), BF16),
        pltpu.VMEM((EV, 8), F32),
        pltpu.VMEM((8, EV), F32),
        pltpu.VMEM((EV, 128), F32),
        pltpu.VMEM((EV, 128), F32),
        pltpu.VMEM((EV, 128), F32),
        pltpu.VMEM((16, OWN, D), BF16),
        pltpu.VMEM((15, OWN, D), BF16),
        pltpu.VMEM((4, 2, 4, OWN, D), BF16),
        pltpu.VMEM((4, 4, OWN, D), BF16),
        pltpu.VMEM((4, 4, OWN, D), BF16),
        pltpu.VMEM((4, 4, OWN, D), BF16),
        pltpu.VMEM((OWN, D), F32),
        dma((2,)),
        dma((2,)),
        dma((2, 4)),
        dma((2,)),
        dma((2,)),
        dma((2, 16, 2)),
        dma((2,)),
        dma((2,)),
        dma,
        dma,
        dma((4,)),
        dma((4,)),
        dma((4, 4)),
        dma((4, 4)),
    ]
    version_grad, node_grad = pl.pallas_call(
        kernel,
        out_shape=(jax.ShapeDtypeStruct((OWN, D), F32), jax.ShapeDtypeStruct((OWN, D), F32)),
        in_specs=[vmem] * 11 + [hbm] * 5,
        out_specs=(vmem, vmem),
        scratch_shapes=scratch,
        compiler_params=pltpu.CompilerParams(
            collective_id=0, has_side_effects=True, vmem_limit_bytes=56 * 1024 * 1024
        ),
        cost_estimate=pl.CostEstimate(
            flops=4_000_000_000, bytes_accessed=8_000_000, transcendentals=1_000_000
        ),
    )(
        message, dest_mem, nbr_rows, emb_grad,
        event_time.reshape(1, EV), nbr_time.T, nbr_count.reshape(1, EV),
        source_id.reshape(1, EV), dest_local.reshape(1, EV),
        read_owner.reshape(1, READS), read_row.reshape(READS // 128, 128),
        w_in, w_hid, w_query, w_keyval, w_out,
    )
    version_grad, node_grad = pl.pallas_call(
        hand_out,
        out_shape=(jax.ShapeDtypeStruct((OWN, D), F32), jax.ShapeDtypeStruct((OWN, D), F32)),
        in_specs=[vmem] * 2,
        out_specs=(vmem, vmem),
        compiler_params=pltpu.CompilerParams(vmem_limit_bytes=60 * 1024 * 1024),
    )(version_grad, node_grad)
    return version_grad, node_grad[None]


def solution(mesh):
    both = P(("tm", "node"))
    in_specs = (
        (P(("tm", "node"), None),) * 4
        + (both, P(("tm", "node"), None), both, both, both, P(("tm", "node"), None), both)
        + (P("node", None),) * 5
    )
    out_specs = (P(("tm", "node"), None), P("tm", "node", None))
    return jax.shard_map(body, mesh=mesh, in_specs=in_specs, out_specs=out_specs, check_vma=False)
```

```python
import math

import jax
import jax.numpy as jnp
from jax import lax
from jax.experimental import pallas as pl
from jax.experimental.pallas import tpu as pltpu
from jax.sharding import PartitionSpec as P

D = 512
HEAD = 256
SLOTS = 6
EV = 256
READS = EV * SLOTS
OWN = 32
CA = 512
CB = 768
F32 = jnp.float32
BF16 = jnp.bfloat16
MESH = pl.DeviceIdType.MESH
FAR = ((5, 6, 7, 8), (9, 10, 11, 12), (1, 2, 3, 4), (13, 14, 15, 0))


def nn(a, b):
    return lax.dot_general(a, b, (((1,), (0,)), ((), ())), preferred_element_type=F32)


def nt(a, b):
    return lax.dot_general(a, b, (((1,), (1,)), ((), ())), preferred_element_type=F32)


def sigmoid(v):
    return 0.5 * jnp.tanh(0.5 * v) + 0.5


def cos_wide(angle):
    half = 0.5 * angle
    turns = jnp.floor(half * (1.0 / math.pi) + 0.5)
    s = (half - turns * 3.140625) - turns * (math.pi - 3.140625)
    q = s * s
    p = q * (-1.0 / 39916800.0) + (1.0 / 362880.0)
    p = p * q + (-1.0 / 5040.0)
    p = p * q + (1.0 / 120.0)
    p = p * q + (-1.0 / 6.0)
    p = p * q + 1.0
    sine = p * s
    return 1.0 - 2.0 * (sine * sine)


def cos_small(angle):
    q = angle * angle
    return 1.0 + q * (q * (1.0 / 24.0) - 0.5)


def kernel(
    msg, dst, nbr, emb, ev_time, nb_time, nb_count, src_id, dst_loc, owner, vrow,
    w_in, w_hid, w_q, w_kv, w_out,
    ver_out, node_out,
    wa, wb, rbuf, keys, gkb, qk, gv, ctx, gates, mem, gmem, gin, gcand, gmsg, tcol, tpack, gwp, scp, wtp,
    vpart, vbuf, npart, nsib, nsend, nrecv, dpart,
    loc_sem, s1_send, s1_recv, r1_send, r2_send, piece_sem, sib_send, sib_recv,
    v_send, v_recv, nd_send, nd_recv, ring_send, ring_recv,
):
    tm = lax.axis_index("tm")
    node = lax.axis_index("node")
    x, y = tm >> 2, tm & 3
    z, c = node >> 1, node & 1
    other = 1 - c
    sibling = (tm, z * 2 + other)
    zq, zy = z >> 2, z & 3

    def pick(p, q):
        return jnp.where(c == 0, p, q)

    a, b = pick(x, y), pick(y, x)

    def tm_of(aa, bb):
        return pick(aa * 4 + bb, bb * 4 + aa)

    a_left, a_right, a_far = (a + 3) & 3, (a + 1) & 3, (a + 2) & 3
    b_left, b_right, b_far = (b + 3) & 3, (b + 1) & 3, (b + 2) & 3
    dev_a_left, dev_a_right = (tm_of(a_left, b), node), (tm_of(a_right, b), node)
    dev_b_left, dev_b_right = (tm_of(a, b_left), node), (tm_of(a, b_right), node)

    bufs = ((wa, CA), (wb, CB))

    def share(ph, q):
        buf, _ = bufs[ph]
        return buf.at[x, q, y, c]

    blocks = (((w_kv, 0), (w_in, 0)), ((w_kv, CA), (w_in, CB)), ((w_out, 0), (w_hid, 0)), ((w_q, 0), (w_hid, CB)))
    for k, pair in enumerate(blocks):
        @pl.when(jnp.logical_and(zy == y, x == k))
        def _(pair=pair):
            for ph, (ref, at) in enumerate(pair):
                pltpu.make_async_copy(
                    ref.at[:, pl.ds(at, bufs[ph][1])], share(ph, zq), loc_sem.at[ph]
                ).start()

    barrier = pltpu.get_barrier_semaphore()

    def greet(k, carry):
        pl.semaphore_signal(barrier, inc=1, device_id=(tm, (node + 2 * k) & 31), device_id_type=MESH)
        pl.semaphore_signal(barrier, inc=1, device_id=((tm + k) & 15, node), device_id_type=MESH)
        return carry

    lax.fori_loop(1, 16, greet, 0)
    pl.semaphore_signal(barrier, inc=1, device_id=sibling, device_id_type=MESH)

    pl.semaphore_wait(barrier, 31)

    @pl.when(zy == y)
    def _():
        for ph in range(2):
            def send(i, carry, ph=ph):
                k = jnp.where((i & 1) == 0, 8 - (i >> 1), 8 + ((i + 1) >> 1))
                pltpu.make_async_remote_copy(
                    src_ref=share(ph, zq), dst_ref=share(ph, zq),
                    send_sem=s1_send.at[ph], recv_sem=s1_recv.at[ph, zq],
                    device_id=(tm, ((z + k) & 15) * 2 + c), device_id_type=MESH,
                ).start()
                return carry
            pltpu.make_async_copy(share(ph, zq), share(ph, zq), loc_sem.at[ph]).wait()
            lax.fori_loop(0, 15, send, 0)

    def stage1_wait(ph):
        for q in range(4):
            @pl.when(4 * q + y != z)
            def _(q=q):
                pltpu.make_async_copy(share(ph, q), share(ph, q), s1_recv.at[ph, q]).wait()

    def piece(ph, aa, bb, part=None):
        buf, _ = bufs[ph]
        xx, yy = pick(aa, bb), pick(bb, aa)
        rows = pl.ds(0, 4) if part is None else pl.ds(2 * part, 2)
        return buf.at[xx, rows, yy, c]

    def send_piece(ph, aa, bb, device, send_sem, part=None, slot=0):
        ref = piece(ph, aa, bb, part)
        pltpu.make_async_remote_copy(
            src_ref=ref, dst_ref=ref, send_sem=send_sem.at[ph],
            recv_sem=piece_sem.at[ph, aa * 4 + bb, slot],
            device_id=device, device_id_type=MESH,
        ).start()

    def wait_piece(ph, aa, bb, part=None, slot=0):
        ref = piece(ph, aa, bb, part)
        pltpu.make_async_copy(ref, ref, piece_sem.at[ph, aa * 4 + bb, slot]).wait()

    def to_sibling(ph, bb):
        buf, _ = bufs[ph]

        def send(ref):
            pltpu.make_async_remote_copy(
                src_ref=ref, dst_ref=ref, send_sem=sib_send.at[ph], recv_sem=sib_recv.at[ph],
                device_id=sibling, device_id_type=MESH,
            ).start()

        @pl.when(c == 0)
        def _():
            send(buf.at[:, :, bb, 0])

        @pl.when(c == 1)
        def _():
            send(buf.at[bb, :, :, 1])

    def second_ring(ph, aa):
        send_piece(ph, aa, b, dev_b_left, r2_send)
        send_piece(ph, aa, b, dev_b_right, r2_send)

    def step0(ph):
        stage1_wait(ph)
        send_piece(ph, a, b, dev_a_left, r1_send)
        send_piece(ph, a, b, dev_a_right, r1_send)
        second_ring(ph, a)

    def step1(ph):
        wait_piece(ph, a_left, b)
        send_piece(ph, a_left, b, dev_a_right, r1_send, 0, 0)
        second_ring(ph, a_left)
        wait_piece(ph, a_right, b)
        send_piece(ph, a_right, b, dev_a_left, r1_send, 1, 1)
        second_ring(ph, a_right)

    def step2(ph):
        wait_piece(ph, a_far, b, 0, 0)
        wait_piece(ph, a_far, b, 1, 1)
        second_ring(ph, a_far)
        to_sibling(ph, b)

    def step3(ph):
        for aa in (a, a_left, a_right, a_far):
            wait_piece(ph, aa, b_left)
            send_piece(ph, aa, b_left, dev_b_right, r2_send, 0, 0)
            wait_piece(ph, aa, b_right)
            send_piece(ph, aa, b_right, dev_b_left, r2_send, 1, 1)
        to_sibling(ph, b_left)
        to_sibling(ph, b_right)

    def step4(ph):
        for aa in (a, a_left, a_right, a_far):
            wait_piece(ph, aa, b_far, 0, 0)
            wait_piece(ph, aa, b_far, 1, 1)
        to_sibling(ph, b_far)

    def all_here(ph):
        ref = bufs[ph][0].at[:, :, :, other]
        pltpu.make_async_copy(ref, ref, sib_recv.at[ph]).wait()

    def widen(i, carry):
        at = pl.ds(pl.multiple_of(i * 64, 64), 64)
        for t in range(4):
            rbuf[t, at, :] = nbr[at, t * 128 : (t + 1) * 128].astype(F32)
        return carry

    lax.fori_loop(0, READS // 64, widen, 0)
    tpack[0:6, :] = (ev_time[...] - nb_time[...]).astype(F32)
    tpack[6:7, :] = nb_count[...].astype(F32)
    tpack[7:8, :] = jnp.zeros((1, EV), F32)
    tcol[...] = jnp.transpose(tpack[...])
    lanes = lax.broadcasted_iota(jnp.int32, (1, D), 1).astype(F32)
    freq = jnp.exp(lanes * (-9.0 * math.log(10.0) / D))

    def make_keys(i, carry):
        at = pl.ds(pl.multiple_of(i * 16, 16), 16)
        gaps = tcol[at, :]
        for j in range(SLOTS):
            gap = gaps[:, j : j + 1]
            for t, cosine in enumerate((cos_wide, cos_wide, cos_small, cos_small)):
                cut = slice(t * 128, (t + 1) * 128)
                rows = rbuf[t, pl.ds(i * (16 * SLOTS) + j, 16, stride=SLOTS), :]
                keys[j, at, cut] = rows + cosine(gap * freq[:, cut])
        return carry

    lax.fori_loop(0, EV // 16, make_keys, 0)

    step0(1)
    step0(0)
    step1(1)
    step2(1)
    step1(0)
    step2(0)
    step3(1)
    step3(0)
    step4(1)

    def wide(ref, start, width):
        size = ref.shape[-1]
        out = []
        while width:
            block, at = divmod(start, size)
            take = min(width, size - at)
            out.append(ref[block, :, :, :, :, at : at + take].reshape(D, take))
            start, width = start + take, width - take
        return out[0] if len(out) == 1 else jnp.concatenate(out, axis=1)

    all_here(1)

    def gate(k):
        return (nn(msg[...], wide(wb, k * D, D)), nn(dst[...], wide(wb, 1536 + k * D, D)))

    gi, gh = gate(0)
    gates[0] = sigmoid(gi + gh)
    gi, gh = gate(2)
    gates[3] = gh
    gates[2] = jnp.tanh(gi + gates[0] * gh)
    gi, gh = gate(1)
    update = sigmoid(gi + gh)
    gates[1] = update
    mem[...] = ((1.0 - update) * gates[2] + update * dst[...].astype(F32)).astype(BF16)

    step4(0)
    all_here(0)

    gatt = nt(emb[...], wide(wa, 1024, 512)).astype(BF16)
    for h in range(2):
        gv[h] = nt(gatt[:, h * HEAD : (h + 1) * HEAD], wide(wa, 512 + h * HEAD, HEAD))

    lane16 = lax.broadcasted_iota(jnp.int32, (16, 128), 1)

    def row_dots(vec, out):
        def block(i, carry):
            at = pl.ds(pl.multiple_of(i * 16, 16), 16)
            acc = jnp.zeros((16, 128), F32)
            v0, v1 = vec[0, at, :], vec[1, at, :]
            for j in range(SLOTS):
                key = keys[j, at, :]
                for h, v in enumerate((v0, v1)):
                    prod = key * v
                    part = (prod[:, 0:128] + prod[:, 128:256]) + (prod[:, 256:384] + prod[:, 384:512])
                    acc = jnp.where(lane16 == h * SLOTS + j, jnp.sum(part, axis=1, keepdims=True), acc)
            out[at, :] = acc
            return carry
        lax.fori_loop(0, EV // 16, block, 0)

    row_dots(gv, gwp)

    quer = nn(mem[...], wide(wa, 1536, 512)).astype(BF16)
    for h in range(2):
        qk[h] = nt(quer[:, h * HEAD : (h + 1) * HEAD], wide(wa, h * HEAD, HEAD))

    row_dots(qk, scp)

    lane = lax.broadcasted_iota(jnp.int32, (EV, 128), 1)
    slot = jnp.where(lane >= SLOTS, lane - SLOTS, lane).astype(F32)
    head0, head1 = lane < SLOTS, jnp.logical_and(lane >= SLOTS, lane < 2 * SLOTS)
    live = jnp.logical_and(lane < 2 * SLOTS, slot < tcol[:, 6:7])
    raw = jnp.where(live, jnp.exp(scp[...] * (1.0 / 16.0)), 0.0)

    def per_head(v):
        s0 = jnp.sum(jnp.where(head0, v, 0.0), axis=1, keepdims=True)
        s1 = jnp.sum(jnp.where(head1, v, 0.0), axis=1, keepdims=True)
        return jnp.where(head0, s0, s1)

    weight = raw / per_head(raw)
    gw = gwp[...]
    wtp[...] = weight
    scp[...] = weight * (gw - per_head(weight * gw)) * (1.0 / 16.0)

    def gather_slots(i, carry):
        at = pl.ds(pl.multiple_of(i * 16, 16), 16)
        sc = scp[at, :]
        c0 = jnp.zeros((16, D), F32)
        c1 = jnp.zeros((16, D), F32)
        for j in range(SLOTS):
            key = keys[j, at, :]
            c0 = c0 + sc[:, j : j + 1] * key
            c1 = c1 + sc[:, SLOTS + j : SLOTS + j + 1] * key
        ctx[0, at, :] = c0.astype(BF16)
        ctx[1, at, :] = c1.astype(BF16)
        return carry

    lax.fori_loop(0, EV // 16, gather_slots, 0)
    gq = [nn(ctx[h], wide(wa, h * HEAD, HEAD)).astype(BF16) for h in range(2)]
    gmem[...] = emb[...].astype(F32) + (
        nt(gq[0], wide(wa, 1536, HEAD)) + nt(gq[1], wide(wa, 1536 + HEAD, HEAD))
    )

    def gru(i, carry):
        at = pl.ds(pl.multiple_of(i * 16, 16), 16)
        gm = gmem[at, :]
        r, u, cand, hc = gates[0, at, :], gates[1, at, :], gates[2, at, :], gates[3, at, :]
        gu = gm * (dst[at, :].astype(F32) - cand)
        gc = gm * (1.0 - u) * (1.0 - cand * cand)
        gin[at, 0:512] = (gc * hc * (r * (1.0 - r))).astype(BF16)
        gin[at, 512:1024] = (gu * (u * (1.0 - u))).astype(BF16)
        gin[at, 1024:1536] = gc.astype(BF16)
        gcand[at, :] = (gc * r).astype(BF16)
        gmem[at, :] = gm * u
        return carry

    lax.fori_loop(0, EV // 16, gru, 0)

    gmsg[...] = nt(gin[...], wide(wb, 0, 1536)).astype(BF16)

    def part_copy(g):
        return pltpu.make_async_remote_copy(
            src_ref=npart.at[g, other], dst_ref=nsib.at[g], send_sem=nd_send.at[g], recv_sem=nd_recv.at[g],
            device_id=sibling, device_id_type=MESH,
        )

    for g, offsets in enumerate(FAR):
        base = ((z + offsets[0]) & 15) * 64
        wanted = (lax.broadcasted_iota(jnp.int32, (256, EV), 0) + base) & 1023
        hot = (wanted == src_id[...]).astype(F32).astype(BF16)
        sums = nn(hot, gmsg[...]).astype(BF16).reshape(4, 2, OWN, D)
        npart[g, 0] = sums[:, 0]
        npart[g, 1] = sums[:, 1]
        part_copy(g).start()

    def mine(rel):
        for g, offsets in enumerate(FAR):
            if rel in offsets:
                k = offsets.index(rel)
                return npart[g, c, k].astype(F32) + nsib[g, k].astype(F32)

    chains = (((8, 9, 10, 11), -1, -5), ((7, 6, 5), 1, 5), ((12, 13, 14, 15), -1, -1), ((4, 3, 2, 1), 1, 1))

    def hop(way, s):
        steps, near, last = chains[way]
        to = (z + (last if s == len(steps) - 1 else near) + 16) & 15
        return pltpu.make_async_remote_copy(
            src_ref=nsend.at[way, s], dst_ref=nrecv.at[way, s],
            send_sem=ring_send.at[way, s], recv_sem=ring_recv.at[way, s],
            device_id=(tm, to * 2 + c), device_id_type=MESH,
        )

    def chain_step(way, s):
        total = mine(chains[way][0][s])
        if s > 0:
            hop(way, s - 1).wait_recv()
            total = total + nrecv[way, s - 1].astype(F32)
        nsend[way, s] = total.astype(BF16)
        hop(way, s).start()

    def chain_steps(s):
        for way in range(4):
            if s < len(chains[way][0]):
                chain_step(way, s)

    def spread(i, carry):
        at = pl.ds(pl.multiple_of(i * 16, 16), 16)
        sc, wt = scp[at, :], wtp[at, :]
        for j in range(SLOTS):
            s0, s1 = sc[:, j : j + 1], sc[:, SLOTS + j : SLOTS + j + 1]
            w0, w1 = wt[:, j : j + 1], wt[:, SLOTS + j : SLOTS + j + 1]
            for t in range(4):
                cut = slice(t * 128, (t + 1) * 128)
                rbuf[t, pl.ds(i * (16 * SLOTS) + j, 16, stride=SLOTS), :] = (
                    (s0 * qk[0, at, cut] + s1 * qk[1, at, cut]) + (w0 * gv[0, at, cut] + w1 * gv[1, at, cut])
                )
        return carry

    def narrow(i, carry):
        at = pl.ds(pl.multiple_of(i * 64, 64), 64)
        for t in range(4):
            gkb[at, t * 128 : (t + 1) * 128] = rbuf[t, at, :].astype(BF16)
        return carry

    def version_sums(m):
        ids = []
        for k in range(READS // 128):
            vid = owner[:, k * 128 : (k + 1) * 128] * OWN + vrow[k : k + 1, :]
            ids.append((lax.broadcasted_iota(jnp.int32, (256, 128), 0) + 256 * m == vid).astype(F32).astype(BF16))
        sums = nn(jnp.concatenate(ids, axis=1), gkb[...]).astype(BF16)
        vpart[pl.ds(8 * m, 8)] = sums.reshape(8, OWN, D)
        for t in range(8 * m, 8 * m + 8):
            @pl.when(tm != t)
            def _(t=t):
                pltpu.make_async_remote_copy(
                    src_ref=vpart.at[t], dst_ref=vbuf.at[(t - tm + 15) & 15],
                    send_sem=v_send, recv_sem=v_recv,
                    device_id=(t, node), device_id_type=MESH,
                ).start()

    lax.fori_loop(0, EV // 32, spread, 0)
    for g in range(3):
        part_copy(g).wait()
    chain_steps(0)
    lax.fori_loop(EV // 32, EV // 16, spread, 0)
    part_copy(3).wait()
    chain_steps(1)
    lax.fori_loop(0, READS // 64, narrow, 0)
    version_sums(0)
    chain_steps(2)
    version_sums(1)
    chain_steps(3)

    gdst = (nt(gin[:, 0:1024], wide(wb, 1536, 1024)) + nt(gcand[...], wide(wb, 2560, 512))) + gmem[...]
    hot = (lax.broadcasted_iota(jnp.int32, (OWN, EV), 0) == dst_loc[...]).astype(F32).astype(BF16)
    dpart[...] = mine(0) + nn(hot, gdst.astype(BF16))

    ends = [(way, len(chains[way][0]) - 1) for way in range(4)]
    for way, s in ends:
        hop(way, s).wait_recv()
    node_out[...] = dpart[...] + (
        (nrecv[0, 3].astype(F32) + nrecv[1, 2].astype(F32)) + (nrecv[2, 3].astype(F32) + nrecv[3, 3].astype(F32))
    )
    pltpu.make_async_copy(vbuf, vbuf, v_recv).wait()
    total = vpart[tm].astype(F32)
    for k in range(15):
        total = total + vbuf[k].astype(F32)
    ver_out[...] = total

    for way in range(4):
        for s in range(len(chains[way][0])):
            hop(way, s).wait_send()
    pltpu.make_async_copy(vbuf, vbuf, v_send).wait()
    for ph, (buf, _) in enumerate(bufs):
        ref = buf.at[:, :, :, c]
        pltpu.make_async_copy(ref, ref, sib_send.at[ph]).wait()
        ref = buf.at[0:3, :, 0, c]
        pltpu.make_async_copy(ref, ref, r1_send.at[ph]).wait()
        ref = buf.at[0:3, :, :, c]
        pltpu.make_async_copy(ref, ref, r2_send.at[ph]).wait()

    @pl.when(zy == y)
    def _():
        ref = wb.at[0:3, :, 0, 0, :, 0:640]
        pltpu.make_async_copy(ref, ref, s1_send.at[0]).wait()
        ref = wb.at[0:3, 0:3, 0, :, :, 0:640]
        pltpu.make_async_copy(ref, ref, s1_send.at[1]).wait()


def hand_out(ver_in, node_in, ver_out, node_out):
    ver_out[...] = ver_in[...]
    node_out[...] = node_in[...]


def body(
    message, dest_mem, nbr_rows, emb_grad, event_time, nbr_time, nbr_count, source_id, dest_local,
    read_owner, read_row, w_in, w_hid, w_query, w_keyval, w_out,
):
    vmem = pl.BlockSpec(memory_space=pltpu.VMEM)
    hbm = pl.BlockSpec(memory_space=pl.ANY)
    dma = pltpu.SemaphoreType.DMA
    scratch = [
        pltpu.VMEM((4, 4, 4, 2, 16, CA), BF16),
        pltpu.VMEM((4, 4, 4, 2, 16, CB), BF16),
        pltpu.VMEM((4, READS, 128), F32),
        pltpu.VMEM((SLOTS, EV, D), F32),
        pltpu.VMEM((READS, D), BF16),
        pltpu.VMEM((2, EV, D), F32),
        pltpu.VMEM((2, EV, D), F32),
        pltpu.VMEM((2, EV, D), BF16),
        pltpu.VMEM((4, EV, D), F32),
        pltpu.VMEM((EV, D), BF16),
        pltpu.VMEM((EV, D), F32),
        pltpu.VMEM((EV, 3 * D), BF16),
        pltpu.VMEM((EV, D), BF16),
        pltpu.VMEM((EV, D), BF16),
        pltpu.VMEM((EV, 8), F32),
        pltpu.VMEM((8, EV), F32),
        pltpu.VMEM((EV, 128), F32),
        pltpu.VMEM((EV, 128), F32),
        pltpu.VMEM((EV, 128), F32),
        pltpu.VMEM((16, OWN, D), BF16),
        pltpu.VMEM((15, OWN, D), BF16),
        pltpu.VMEM((4, 2, 4, OWN, D), BF16),
        pltpu.VMEM((4, 4, OWN, D), BF16),
        pltpu.VMEM((4, 4, OWN, D), BF16),
        pltpu.VMEM((4, 4, OWN, D), BF16),
        pltpu.VMEM((OWN, D), F32),
        dma((2,)),
        dma((2,)),
        dma((2, 4)),
        dma((2,)),
        dma((2,)),
        dma((2, 16, 2)),
        dma((2,)),
        dma((2,)),
        dma,
        dma,
        dma((4,)),
        dma((4,)),
        dma((4, 4)),
        dma((4, 4)),
    ]
    version_grad, node_grad = pl.pallas_call(
        kernel,
        out_shape=(jax.ShapeDtypeStruct((OWN, D), F32), jax.ShapeDtypeStruct((OWN, D), F32)),
        in_specs=[vmem] * 11 + [hbm] * 5,
        out_specs=(vmem, vmem),
        scratch_shapes=scratch,
        compiler_params=pltpu.CompilerParams(
            collective_id=0, has_side_effects=True, vmem_limit_bytes=56 * 1024 * 1024
        ),
        cost_estimate=pl.CostEstimate(
            flops=4_000_000_000, bytes_accessed=8_000_000, transcendentals=1_000_000
        ),
    )(
        message, dest_mem, nbr_rows, emb_grad,
        event_time.reshape(1, EV), nbr_time.T, nbr_count.reshape(1, EV),
        source_id.reshape(1, EV), dest_local.reshape(1, EV),
        read_owner.reshape(1, READS), read_row.reshape(READS // 128, 128),
        w_in, w_hid, w_query, w_keyval, w_out,
    )
    version_grad, node_grad = pl.pallas_call(
        hand_out,
        out_shape=(jax.ShapeDtypeStruct((OWN, D), F32), jax.ShapeDtypeStruct((OWN, D), F32)),
        in_specs=[vmem] * 2,
        out_specs=(vmem, vmem),
        compiler_params=pltpu.CompilerParams(vmem_limit_bytes=60 * 1024 * 1024),
    )(version_grad, node_grad)
    return version_grad, node_grad[None]


def solution(mesh):
    both = P(("tm", "node"))
    in_specs = (
        (P(("tm", "node"), None),) * 4
        + (both, P(("tm", "node"), None), both, both, both, P(("tm", "node"), None), both)
        + (P("node", None),) * 5
    )
    out_specs = (P(("tm", "node"), None), P("tm", "node", None))
    return jax.shard_map(body, mesh=mesh, in_specs=in_specs, out_specs=out_specs, check_vma=False)
```

```python
import math

import jax
import jax.numpy as jnp
from jax import lax
from jax.experimental import pallas as pl
from jax.experimental.pallas import tpu as pltpu
from jax.sharding import PartitionSpec as P

D = 512
HEAD = 256
SLOTS = 6
EV = 256
READS = EV * SLOTS
OWN = 32
CA = 512
CB = 768
F32 = jnp.float32
BF16 = jnp.bfloat16
MESH = pl.DeviceIdType.MESH
FAR = ((5, 6, 7, 8), (9, 10, 11, 12), (1, 2, 3, 4), (13, 14, 15, 0))


def nn(a, b):
    return lax.dot_general(a, b, (((1,), (0,)), ((), ())), preferred_element_type=F32)


def nt(a, b):
    return lax.dot_general(a, b, (((1,), (1,)), ((), ())), preferred_element_type=F32)


def sigmoid(v):
    return 0.5 * jnp.tanh(0.5 * v) + 0.5


def cos_wide(angle):
    half = 0.5 * angle
    turns = jnp.floor(half * (1.0 / math.pi) + 0.5)
    s = (half - turns * 3.140625) - turns * (math.pi - 3.140625)
    q = s * s
    p = q * (-1.0 / 39916800.0) + (1.0 / 362880.0)
    p = p * q + (-1.0 / 5040.0)
    p = p * q + (1.0 / 120.0)
    p = p * q + (-1.0 / 6.0)
    p = p * q + 1.0
    sine = p * s
    return 1.0 - 2.0 * (sine * sine)


def cos_small(angle):
    q = angle * angle
    return 1.0 + q * (q * (1.0 / 24.0) - 0.5)


def kernel(
    msg_in, dst_in, nbr_in, emb_in, ev_in, nbt_in, cnt_in, src_in, dloc_in, own_in, vrow_in,
    w_in, w_hid, w_q, w_kv, w_out,
    ver_out, node_out,
    msg, dst, nbr, emb, ev_time, nb_time, nb_count, src_id, dst_loc, owner, vrow,
    wa, wb, rbuf, keys, gkb, qk, gv, ctx, gates, mem, gmem, gin, gcand, gmsg, tcol, tpack, gwp, scp, wtp,
    vpart, vbuf, npart, nsib, nsend, nrecv, dpart,
    vcol, vids, idp,
    in_sem, loc_sem, s1_send, s1_recv, r1_send, r2_send, piece_sem, sib_send, sib_recv,
    v_send, v_recv, nd_send, nd_recv, ring_send, ring_recv,
):
    tm = lax.axis_index("tm")
    node = lax.axis_index("node")
    x, y = tm >> 2, tm & 3
    z, c = node >> 1, node & 1
    other = 1 - c
    sibling = (tm, z * 2 + other)
    zq, zy = z >> 2, z & 3

    def pick(p, q):
        return jnp.where(c == 0, p, q)

    a, b = pick(x, y), pick(y, x)

    def tm_of(aa, bb):
        return pick(aa * 4 + bb, bb * 4 + aa)

    a_left, a_right, a_far = (a + 3) & 3, (a + 1) & 3, (a + 2) & 3
    b_left, b_right, b_far = (b + 3) & 3, (b + 1) & 3, (b + 2) & 3
    dev_a_left, dev_a_right = (tm_of(a_left, b), node), (tm_of(a_right, b), node)
    dev_b_left, dev_b_right = (tm_of(a, b_left), node), (tm_of(a, b_right), node)

    bufs = ((wa, CA), (wb, CB))

    kind = (y + 2 * c) & 3

    def share(ph, q):
        buf, _ = bufs[ph]
        return buf.at[x, q, kind, c]

    inputs = (
        (nbr_in, nbr), (ev_in, ev_time), (nbt_in, nb_time), (cnt_in, nb_count), (own_in, owner), (vrow_in, vrow),
        (msg_in, msg), (dst_in, dst), (emb_in, emb), (src_in, src_id), (dloc_in, dst_loc),
    )

    def copy_in(i):
        return pltpu.make_async_copy(inputs[i][0], inputs[i][1], in_sem.at[i])

    blocks = (((w_kv, 0), (w_in, 0)), ((w_kv, CA), (w_in, CB)), ((w_out, 0), (w_hid, 0)), ((w_q, 0), (w_hid, CB)))
    for k, pair in enumerate(blocks):
        @pl.when(jnp.logical_and(zy == kind, x == k))
        def _(pair=pair):
            for ph, (ref, at) in enumerate(pair):
                pltpu.make_async_copy(
                    ref.at[:, pl.ds(at, bufs[ph][1])], share(ph, zq), loc_sem.at[ph]
                ).start()

    barrier = pltpu.get_barrier_semaphore()

    def greet(k, carry):
        pl.semaphore_signal(barrier, inc=1, device_id=(tm, (node + 2 * k) & 31), device_id_type=MESH)
        pl.semaphore_signal(barrier, inc=1, device_id=((tm + k) & 15, node), device_id_type=MESH)
        return carry

    lax.fori_loop(1, 16, greet, 0)
    pl.semaphore_signal(barrier, inc=1, device_id=sibling, device_id_type=MESH)

    for i in range(11):
        copy_in(i).start()
    pl.semaphore_wait(barrier, 31)

    @pl.when(zy == kind)
    def _():
        for ph in range(2):
            def send(i, carry, ph=ph):
                k = jnp.where((i & 1) == 0, 8 - (i >> 1), 8 + ((i + 1) >> 1))
                pltpu.make_async_remote_copy(
                    src_ref=share(ph, zq), dst_ref=share(ph, zq),
                    send_sem=s1_send.at[ph], recv_sem=s1_recv.at[ph, zq],
                    device_id=(tm, ((z + k) & 15) * 2 + c), device_id_type=MESH,
                ).start()
                return carry
            pltpu.make_async_copy(share(ph, zq), share(ph, zq), loc_sem.at[ph]).wait()
            lax.fori_loop(0, 15, send, 0)

    def stage1_wait(ph):
        for q in range(4):
            @pl.when(4 * q + kind != z)
            def _(q=q):
                pltpu.make_async_copy(share(ph, q), share(ph, q), s1_recv.at[ph, q]).wait()

    def piece(ph, aa, bb, part=None):
        buf, _ = bufs[ph]
        xx, yy = pick(aa, bb), pick(bb, (aa + 2) & 3)
        rows = pl.ds(0, 4) if part is None else pl.ds(2 * part, 2)
        return buf.at[xx, rows, yy, c]

    def send_piece(ph, aa, bb, device, send_sem, part=None, slot=0):
        ref = piece(ph, aa, bb, part)
        pltpu.make_async_remote_copy(
            src_ref=ref, dst_ref=ref, send_sem=send_sem.at[ph],
            recv_sem=piece_sem.at[ph, aa * 4 + bb, slot],
            device_id=device, device_id_type=MESH,
        ).start()

    def wait_piece(ph, aa, bb, part=None, slot=0):
        ref = piece(ph, aa, bb, part)
        pltpu.make_async_copy(ref, ref, piece_sem.at[ph, aa * 4 + bb, slot]).wait()

    def to_sibling(ph, bb):
        buf, _ = bufs[ph]

        def send(ref):
            pltpu.make_async_remote_copy(
                src_ref=ref, dst_ref=ref, send_sem=sib_send.at[ph], recv_sem=sib_recv.at[ph],
                device_id=sibling, device_id_type=MESH,
            ).start()

        @pl.when(c == 0)
        def _():
            send(buf.at[:, :, bb, 0])

        @pl.when(c == 1)
        def _():
            send(buf.at[bb, :, :, 1])

    def second_ring(ph, aa):
        send_piece(ph, aa, b, dev_b_left, r2_send)
        send_piece(ph, aa, b, dev_b_right, r2_send)

    def step0(ph):
        stage1_wait(ph)
        send_piece(ph, a, b, dev_a_left, r1_send)
        send_piece(ph, a, b, dev_a_right, r1_send)
        second_ring(ph, a)

    def step1(ph):
        wait_piece(ph, a_left, b)
        send_piece(ph, a_left, b, dev_a_right, r1_send, 0, 0)
        second_ring(ph, a_left)
        wait_piece(ph, a_right, b)
        send_piece(ph, a_right, b, dev_a_left, r1_send, 1, 1)
        second_ring(ph, a_right)

    def step2(ph):
        wait_piece(ph, a_far, b, 0, 0)
        wait_piece(ph, a_far, b, 1, 1)
        second_ring(ph, a_far)
        to_sibling(ph, b)

    def step3(ph):
        for aa in (a, a_left, a_right, a_far):
            wait_piece(ph, aa, b_left)
            send_piece(ph, aa, b_left, dev_b_right, r2_send, 0, 0)
            wait_piece(ph, aa, b_right)
            send_piece(ph, aa, b_right, dev_b_left, r2_send, 1, 1)
        to_sibling(ph, b_left)
        to_sibling(ph, b_right)

    def step4(ph):
        for aa in (a, a_left, a_right, a_far):
            wait_piece(ph, aa, b_far, 0, 0)
            wait_piece(ph, aa, b_far, 1, 1)
        to_sibling(ph, b_far)

    def all_here(ph):
        ref = bufs[ph][0].at[:, :, :, other]
        pltpu.make_async_copy(ref, ref, sib_recv.at[ph]).wait()

    def widen(i, carry):
        at = pl.ds(pl.multiple_of(i * 64, 64), 64)
        for t in range(4):
            rbuf[t, at, :] = nbr[at, t * 128 : (t + 1) * 128].astype(F32)
        return carry

    for i in range(6):
        copy_in(i).wait()
    lax.fori_loop(0, READS // 64, widen, 0)
    tpack[0:6, :] = (ev_time[...] - nb_time[...]).astype(F32)
    tpack[6:7, :] = nb_count[...].astype(F32)
    tpack[7:8, :] = jnp.zeros((1, EV), F32)
    tcol[...] = jnp.transpose(tpack[...])
    lanes = lax.broadcasted_iota(jnp.int32, (1, D), 1).astype(F32)
    freq = jnp.exp(lanes * (-9.0 * math.log(10.0) / D))

    def make_keys(i, carry):
        at = pl.ds(pl.multiple_of(i * 16, 16), 16)
        gaps = tcol[at, :]
        for j in range(SLOTS):
            gap = gaps[:, j : j + 1]
            for t, cosine in enumerate((cos_wide, cos_wide, cos_small, cos_small)):
                cut = slice(t * 128, (t + 1) * 128)
                rows = rbuf[t, pl.ds(i * (16 * SLOTS) + j, 16, stride=SLOTS), :]
                keys[j, at, cut] = rows + cosine(gap * freq[:, cut])
        return carry

    lax.fori_loop(0, EV // 16, make_keys, 0)

    for k in range(READS // 128):
        idp[k : k + 1, :] = (owner[:, k * 128 : (k + 1) * 128] * OWN + vrow[k : k + 1, :]).astype(F32)
    idp[12:16, :] = jnp.zeros((4, 128), F32)
    columns = jnp.transpose(idp[...])
    for k in range(READS // 128):
        vcol[k * 128 : (k + 1) * 128, :] = jnp.broadcast_to(columns[:, k : k + 1], (128, 128))
    for j in range(SLOTS):
        vids[j : j + 1, :] = jnp.transpose(vcol[pl.ds(j, EV, stride=SLOTS), :])[0:1, :]
    for i in range(6, 11):
        copy_in(i).wait()

    step0(1)
    step0(0)
    step1(1)
    step2(1)
    step1(0)
    step2(0)
    step3(1)
    step3(0)
    step4(1)

    def wide(ref, start, width):
        size = ref.shape[-1]
        out = []
        while width:
            block, at = divmod(start, size)
            take = min(width, size - at)
            out.append(ref[block, :, :, :, :, at : at + take].reshape(D, take))
            start, width = start + take, width - take
        return out[0] if len(out) == 1 else jnp.concatenate(out, axis=1)

    all_here(1)

    def gate(k):
        return (nn(msg[...], wide(wb, k * D, D)), nn(dst[...], wide(wb, 1536 + k * D, D)))

    gi, gh = gate(0)
    gates[0] = sigmoid(gi + gh)
    gi, gh = gate(2)
    gates[3] = gh
    gates[2] = jnp.tanh(gi + gates[0] * gh)
    gi, gh = gate(1)
    update = sigmoid(gi + gh)
    gates[1] = update
    mem[...] = ((1.0 - update) * gates[2] + update * dst[...].astype(F32)).astype(BF16)

    step4(0)
    all_here(0)

    gatt = nt(emb[...], wide(wa, 1024, 512)).astype(BF16)
    for h in range(2):
        gv[h] = nt(gatt[:, h * HEAD : (h + 1) * HEAD], wide(wa, 512 + h * HEAD, HEAD))

    lane16 = lax.broadcasted_iota(jnp.int32, (16, 128), 1)

    def row_dots(vec, out):
        def block(i, carry):
            at = pl.ds(pl.multiple_of(i * 16, 16), 16)
            acc = jnp.zeros((16, 128), F32)
            v0, v1 = vec[0, at, :], vec[1, at, :]
            for j in range(SLOTS):
                key = keys[j, at, :]
                for h, v in enumerate((v0, v1)):
                    prod = key * v
                    part = (prod[:, 0:128] + prod[:, 128:256]) + (prod[:, 256:384] + prod[:, 384:512])
                    acc = jnp.where(lane16 == h * SLOTS + j, jnp.sum(part, axis=1, keepdims=True), acc)
            out[at, :] = acc
            return carry
        lax.fori_loop(0, EV // 16, block, 0)

    row_dots(gv, gwp)

    quer = nn(mem[...], wide(wa, 1536, 512)).astype(BF16)
    for h in range(2):
        qk[h] = nt(quer[:, h * HEAD : (h + 1) * HEAD], wide(wa, h * HEAD, HEAD))

    row_dots(qk, scp)

    lane = lax.broadcasted_iota(jnp.int32, (EV, 128), 1)
    slot = jnp.where(lane >= SLOTS, lane - SLOTS, lane).astype(F32)
    head0, head1 = lane < SLOTS, jnp.logical_and(lane >= SLOTS, lane < 2 * SLOTS)
    live = jnp.logical_and(lane < 2 * SLOTS, slot < tcol[:, 6:7])
    raw = jnp.where(live, jnp.exp(scp[...] * (1.0 / 16.0)), 0.0)

    def per_head(v):
        s0 = jnp.sum(jnp.where(head0, v, 0.0), axis=1, keepdims=True)
        s1 = jnp.sum(jnp.where(head1, v, 0.0), axis=1, keepdims=True)
        return jnp.where(head0, s0, s1)

    weight = raw / per_head(raw)
    gw = gwp[...]
    wtp[...] = weight
    scp[...] = weight * (gw - per_head(weight * gw)) * (1.0 / 16.0)

    def gather_slots(i, carry):
        at = pl.ds(pl.multiple_of(i * 16, 16), 16)
        sc = scp[at, :]
        c0 = jnp.zeros((16, D), F32)
        c1 = jnp.zeros((16, D), F32)
        for j in range(SLOTS):
            key = keys[j, at, :]
            c0 = c0 + sc[:, j : j + 1] * key
            c1 = c1 + sc[:, SLOTS + j : SLOTS + j + 1] * key
        ctx[0, at, :] = c0.astype(BF16)
        ctx[1, at, :] = c1.astype(BF16)
        return carry

    lax.fori_loop(0, EV // 16, gather_slots, 0)
    gq = [nn(ctx[h], wide(wa, h * HEAD, HEAD)).astype(BF16) for h in range(2)]
    gmem[...] = emb[...].astype(F32) + (
        nt(gq[0], wide(wa, 1536, HEAD)) + nt(gq[1], wide(wa, 1536 + HEAD, HEAD))
    )

    def gru(i, carry):
        at = pl.ds(pl.multiple_of(i * 16, 16), 16)
        gm = gmem[at, :]
        r, u, cand, hc = gates[0, at, :], gates[1, at, :], gates[2, at, :], gates[3, at, :]
        gu = gm * (dst[at, :].astype(F32) - cand)
        gc = gm * (1.0 - u) * (1.0 - cand * cand)
        gin[at, 0:512] = (gc * hc * (r * (1.0 - r))).astype(BF16)
        gin[at, 512:1024] = (gu * (u * (1.0 - u))).astype(BF16)
        gin[at, 1024:1536] = gc.astype(BF16)
        gcand[at, :] = (gc * r).astype(BF16)
        gmem[at, :] = gm * u
        return carry

    lax.fori_loop(0, EV // 16, gru, 0)

    gmsg[...] = nt(gin[...], wide(wb, 0, 1536)).astype(BF16)

    def part_copy(g):
        return pltpu.make_async_remote_copy(
            src_ref=npart.at[g, other], dst_ref=nsib.at[g], send_sem=nd_send.at[g], recv_sem=nd_recv.at[g],
            device_id=sibling, device_id_type=MESH,
        )

    for g, offsets in enumerate(FAR):
        base = ((z + offsets[0]) & 15) * 64
        wanted = (lax.broadcasted_iota(jnp.int32, (256, EV), 0) + base) & 1023
        hot = (wanted == src_id[...]).astype(F32).astype(BF16)
        sums = nn(hot, gmsg[...]).astype(BF16).reshape(4, 2, OWN, D)
        npart[g, 0] = sums[:, 0]
        npart[g, 1] = sums[:, 1]
        part_copy(g).start()

    def mine(rel):
        for g, offsets in enumerate(FAR):
            if rel in offsets:
                k = offsets.index(rel)
                return npart[g, c, k].astype(F32) + nsib[g, k].astype(F32)

    chains = (((8, 9, 10, 11), -1, -5), ((7, 6, 5), 1, 5), ((12, 13, 14, 15), -1, -1), ((4, 3, 2, 1), 1, 1))

    def hop(way, s):
        steps, near, last = chains[way]
        to = (z + (last if s == len(steps) - 1 else near) + 16) & 15
        return pltpu.make_async_remote_copy(
            src_ref=nsend.at[way, s], dst_ref=nrecv.at[way, s],
            send_sem=ring_send.at[way, s], recv_sem=ring_recv.at[way, s],
            device_id=(tm, to * 2 + c), device_id_type=MESH,
        )

    def chain_step(way, s):
        total = mine(chains[way][0][s])
        if s > 0:
            hop(way, s - 1).wait_recv()
            total = total + nrecv[way, s - 1].astype(F32)
        nsend[way, s] = total.astype(BF16)
        hop(way, s).start()

    def chain_steps(s):
        for way in range(4):
            if s < len(chains[way][0]):
                chain_step(way, s)

    def spread(i, carry):
        at = pl.ds(pl.multiple_of(i * 16, 16), 16)
        sc, wt = scp[at, :], wtp[at, :]
        for j in range(SLOTS):
            s0, s1 = sc[:, j : j + 1], sc[:, SLOTS + j : SLOTS + j + 1]
            w0, w1 = wt[:, j : j + 1], wt[:, SLOTS + j : SLOTS + j + 1]
            gkb[j, at, :] = (
                (s0 * qk[0, at, :] + s1 * qk[1, at, :]) + (w0 * gv[0, at, :] + w1 * gv[1, at, :])
            ).astype(BF16)
        return carry

    def version_sums(m):
        wanted = (lax.broadcasted_iota(jnp.int32, (256, 128), 0) + 256 * m).astype(F32)
        ids = []
        for k in range(READS // 128):
            vid = vids[k // 2 : k // 2 + 1, (k % 2) * 128 : (k % 2) * 128 + 128]
            ids.append((wanted == vid).astype(F32).astype(BF16))
        sums = nn(jnp.concatenate(ids, axis=1), gkb[...].reshape(READS, D)).astype(BF16)
        vpart[pl.ds(8 * m, 8)] = sums.reshape(8, OWN, D)
        for t in range(8 * m, 8 * m + 8):
            @pl.when(tm != t)
            def _(t=t):
                pltpu.make_async_remote_copy(
                    src_ref=vpart.at[t], dst_ref=vbuf.at[(t - tm + 15) & 15],
                    send_sem=v_send, recv_sem=v_recv,
                    device_id=(t, node), device_id_type=MESH,
                ).start()

    lax.fori_loop(0, EV // 32, spread, 0)
    for g in range(3):
        part_copy(g).wait()
    chain_steps(0)
    lax.fori_loop(EV // 32, EV // 16, spread, 0)
    version_sums(0)
    part_copy(3).wait()
    chain_steps(1)
    version_sums(1)
    chain_steps(2)

    gdst = (nt(gin[:, 0:1024], wide(wb, 1536, 1024)) + nt(gcand[...], wide(wb, 2560, 512))) + gmem[...]
    hot = (lax.broadcasted_iota(jnp.int32, (OWN, EV), 0) == dst_loc[...]).astype(F32).astype(BF16)
    dpart[...] = mine(0) + nn(hot, gdst.astype(BF16))
    chain_steps(3)

    ends = [(way, len(chains[way][0]) - 1) for way in range(4)]
    for way, s in ends:
        hop(way, s).wait_recv()
    node_out[...] = dpart[...] + (
        (nrecv[0, 3].astype(F32) + nrecv[1, 2].astype(F32)) + (nrecv[2, 3].astype(F32) + nrecv[3, 3].astype(F32))
    )
    pltpu.make_async_copy(vbuf, vbuf, v_recv).wait()
    total = vpart[tm].astype(F32)
    for k in range(15):
        total = total + vbuf[k].astype(F32)
    ver_out[...] = total

    for way in range(4):
        for s in range(len(chains[way][0])):
            hop(way, s).wait_send()
    pltpu.make_async_copy(vbuf, vbuf, v_send).wait()
    for ph, (buf, _) in enumerate(bufs):
        ref = buf.at[:, :, :, c]
        pltpu.make_async_copy(ref, ref, sib_send.at[ph]).wait()
        ref = buf.at[0:3, :, 0, c]
        pltpu.make_async_copy(ref, ref, r1_send.at[ph]).wait()
        ref = buf.at[0:3, :, :, c]
        pltpu.make_async_copy(ref, ref, r2_send.at[ph]).wait()

    @pl.when(zy == kind)
    def _():
        ref = wb.at[0:3, :, 0, 0, :, 0:640]
        pltpu.make_async_copy(ref, ref, s1_send.at[0]).wait()
        ref = wb.at[0:3, 0:3, 0, :, :, 0:640]
        pltpu.make_async_copy(ref, ref, s1_send.at[1]).wait()


def hand_out(ver_in, node_in, ver_out, node_out):
    ver_out[...] = ver_in[...]
    node_out[...] = node_in[...]


def body(
    message, dest_mem, nbr_rows, emb_grad, event_time, nbr_time, nbr_count, source_id, dest_local,
    read_owner, read_row, w_in, w_hid, w_query, w_keyval, w_out,
):
    vmem = pl.BlockSpec(memory_space=pltpu.VMEM)
    hbm = pl.BlockSpec(memory_space=pl.ANY)
    dma = pltpu.SemaphoreType.DMA
    scratch = [
        pltpu.VMEM((EV, D), BF16),
        pltpu.VMEM((EV, D), BF16),
        pltpu.VMEM((READS, D), BF16),
        pltpu.VMEM((EV, D), BF16),
        pltpu.VMEM((1, EV), jnp.int32),
        pltpu.VMEM((SLOTS, EV), jnp.int32),
        pltpu.VMEM((1, EV), jnp.int32),
        pltpu.VMEM((1, EV), jnp.int32),
        pltpu.VMEM((1, EV), jnp.int32),
        pltpu.VMEM((1, READS), jnp.int32),
        pltpu.VMEM((READS // 128, 128), jnp.int32),
        pltpu.VMEM((4, 4, 4, 2, 16, CA), BF16),
        pltpu.VMEM((4, 4, 4, 2, 16, CB), BF16),
        pltpu.VMEM((4, READS, 128), F32),
        pltpu.VMEM((SLOTS, EV, D), F32),
        pltpu.VMEM((SLOTS, EV, D), BF16),
        pltpu.VMEM((2, EV, D), F32),
        pltpu.VMEM((2, EV, D), F32),
        pltpu.VMEM((2, EV, D), BF16),
        pltpu.VMEM((4, EV, D), F32),
        pltpu.VMEM((EV, D), BF16),
        pltpu.VMEM((EV, D), F32),
        pltpu.VMEM((EV, 3 * D), BF16),
        pltpu.VMEM((EV, D), BF16),
        pltpu.VMEM((EV, D), BF16),
        pltpu.VMEM((EV, 8), F32),
        pltpu.VMEM((8, EV), F32),
        pltpu.VMEM((EV, 128), F32),
        pltpu.VMEM((EV, 128), F32),
        pltpu.VMEM((EV, 128), F32),
        pltpu.VMEM((16, OWN, D), BF16),
        pltpu.VMEM((15, OWN, D), BF16),
        pltpu.VMEM((4, 2, 4, OWN, D), BF16),
        pltpu.VMEM((4, 4, OWN, D), BF16),
        pltpu.VMEM((4, 4, OWN, D), BF16),
        pltpu.VMEM((4, 4, OWN, D), BF16),
        pltpu.VMEM((OWN, D), F32),
        pltpu.VMEM((READS, 128), F32),
        pltpu.VMEM((8, EV), F32),
        pltpu.VMEM((16, 128), F32),
        dma((11,)),
        dma((2,)),
        dma((2,)),
        dma((2, 4)),
        dma((2,)),
        dma((2,)),
        dma((2, 16, 2)),
        dma((2,)),
        dma((2,)),
        dma,
        dma,
        dma((4,)),
        dma((4,)),
        dma((4, 4)),
        dma((4, 4)),
    ]
    version_grad, node_grad = pl.pallas_call(
        kernel,
        out_shape=(jax.ShapeDtypeStruct((OWN, D), F32), jax.ShapeDtypeStruct((OWN, D), F32)),
        in_specs=[hbm] * 16,
        out_specs=(vmem, vmem),
        scratch_shapes=scratch,
        compiler_params=pltpu.CompilerParams(
            collective_id=0, has_side_effects=True, vmem_limit_bytes=56 * 1024 * 1024
        ),
        cost_estimate=pl.CostEstimate(
            flops=4_000_000_000, bytes_accessed=8_000_000, transcendentals=1_000_000
        ),
    )(
        message, dest_mem, nbr_rows, emb_grad,
        event_time.reshape(1, EV), nbr_time.T, nbr_count.reshape(1, EV),
        source_id.reshape(1, EV), dest_local.reshape(1, EV),
        read_owner.reshape(1, READS), read_row.reshape(READS // 128, 128),
        w_in, w_hid, w_query, w_keyval, w_out,
    )
    version_grad, node_grad = pl.pallas_call(
        hand_out,
        out_shape=(jax.ShapeDtypeStruct((OWN, D), F32), jax.ShapeDtypeStruct((OWN, D), F32)),
        in_specs=[vmem] * 2,
        out_specs=(vmem, vmem),
        compiler_params=pltpu.CompilerParams(vmem_limit_bytes=60 * 1024 * 1024),
    )(version_grad, node_grad)
    return version_grad, node_grad[None]


def solution(mesh):
    both = P(("tm", "node"))
    in_specs = (
        (P(("tm", "node"), None),) * 4
        + (both, P(("tm", "node"), None), both, both, both, P(("tm", "node"), None), both)
        + (P("node", None),) * 5
    )
    out_specs = (P(("tm", "node"), None), P("tm", "node", None))
    return jax.shard_map(body, mesh=mesh, in_specs=in_specs, out_specs=out_specs, check_vma=False)
```

```python
import math

import jax
import jax.numpy as jnp
from jax import lax
from jax.experimental import pallas as pl
from jax.experimental.pallas import tpu as pltpu
from jax.sharding import PartitionSpec as P

D = 512
HEAD = 256
SLOTS = 6
EV = 256
READS = EV * SLOTS
OWN = 32
CA = 512
CB = 768
F32 = jnp.float32
BF16 = jnp.bfloat16
MESH = pl.DeviceIdType.MESH
FAR = ((5, 6, 7, 8), (9, 10, 11, 12), (1, 2, 3, 4), (13, 14, 15, 0))


def nn(a, b):
    return lax.dot_general(a, b, (((1,), (0,)), ((), ())), preferred_element_type=F32)


def nt(a, b):
    return lax.dot_general(a, b, (((1,), (1,)), ((), ())), preferred_element_type=F32)


def sigmoid(v):
    return 0.5 * jnp.tanh(0.5 * v) + 0.5


def cos_wide(angle):
    half = 0.5 * angle
    turns = jnp.floor(half * (1.0 / math.pi) + 0.5)
    s = (half - turns * 3.140625) - turns * (math.pi - 3.140625)
    q = s * s
    p = q * (-1.0 / 39916800.0) + (1.0 / 362880.0)
    p = p * q + (-1.0 / 5040.0)
    p = p * q + (1.0 / 120.0)
    p = p * q + (-1.0 / 6.0)
    p = p * q + 1.0
    sine = p * s
    return 1.0 - 2.0 * (sine * sine)


def cos_small(angle):
    q = angle * angle
    return 1.0 + q * (q * (1.0 / 24.0) - 0.5)


def kernel(
    msg_in, dst_in, nbr_in, emb_in, ev_in, nbt_in, cnt_in, src_in, dloc_in, own_in, vrow_in,
    w_in, w_hid, w_q, w_kv, w_out,
    ver_out, node_out,
    msg, dst, nbr, emb, ev_time, nb_time, nb_count, src_id, dst_loc, owner, vrow,
    wa, wb, rbuf, keys, gkb, qk, gv, ctx, gates, mem, gmem, gin, gcand, gmsg, tcol, tpack, gwp, scp, wtp,
    vpart, vbuf, npart, nsib, nsend, nrecv, dpart,
    vcol, vids, idp,
    in_sem, loc_sem, s1_send, s1_recv, r1_send, r2_send, piece_sem, sib_send, sib_recv,
    v_send, v_recv, nd_send, nd_recv, ring_send, ring_recv,
):
    tm = lax.axis_index("tm")
    node = lax.axis_index("node")
    x, y = tm >> 2, tm & 3
    z, c = node >> 1, node & 1
    other = 1 - c
    sibling = (tm, z * 2 + other)
    zq, zy = z >> 2, z & 3

    def pick(p, q):
        return jnp.where(c == 0, p, q)

    a, b = pick(x, y), pick(y, x)

    def tm_of(aa, bb):
        return pick(aa * 4 + bb, bb * 4 + aa)

    a_left, a_right, a_far = (a + 3) & 3, (a + 1) & 3, (a + 2) & 3
    b_left, b_right, b_far = (b + 3) & 3, (b + 1) & 3, (b + 2) & 3
    dev_a_left, dev_a_right = (tm_of(a_left, b), node), (tm_of(a_right, b), node)
    dev_b_left, dev_b_right = (tm_of(a, b_left), node), (tm_of(a, b_right), node)

    bufs = ((wa, CA), (wb, CB))

    kind = (y + 2 * c) & 3

    def share(ph, q):
        buf, _ = bufs[ph]
        return buf.at[x, q, kind, c]

    inputs = (
        (nbr_in, nbr), (ev_in, ev_time), (nbt_in, nb_time), (cnt_in, nb_count), (own_in, owner), (vrow_in, vrow),
        (msg_in, msg), (dst_in, dst), (emb_in, emb), (src_in, src_id), (dloc_in, dst_loc),
    )

    def copy_in(i):
        return pltpu.make_async_copy(inputs[i][0], inputs[i][1], in_sem.at[i])

    blocks = (((w_kv, 0), (w_in, 0)), ((w_kv, CA), (w_in, CB)), ((w_out, 0), (w_hid, 0)), ((w_q, 0), (w_hid, CB)))
    for k, pair in enumerate(blocks):
        @pl.when(jnp.logical_and(zy == kind, x == k))
        def _(pair=pair):
            for ph, (ref, at) in enumerate(pair):
                pltpu.make_async_copy(
                    ref.at[:, pl.ds(at, bufs[ph][1])], share(ph, zq), loc_sem.at[ph]
                ).start()

    barrier = pltpu.get_barrier_semaphore()

    def greet(k, carry):
        pl.semaphore_signal(barrier, inc=1, device_id=(tm, (node + 2 * k) & 31), device_id_type=MESH)
        pl.semaphore_signal(barrier, inc=1, device_id=((tm + k) & 15, node), device_id_type=MESH)
        return carry

    lax.fori_loop(1, 16, greet, 0)
    pl.semaphore_signal(barrier, inc=1, device_id=sibling, device_id_type=MESH)

    for i in range(11):
        copy_in(i).start()
    pl.semaphore_wait(barrier, 31)

    @pl.when(zy == kind)
    def _():
        for ph in range(2):
            def send(i, carry, ph=ph):
                k = jnp.where((i & 1) == 0, 8 - (i >> 1), 8 + ((i + 1) >> 1))
                pltpu.make_async_remote_copy(
                    src_ref=share(ph, zq), dst_ref=share(ph, zq),
                    send_sem=s1_send.at[ph], recv_sem=s1_recv.at[ph, zq],
                    device_id=(tm, ((z + k) & 15) * 2 + c), device_id_type=MESH,
                ).start()
                return carry
            pltpu.make_async_copy(share(ph, zq), share(ph, zq), loc_sem.at[ph]).wait()
            lax.fori_loop(0, 15, send, 0)

    def stage1_wait(ph):
        for q in range(4):
            @pl.when(4 * q + kind != z)
            def _(q=q):
                pltpu.make_async_copy(share(ph, q), share(ph, q), s1_recv.at[ph, q]).wait()

    def piece(ph, aa, bb, part=None):
        buf, _ = bufs[ph]
        xx, yy = pick(aa, bb), pick(bb, (aa + 2) & 3)
        rows = pl.ds(0, 4) if part is None else pl.ds(2 * part, 2)
        return buf.at[xx, rows, yy, c]

    def send_piece(ph, aa, bb, device, send_sem, part=None, slot=0):
        ref = piece(ph, aa, bb, part)
        pltpu.make_async_remote_copy(
            src_ref=ref, dst_ref=ref, send_sem=send_sem.at[ph],
            recv_sem=piece_sem.at[ph, aa * 4 + bb, slot],
            device_id=device, device_id_type=MESH,
        ).start()

    def wait_piece(ph, aa, bb, part=None, slot=0):
        ref = piece(ph, aa, bb, part)
        pltpu.make_async_copy(ref, ref, piece_sem.at[ph, aa * 4 + bb, slot]).wait()

    def to_sibling(ph, bb):
        buf, _ = bufs[ph]

        def send(ref):
            pltpu.make_async_remote_copy(
                src_ref=ref, dst_ref=ref, send_sem=sib_send.at[ph], recv_sem=sib_recv.at[ph],
                device_id=sibling, device_id_type=MESH,
            ).start()

        @pl.when(c == 0)
        def _():
            send(buf.at[:, :, bb, 0])

        @pl.when(c == 1)
        def _():
            send(buf.at[bb, :, :, 1])

    def second_ring(ph, aa):
        send_piece(ph, aa, b, dev_b_left, r2_send)
        send_piece(ph, aa, b, dev_b_right, r2_send)

    def step0(ph):
        stage1_wait(ph)
        send_piece(ph, a, b, dev_a_left, r1_send)
        send_piece(ph, a, b, dev_a_right, r1_send)
        second_ring(ph, a)

    def step1(ph):
        wait_piece(ph, a_left, b)
        send_piece(ph, a_left, b, dev_a_right, r1_send, 0, 0)
        second_ring(ph, a_left)
        wait_piece(ph, a_right, b)
        send_piece(ph, a_right, b, dev_a_left, r1_send, 1, 1)
        second_ring(ph, a_right)

    def step2(ph):
        wait_piece(ph, a_far, b, 0, 0)
        wait_piece(ph, a_far, b, 1, 1)
        second_ring(ph, a_far)
        to_sibling(ph, b)

    def step3(ph):
        for aa in (a, a_left, a_right, a_far):
            wait_piece(ph, aa, b_left)
            send_piece(ph, aa, b_left, dev_b_right, r2_send, 0, 0)
            wait_piece(ph, aa, b_right)
            send_piece(ph, aa, b_right, dev_b_left, r2_send, 1, 1)
        to_sibling(ph, b_left)
        to_sibling(ph, b_right)

    def step4(ph):
        for aa in (a, a_left, a_right, a_far):
            wait_piece(ph, aa, b_far, 0, 0)
            wait_piece(ph, aa, b_far, 1, 1)
        to_sibling(ph, b_far)

    def all_here(ph):
        ref = bufs[ph][0].at[:, :, :, other]
        pltpu.make_async_copy(ref, ref, sib_recv.at[ph]).wait()

    def widen(i, carry):
        at = pl.ds(pl.multiple_of(i * 64, 64), 64)
        for t in range(4):
            rbuf[t, at, :] = nbr[at, t * 128 : (t + 1) * 128].astype(F32)
        return carry

    for i in range(6):
        copy_in(i).wait()
    lax.fori_loop(0, READS // 64, widen, 0)
    tpack[0:6, :] = (ev_time[...] - nb_time[...]).astype(F32)
    tpack[6:7, :] = nb_count[...].astype(F32)
    tpack[7:8, :] = jnp.zeros((1, EV), F32)
    tcol[...] = jnp.transpose(tpack[...])
    lanes = lax.broadcasted_iota(jnp.int32, (1, D), 1).astype(F32)
    freq = jnp.exp(lanes * (-9.0 * math.log(10.0) / D))

    def make_keys(i, carry):
        at = pl.ds(pl.multiple_of(i * 16, 16), 16)
        gaps = tcol[at, :]
        for j in range(SLOTS):
            gap = gaps[:, j : j + 1]
            for t, cosine in enumerate((cos_wide, cos_wide, cos_small, cos_small)):
                cut = slice(t * 128, (t + 1) * 128)
                rows = rbuf[t, pl.ds(i * (16 * SLOTS) + j, 16, stride=SLOTS), :]
                keys[j, at, cut] = rows + cosine(gap * freq[:, cut])
        return carry

    lax.fori_loop(0, EV // 16, make_keys, 0)

    for k in range(READS // 128):
        idp[k : k + 1, :] = (owner[:, k * 128 : (k + 1) * 128] * OWN + vrow[k : k + 1, :]).astype(F32)
    idp[12:16, :] = jnp.zeros((4, 128), F32)
    columns = jnp.transpose(idp[...])
    for k in range(READS // 128):
        vcol[k * 128 : (k + 1) * 128, :] = jnp.broadcast_to(columns[:, k : k + 1], (128, 128))
    for j in range(SLOTS):
        vids[j : j + 1, :] = jnp.transpose(vcol[pl.ds(j, EV, stride=SLOTS), :])[0:1, :]
    for i in range(6, 11):
        copy_in(i).wait()

    step0(1)
    step0(0)
    step1(1)
    step2(1)
    step1(0)
    step2(0)
    step3(1)
    step3(0)
    step4(1)
    step4(0)

    def wide(ref, start, width):
        size = ref.shape[-1]
        out = []
        while width:
            block, at = divmod(start, size)
            take = min(width, size - at)
            out.append(ref[block, :, :, :, :, at : at + take].reshape(D, take))
            start, width = start + take, width - take
        return out[0] if len(out) == 1 else jnp.concatenate(out, axis=1)

    all_here(1)

    def gate(k):
        return (nn(msg[...], wide(wb, k * D, D)), nn(dst[...], wide(wb, 1536 + k * D, D)))

    gi, gh = gate(0)
    gates[0] = sigmoid(gi + gh)
    gi, gh = gate(2)
    gates[3] = gh
    gates[2] = jnp.tanh(gi + gates[0] * gh)
    gi, gh = gate(1)
    update = sigmoid(gi + gh)
    gates[1] = update
    mem[...] = ((1.0 - update) * gates[2] + update * dst[...].astype(F32)).astype(BF16)

    all_here(0)

    gatt = nt(emb[...], wide(wa, 1024, 512)).astype(BF16)
    for h in range(2):
        gv[h] = nt(gatt[:, h * HEAD : (h + 1) * HEAD], wide(wa, 512 + h * HEAD, HEAD))

    lane16 = lax.broadcasted_iota(jnp.int32, (16, 128), 1)

    def row_dots(vec, out):
        def block(i, carry):
            at = pl.ds(pl.multiple_of(i * 16, 16), 16)
            acc = jnp.zeros((16, 128), F32)
            v0, v1 = vec[0, at, :], vec[1, at, :]
            for j in range(SLOTS):
                key = keys[j, at, :]
                for h, v in enumerate((v0, v1)):
                    prod = key * v
                    part = (prod[:, 0:128] + prod[:, 128:256]) + (prod[:, 256:384] + prod[:, 384:512])
                    acc = jnp.where(lane16 == h * SLOTS + j, jnp.sum(part, axis=1, keepdims=True), acc)
            out[at, :] = acc
            return carry
        lax.fori_loop(0, EV // 16, block, 0)

    row_dots(gv, gwp)

    quer = nn(mem[...], wide(wa, 1536, 512)).astype(BF16)
    for h in range(2):
        qk[h] = nt(quer[:, h * HEAD : (h + 1) * HEAD], wide(wa, h * HEAD, HEAD))

    row_dots(qk, scp)

    lane = lax.broadcasted_iota(jnp.int32, (EV, 128), 1)
    slot = jnp.where(lane >= SLOTS, lane - SLOTS, lane).astype(F32)
    head0, head1 = lane < SLOTS, jnp.logical_and(lane >= SLOTS, lane < 2 * SLOTS)
    live = jnp.logical_and(lane < 2 * SLOTS, slot < tcol[:, 6:7])
    raw = jnp.where(live, jnp.exp(scp[...] * (1.0 / 16.0)), 0.0)

    def per_head(v):
        s0 = jnp.sum(jnp.where(head0, v, 0.0), axis=1, keepdims=True)
        s1 = jnp.sum(jnp.where(head1, v, 0.0), axis=1, keepdims=True)
        return jnp.where(head0, s0, s1)

    weight = raw / per_head(raw)
    gw = gwp[...]
    wtp[...] = weight
    scp[...] = weight * (gw - per_head(weight * gw)) * (1.0 / 16.0)

    def gather_slots(i, carry):
        at = pl.ds(pl.multiple_of(i * 16, 16), 16)
        sc = scp[at, :]
        c0 = jnp.zeros((16, D), F32)
        c1 = jnp.zeros((16, D), F32)
        for j in range(SLOTS):
            key = keys[j, at, :]
            c0 = c0 + sc[:, j : j + 1] * key
            c1 = c1 + sc[:, SLOTS + j : SLOTS + j + 1] * key
        ctx[0, at, :] = c0.astype(BF16)
        ctx[1, at, :] = c1.astype(BF16)
        return carry

    lax.fori_loop(0, EV // 16, gather_slots, 0)
    gq = [nn(ctx[h], wide(wa, h * HEAD, HEAD)).astype(BF16) for h in range(2)]
    gmem[...] = emb[...].astype(F32) + (
        nt(gq[0], wide(wa, 1536, HEAD)) + nt(gq[1], wide(wa, 1536 + HEAD, HEAD))
    )

    def gru(i, carry):
        at = pl.ds(pl.multiple_of(i * 16, 16), 16)
        gm = gmem[at, :]
        r, u, cand, hc = gates[0, at, :], gates[1, at, :], gates[2, at, :], gates[3, at, :]
        gu = gm * (dst[at, :].astype(F32) - cand)
        gc = gm * (1.0 - u) * (1.0 - cand * cand)
        gin[at, 0:512] = (gc * hc * (r * (1.0 - r))).astype(BF16)
        gin[at, 512:1024] = (gu * (u * (1.0 - u))).astype(BF16)
        gin[at, 1024:1536] = gc.astype(BF16)
        gcand[at, :] = (gc * r).astype(BF16)
        gmem[at, :] = gm * u
        return carry

    lax.fori_loop(0, EV // 16, gru, 0)

    gmsg[...] = nt(gin[...], wide(wb, 0, 1536)).astype(BF16)

    def part_copy(g):
        return pltpu.make_async_remote_copy(
            src_ref=npart.at[g, other], dst_ref=nsib.at[g], send_sem=nd_send.at[g], recv_sem=nd_recv.at[g],
            device_id=sibling, device_id_type=MESH,
        )

    for g, offsets in enumerate(FAR):
        base = ((z + offsets[0]) & 15) * 64
        wanted = (lax.broadcasted_iota(jnp.int32, (256, EV), 0) + base) & 1023
        hot = (wanted == src_id[...]).astype(F32).astype(BF16)
        sums = nn(hot, gmsg[...]).astype(BF16).reshape(4, 2, OWN, D)
        npart[g, 0] = sums[:, 0]
        npart[g, 1] = sums[:, 1]
        part_copy(g).start()

    def mine(rel):
        for g, offsets in enumerate(FAR):
            if rel in offsets:
                k = offsets.index(rel)
                return npart[g, c, k].astype(F32) + nsib[g, k].astype(F32)

    chains = (((8, 9, 10, 11), -1, -5), ((7, 6, 5), 1, 5), ((12, 13, 14, 15), -1, -1), ((4, 3, 2, 1), 1, 1))

    def hop(way, s):
        steps, near, last = chains[way]
        to = (z + (last if s == len(steps) - 1 else near) + 16) & 15
        return pltpu.make_async_remote_copy(
            src_ref=nsend.at[way, s], dst_ref=nrecv.at[way, s],
            send_sem=ring_send.at[way, s], recv_sem=ring_recv.at[way, s],
            device_id=(tm, to * 2 + c), device_id_type=MESH,
        )

    def chain_step(way, s):
        total = mine(chains[way][0][s])
        if s > 0:
            hop(way, s - 1).wait_recv()
            total = total + nrecv[way, s - 1].astype(F32)
        nsend[way, s] = total.astype(BF16)
        hop(way, s).start()

    def chain_steps(s):
        for way in range(4):
            if s < len(chains[way][0]):
                chain_step(way, s)

    def spread(i, carry):
        at = pl.ds(pl.multiple_of(i * 16, 16), 16)
        sc, wt = scp[at, :], wtp[at, :]
        for j in range(SLOTS):
            s0, s1 = sc[:, j : j + 1], sc[:, SLOTS + j : SLOTS + j + 1]
            w0, w1 = wt[:, j : j + 1], wt[:, SLOTS + j : SLOTS + j + 1]
            gkb[j, at, :] = (
                (s0 * qk[0, at, :] + s1 * qk[1, at, :]) + (w0 * gv[0, at, :] + w1 * gv[1, at, :])
            ).astype(BF16)
        return carry

    def version_sums(m):
        wanted = (lax.broadcasted_iota(jnp.int32, (256, 128), 0) + 256 * m).astype(F32)
        ids = []
        for k in range(READS // 128):
            vid = vids[k // 2 : k // 2 + 1, (k % 2) * 128 : (k % 2) * 128 + 128]
            ids.append((wanted == vid).astype(F32).astype(BF16))
        sums = nn(jnp.concatenate(ids, axis=1), gkb[...].reshape(READS, D)).astype(BF16)
        vpart[pl.ds(8 * m, 8)] = sums.reshape(8, OWN, D)
        for i in range(8):
            to = 8 * m + ((tm + i) & 7)

            @pl.when(to != tm)
            def _(to=to):
                pltpu.make_async_remote_copy(
                    src_ref=vpart.at[to], dst_ref=vbuf.at[(to - tm + 15) & 15],
                    send_sem=v_send, recv_sem=v_recv,
                    device_id=(to, node), device_id_type=MESH,
                ).start()

    lax.fori_loop(0, EV // 32, spread, 0)
    for g in range(3):
        part_copy(g).wait()
    chain_steps(0)
    lax.fori_loop(EV // 32, EV // 16, spread, 0)
    version_sums(0)
    part_copy(3).wait()
    chain_steps(1)
    version_sums(1)
    chain_steps(2)

    gdst = (nt(gin[:, 0:1024], wide(wb, 1536, 1024)) + nt(gcand[...], wide(wb, 2560, 512))) + gmem[...]
    hot = (lax.broadcasted_iota(jnp.int32, (OWN, EV), 0) == dst_loc[...]).astype(F32).astype(BF16)
    dpart[...] = mine(0) + nn(hot, gdst.astype(BF16))
    chain_steps(3)

    ends = [(way, len(chains[way][0]) - 1) for way in range(4)]
    for way, s in ends:
        hop(way, s).wait_recv()
    node_out[...] = dpart[...] + (
        (nrecv[0, 3].astype(F32) + nrecv[1, 2].astype(F32)) + (nrecv[2, 3].astype(F32) + nrecv[3, 3].astype(F32))
    )
    pltpu.make_async_copy(vbuf, vbuf, v_recv).wait()
    total = vpart[tm].astype(F32)
    for k in range(15):
        total = total + vbuf[k].astype(F32)
    ver_out[...] = total

    for way in range(4):
        for s in range(len(chains[way][0])):
            hop(way, s).wait_send()
    pltpu.make_async_copy(vbuf, vbuf, v_send).wait()
    for ph, (buf, _) in enumerate(bufs):
        ref = buf.at[:, :, :, c]
        pltpu.make_async_copy(ref, ref, sib_send.at[ph]).wait()
        ref = buf.at[0:3, :, 0, c]
        pltpu.make_async_copy(ref, ref, r1_send.at[ph]).wait()
        ref = buf.at[0:3, :, :, c]
        pltpu.make_async_copy(ref, ref, r2_send.at[ph]).wait()

    @pl.when(zy == kind)
    def _():
        ref = wb.at[0:3, :, 0, 0, :, 0:640]
        pltpu.make_async_copy(ref, ref, s1_send.at[0]).wait()
        ref = wb.at[0:3, 0:3, 0, :, :, 0:640]
        pltpu.make_async_copy(ref, ref, s1_send.at[1]).wait()


def hand_out(ver_in, node_in, ver_out, node_out):
    ver_out[...] = ver_in[...]
    node_out[...] = node_in[...]


def body(
    message, dest_mem, nbr_rows, emb_grad, event_time, nbr_time, nbr_count, source_id, dest_local,
    read_owner, read_row, w_in, w_hid, w_query, w_keyval, w_out,
):
    vmem = pl.BlockSpec(memory_space=pltpu.VMEM)
    hbm = pl.BlockSpec(memory_space=pl.ANY)
    dma = pltpu.SemaphoreType.DMA
    scratch = [
        pltpu.VMEM((EV, D), BF16),
        pltpu.VMEM((EV, D), BF16),
        pltpu.VMEM((READS, D), BF16),
        pltpu.VMEM((EV, D), BF16),
        pltpu.VMEM((1, EV), jnp.int32),
        pltpu.VMEM((SLOTS, EV), jnp.int32),
        pltpu.VMEM((1, EV), jnp.int32),
        pltpu.VMEM((1, EV), jnp.int32),
        pltpu.VMEM((1, EV), jnp.int32),
        pltpu.VMEM((1, READS), jnp.int32),
        pltpu.VMEM((READS // 128, 128), jnp.int32),
        pltpu.VMEM((4, 4, 4, 2, 16, CA), BF16),
        pltpu.VMEM((4, 4, 4, 2, 16, CB), BF16),
        pltpu.VMEM((4, READS, 128), F32),
        pltpu.VMEM((SLOTS, EV, D), F32),
        pltpu.VMEM((SLOTS, EV, D), BF16),
        pltpu.VMEM((2, EV, D), F32),
        pltpu.VMEM((2, EV, D), F32),
        pltpu.VMEM((2, EV, D), BF16),
        pltpu.VMEM((4, EV, D), F32),
        pltpu.VMEM((EV, D), BF16),
        pltpu.VMEM((EV, D), F32),
        pltpu.VMEM((EV, 3 * D), BF16),
        pltpu.VMEM((EV, D), BF16),
        pltpu.VMEM((EV, D), BF16),
        pltpu.VMEM((EV, 8), F32),
        pltpu.VMEM((8, EV), F32),
        pltpu.VMEM((EV, 128), F32),
        pltpu.VMEM((EV, 128), F32),
        pltpu.VMEM((EV, 128), F32),
        pltpu.VMEM((16, OWN, D), BF16),
        pltpu.VMEM((15, OWN, D), BF16),
        pltpu.VMEM((4, 2, 4, OWN, D), BF16),
        pltpu.VMEM((4, 4, OWN, D), BF16),
        pltpu.VMEM((4, 4, OWN, D), BF16),
        pltpu.VMEM((4, 4, OWN, D), BF16),
        pltpu.VMEM((OWN, D), F32),
        pltpu.VMEM((READS, 128), F32),
        pltpu.VMEM((8, EV), F32),
        pltpu.VMEM((16, 128), F32),
        dma((11,)),
        dma((2,)),
        dma((2,)),
        dma((2, 4)),
        dma((2,)),
        dma((2,)),
        dma((2, 16, 2)),
        dma((2,)),
        dma((2,)),
        dma,
        dma,
        dma((4,)),
        dma((4,)),
        dma((4, 4)),
        dma((4, 4)),
    ]
    version_grad, node_grad = pl.pallas_call(
        kernel,
        out_shape=(jax.ShapeDtypeStruct((OWN, D), F32), jax.ShapeDtypeStruct((OWN, D), F32)),
        in_specs=[hbm] * 16,
        out_specs=(vmem, vmem),
        scratch_shapes=scratch,
        compiler_params=pltpu.CompilerParams(
            collective_id=0, has_side_effects=True, vmem_limit_bytes=56 * 1024 * 1024
        ),
        cost_estimate=pl.CostEstimate(
            flops=4_000_000_000, bytes_accessed=8_000_000, transcendentals=1_000_000
        ),
    )(
        message, dest_mem, nbr_rows, emb_grad,
        event_time.reshape(1, EV), nbr_time.T, nbr_count.reshape(1, EV),
        source_id.reshape(1, EV), dest_local.reshape(1, EV),
        read_owner.reshape(1, READS), read_row.reshape(READS // 128, 128),
        w_in, w_hid, w_query, w_keyval, w_out,
    )
    version_grad, node_grad = pl.pallas_call(
        hand_out,
        out_shape=(jax.ShapeDtypeStruct((OWN, D), F32), jax.ShapeDtypeStruct((OWN, D), F32)),
        in_specs=[vmem] * 2,
        out_specs=(vmem, vmem),
        compiler_params=pltpu.CompilerParams(vmem_limit_bytes=60 * 1024 * 1024),
    )(version_grad, node_grad)
    return version_grad, node_grad[None]


def solution(mesh):
    both = P(("tm", "node"))
    in_specs = (
        (P(("tm", "node"), None),) * 4
        + (both, P(("tm", "node"), None), both, both, both, P(("tm", "node"), None), both)
        + (P("node", None),) * 5
    )
    out_specs = (P(("tm", "node"), None), P("tm", "node", None))
    return jax.shard_map(body, mesh=mesh, in_specs=in_specs, out_specs=out_specs, check_vma=False)
```

```python
import math

import jax
import jax.numpy as jnp
from jax import lax
from jax.experimental import pallas as pl
from jax.experimental.pallas import tpu as pltpu
from jax.sharding import PartitionSpec as P

D = 512
HEAD = 256
SLOTS = 6
EV = 256
READS = EV * SLOTS
OWN = 32
CA = 512
CB = 768
F32 = jnp.float32
BF16 = jnp.bfloat16
MESH = pl.DeviceIdType.MESH
FAR = ((5, 6, 7, 8), (9, 10, 11, 12), (1, 2, 3, 4), (13, 14, 15, 0))


def nn(a, b):
    return lax.dot_general(a, b, (((1,), (0,)), ((), ())), preferred_element_type=F32)


def nt(a, b):
    return lax.dot_general(a, b, (((1,), (1,)), ((), ())), preferred_element_type=F32)


def sigmoid(v):
    return 0.5 * jnp.tanh(0.5 * v) + 0.5


def cos_wide(angle):
    half = 0.5 * angle
    turns = jnp.floor(half * (1.0 / math.pi) + 0.5)
    s = (half - turns * 3.140625) - turns * (math.pi - 3.140625)
    q = s * s
    p = q * (-1.0 / 39916800.0) + (1.0 / 362880.0)
    p = p * q + (-1.0 / 5040.0)
    p = p * q + (1.0 / 120.0)
    p = p * q + (-1.0 / 6.0)
    p = p * q + 1.0
    sine = p * s
    return 1.0 - 2.0 * (sine * sine)


def cos_small(angle):
    q = angle * angle
    return 1.0 + q * (q * (1.0 / 24.0) - 0.5)


def kernel(
    msg_in, dst_in, nbr_in, emb_in, ev_in, nbt_in, cnt_in, src_in, dloc_in, own_in, vrow_in,
    w_in, w_hid, w_q, w_kv, w_out,
    ver_out, node_out,
    msg, dst, nbr, emb, ev_time, nb_time, nb_count, src_id, dst_loc, owner, vrow,
    wa, wb, rbuf, keys, gkb, qk, gv, ctx, gates, mem, gmem, gin, gcand, gmsg, tcol, tpack, gwp, scp, wtp,
    vpart, vbuf, npart, nsib, nsend, nrecv, dpart,
    vcol, vids, idp,
    in_sem, loc_sem, s1_send, s1_recv, r1_send, r2_send, piece_sem, sib_send, sib_recv,
    v_send, v_recv, nd_send, nd_recv, ring_send, ring_recv,
):
    tm = lax.axis_index("tm")
    node = lax.axis_index("node")
    x, y = tm >> 2, tm & 3
    z, c = node >> 1, node & 1
    other = 1 - c
    sibling = (tm, z * 2 + other)
    zq, zy = z >> 2, z & 3

    def pick(p, q):
        return jnp.where(c == 0, p, q)

    a, b = pick(x, y), pick(y, x)

    def tm_of(aa, bb):
        return pick(aa * 4 + bb, bb * 4 + aa)

    a_left, a_right, a_far = (a + 3) & 3, (a + 1) & 3, (a + 2) & 3
    b_left, b_right, b_far = (b + 3) & 3, (b + 1) & 3, (b + 2) & 3
    dev_a_left, dev_a_right = (tm_of(a_left, b), node), (tm_of(a_right, b), node)
    dev_b_left, dev_b_right = (tm_of(a, b_left), node), (tm_of(a, b_right), node)

    bufs = ((wa, CA), (wb, CB))

    kind = (y + 2 * c) & 3

    def share(ph, q):
        buf, _ = bufs[ph]
        return buf.at[x, q, kind, c]

    inputs = (
        (nbr_in, nbr), (ev_in, ev_time), (nbt_in, nb_time), (cnt_in, nb_count), (own_in, owner), (vrow_in, vrow),
        (msg_in, msg), (dst_in, dst), (emb_in, emb), (src_in, src_id), (dloc_in, dst_loc),
    )

    def copy_in(i):
        return pltpu.make_async_copy(inputs[i][0], inputs[i][1], in_sem.at[i])

    blocks = (((w_kv, 0), (w_in, 0)), ((w_kv, CA), (w_in, CB)), ((w_out, 0), (w_hid, 0)), ((w_q, 0), (w_hid, CB)))
    for k, pair in enumerate(blocks):
        @pl.when(jnp.logical_and(zy == kind, x == k))
        def _(pair=pair):
            for ph, (ref, at) in enumerate(pair):
                pltpu.make_async_copy(
                    ref.at[:, pl.ds(at, bufs[ph][1])], share(ph, zq), loc_sem.at[ph]
                ).start()

    barrier = pltpu.get_barrier_semaphore()

    def greet(k, carry):
        pl.semaphore_signal(barrier, inc=1, device_id=(tm, (node + 2 * k) & 31), device_id_type=MESH)
        pl.semaphore_signal(barrier, inc=1, device_id=((tm + k) & 15, node), device_id_type=MESH)
        return carry

    lax.fori_loop(1, 16, greet, 0)
    pl.semaphore_signal(barrier, inc=1, device_id=sibling, device_id_type=MESH)

    for i in range(11):
        copy_in(i).start()
    pl.semaphore_wait(barrier, 31)

    @pl.when(zy == kind)
    def _():
        for ph in range(2):
            def send(i, carry, ph=ph):
                k = jnp.where((i & 1) == 0, 8 - (i >> 1), 8 + ((i + 1) >> 1))
                pltpu.make_async_remote_copy(
                    src_ref=share(ph, zq), dst_ref=share(ph, zq),
                    send_sem=s1_send.at[ph], recv_sem=s1_recv.at[ph, zq],
                    device_id=(tm, ((z + k) & 15) * 2 + c), device_id_type=MESH,
                ).start()
                return carry
            pltpu.make_async_copy(share(ph, zq), share(ph, zq), loc_sem.at[ph]).wait()
            lax.fori_loop(0, 15, send, 0)

    def stage1_wait(ph):
        for q in range(4):
            @pl.when(4 * q + kind != z)
            def _(q=q):
                pltpu.make_async_copy(share(ph, q), share(ph, q), s1_recv.at[ph, q]).wait()

    def piece(ph, aa, bb, part=None):
        buf, _ = bufs[ph]
        xx, yy = pick(aa, bb), pick(bb, (aa + 2) & 3)
        rows = pl.ds(0, 4) if part is None else pl.ds(2 * part, 2)
        return buf.at[xx, rows, yy, c]

    def send_piece(ph, aa, bb, device, send_sem, part=None, slot=0):
        ref = piece(ph, aa, bb, part)
        pltpu.make_async_remote_copy(
            src_ref=ref, dst_ref=ref, send_sem=send_sem.at[ph],
            recv_sem=piece_sem.at[ph, aa * 4 + bb, slot],
            device_id=device, device_id_type=MESH,
        ).start()

    def wait_piece(ph, aa, bb, part=None, slot=0):
        ref = piece(ph, aa, bb, part)
        pltpu.make_async_copy(ref, ref, piece_sem.at[ph, aa * 4 + bb, slot]).wait()

    def to_sibling(ph, bb):
        buf, _ = bufs[ph]

        def send(ref):
            pltpu.make_async_remote_copy(
                src_ref=ref, dst_ref=ref, send_sem=sib_send.at[ph], recv_sem=sib_recv.at[ph],
                device_id=sibling, device_id_type=MESH,
            ).start()

        @pl.when(c == 0)
        def _():
            send(buf.at[:, :, bb, 0])

        @pl.when(c == 1)
        def _():
            send(buf.at[bb, :, :, 1])

    def second_ring(ph, aa):
        send_piece(ph, aa, b, dev_b_left, r2_send)
        send_piece(ph, aa, b, dev_b_right, r2_send)

    def step0(ph):
        stage1_wait(ph)
        send_piece(ph, a, b, dev_a_left, r1_send)
        send_piece(ph, a, b, dev_a_right, r1_send)
        second_ring(ph, a)

    def step1(ph):
        wait_piece(ph, a_left, b)
        send_piece(ph, a_left, b, dev_a_right, r1_send, 0, 0)
        second_ring(ph, a_left)
        wait_piece(ph, a_right, b)
        send_piece(ph, a_right, b, dev_a_left, r1_send, 1, 1)
        second_ring(ph, a_right)

    def step2(ph):
        wait_piece(ph, a_far, b, 0, 0)
        wait_piece(ph, a_far, b, 1, 1)
        second_ring(ph, a_far)
        to_sibling(ph, b)

    def step3(ph):
        for aa in (a, a_left, a_right, a_far):
            wait_piece(ph, aa, b_left)
            send_piece(ph, aa, b_left, dev_b_right, r2_send, 0, 0)
            wait_piece(ph, aa, b_right)
            send_piece(ph, aa, b_right, dev_b_left, r2_send, 1, 1)
        to_sibling(ph, b_left)
        to_sibling(ph, b_right)

    def step4(ph):
        for aa in (a, a_left, a_right, a_far):
            wait_piece(ph, aa, b_far, 0, 0)
            wait_piece(ph, aa, b_far, 1, 1)
        to_sibling(ph, b_far)

    def all_here(ph):
        ref = bufs[ph][0].at[:, :, :, other]
        pltpu.make_async_copy(ref, ref, sib_recv.at[ph]).wait()

    def widen(i, carry):
        at = pl.ds(pl.multiple_of(i * 64, 64), 64)
        for t in range(4):
            rbuf[t, at, :] = nbr[at, t * 128 : (t + 1) * 128].astype(F32)
        return carry

    for i in range(6):
        copy_in(i).wait()
    lax.fori_loop(0, READS // 64, widen, 0)
    tpack[0:6, :] = (ev_time[...] - nb_time[...]).astype(F32)
    tpack[6:7, :] = nb_count[...].astype(F32)
    tpack[7:8, :] = jnp.zeros((1, EV), F32)
    tcol[...] = jnp.transpose(tpack[...])
    lanes = lax.broadcasted_iota(jnp.int32, (1, D), 1).astype(F32)
    freq = jnp.exp(lanes * (-9.0 * math.log(10.0) / D))

    def make_keys(i, carry):
        at = pl.ds(pl.multiple_of(i * 16, 16), 16)
        gaps = tcol[at, :]
        for j in range(SLOTS):
            gap = gaps[:, j : j + 1]
            for t, cosine in enumerate((cos_wide, cos_wide, cos_small, cos_small)):
                cut = slice(t * 128, (t + 1) * 128)
                rows = rbuf[t, pl.ds(i * (16 * SLOTS) + j, 16, stride=SLOTS), :]
                keys[j, at, cut] = rows + cosine(gap * freq[:, cut])
        return carry

    lax.fori_loop(0, EV // 16, make_keys, 0)

    for k in range(READS // 128):
        idp[k : k + 1, :] = (owner[:, k * 128 : (k + 1) * 128] * OWN + vrow[k : k + 1, :]).astype(F32)
    idp[12:16, :] = jnp.zeros((4, 128), F32)
    columns = jnp.transpose(idp[...])
    for k in range(READS // 128):
        vcol[k * 128 : (k + 1) * 128, :] = jnp.broadcast_to(columns[:, k : k + 1], (128, 128))
    for j in range(SLOTS):
        vids[j : j + 1, :] = jnp.transpose(vcol[pl.ds(j, EV, stride=SLOTS), :])[0:1, :]
    for i in range(6, 11):
        copy_in(i).wait()

    step0(1)
    step1(1)
    step0(0)
    step2(1)
    step3(1)
    step1(0)
    step2(0)
    step4(1)
    step3(0)

    def wide(ref, start, width):
        size = ref.shape[-1]
        out = []
        while width:
            block, at = divmod(start, size)
            take = min(width, size - at)
            out.append(ref[block, :, :, :, :, at : at + take].reshape(D, take))
            start, width = start + take, width - take
        return out[0] if len(out) == 1 else jnp.concatenate(out, axis=1)

    all_here(1)

    def gate(k):
        return (nn(msg[...], wide(wb, k * D, D)), nn(dst[...], wide(wb, 1536 + k * D, D)))

    gi, gh = gate(0)
    gates[0] = sigmoid(gi + gh)
    gi, gh = gate(2)
    gates[3] = gh
    gates[2] = jnp.tanh(gi + gates[0] * gh)
    step4(0)
    gi, gh = gate(1)
    update = sigmoid(gi + gh)
    gates[1] = update
    mem[...] = ((1.0 - update) * gates[2] + update * dst[...].astype(F32)).astype(BF16)

    all_here(0)

    gatt = nt(emb[...], wide(wa, 1024, 512)).astype(BF16)
    for h in range(2):
        gv[h] = nt(gatt[:, h * HEAD : (h + 1) * HEAD], wide(wa, 512 + h * HEAD, HEAD))

    lane16 = lax.broadcasted_iota(jnp.int32, (16, 128), 1)

    def row_dots(vec, out):
        def block(i, carry):
            at = pl.ds(pl.multiple_of(i * 16, 16), 16)
            acc = jnp.zeros((16, 128), F32)
            v0, v1 = vec[0, at, :], vec[1, at, :]
            for j in range(SLOTS):
                key = keys[j, at, :]
                for h, v in enumerate((v0, v1)):
                    prod = key * v
                    part = (prod[:, 0:128] + prod[:, 128:256]) + (prod[:, 256:384] + prod[:, 384:512])
                    acc = jnp.where(lane16 == h * SLOTS + j, jnp.sum(part, axis=1, keepdims=True), acc)
            out[at, :] = acc
            return carry
        lax.fori_loop(0, EV // 16, block, 0)

    row_dots(gv, gwp)

    quer = nn(mem[...], wide(wa, 1536, 512)).astype(BF16)
    for h in range(2):
        qk[h] = nt(quer[:, h * HEAD : (h + 1) * HEAD], wide(wa, h * HEAD, HEAD))

    row_dots(qk, scp)

    lane = lax.broadcasted_iota(jnp.int32, (EV, 128), 1)
    slot = jnp.where(lane >= SLOTS, lane - SLOTS, lane).astype(F32)
    head0, head1 = lane < SLOTS, jnp.logical_and(lane >= SLOTS, lane < 2 * SLOTS)
    live = jnp.logical_and(lane < 2 * SLOTS, slot < tcol[:, 6:7])
    raw = jnp.where(live, jnp.exp(scp[...] * (1.0 / 16.0)), 0.0)

    def per_head(v):
        s0 = jnp.sum(jnp.where(head0, v, 0.0), axis=1, keepdims=True)
        s1 = jnp.sum(jnp.where(head1, v, 0.0), axis=1, keepdims=True)
        return jnp.where(head0, s0, s1)

    weight = raw / per_head(raw)
    gw = gwp[...]
    wtp[...] = weight
    scp[...] = weight * (gw - per_head(weight * gw)) * (1.0 / 16.0)

    def gather_slots(i, carry):
        at = pl.ds(pl.multiple_of(i * 16, 16), 16)
        sc = scp[at, :]
        c0 = jnp.zeros((16, D), F32)
        c1 = jnp.zeros((16, D), F32)
        for j in range(SLOTS):
            key = keys[j, at, :]
            c0 = c0 + sc[:, j : j + 1] * key
            c1 = c1 + sc[:, SLOTS + j : SLOTS + j + 1] * key
        ctx[0, at, :] = c0.astype(BF16)
        ctx[1, at, :] = c1.astype(BF16)
        return carry

    lax.fori_loop(0, EV // 16, gather_slots, 0)
    gq = [nn(ctx[h], wide(wa, h * HEAD, HEAD)).astype(BF16) for h in range(2)]
    gmem[...] = emb[...].astype(F32) + (
        nt(gq[0], wide(wa, 1536, HEAD)) + nt(gq[1], wide(wa, 1536 + HEAD, HEAD))
    )

    def gru(i, carry):
        at = pl.ds(pl.multiple_of(i * 16, 16), 16)
        gm = gmem[at, :]
        r, u, cand, hc = gates[0, at, :], gates[1, at, :], gates[2, at, :], gates[3, at, :]
        gu = gm * (dst[at, :].astype(F32) - cand)
        gc = gm * (1.0 - u) * (1.0 - cand * cand)
        gin[at, 0:512] = (gc * hc * (r * (1.0 - r))).astype(BF16)
        gin[at, 512:1024] = (gu * (u * (1.0 - u))).astype(BF16)
        gin[at, 1024:1536] = gc.astype(BF16)
        gcand[at, :] = (gc * r).astype(BF16)
        gmem[at, :] = gm * u
        return carry

    lax.fori_loop(0, EV // 16, gru, 0)

    gmsg[...] = nt(gin[...], wide(wb, 0, 1536)).astype(BF16)

    def part_copy(g):
        return pltpu.make_async_remote_copy(
            src_ref=npart.at[g, other], dst_ref=nsib.at[g], send_sem=nd_send.at[g], recv_sem=nd_recv.at[g],
            device_id=sibling, device_id_type=MESH,
        )

    for g, offsets in enumerate(FAR):
        base = ((z + offsets[0]) & 15) * 64
        wanted = (lax.broadcasted_iota(jnp.int32, (256, EV), 0) + base) & 1023
        hot = (wanted == src_id[...]).astype(F32).astype(BF16)
        sums = nn(hot, gmsg[...]).astype(BF16).reshape(4, 2, OWN, D)
        npart[g, 0] = sums[:, 0]
        npart[g, 1] = sums[:, 1]
        part_copy(g).start()

    def mine(rel):
        for g, offsets in enumerate(FAR):
            if rel in offsets:
                k = offsets.index(rel)
                return npart[g, c, k].astype(F32) + nsib[g, k].astype(F32)

    chains = (((8, 9, 10, 11), -1, -5), ((7, 6, 5), 1, 5), ((12, 13, 14, 15), -1, -1), ((4, 3, 2, 1), 1, 1))

    def hop(way, s):
        steps, near, last = chains[way]
        to = (z + (last if s == len(steps) - 1 else near) + 16) & 15
        return pltpu.make_async_remote_copy(
            src_ref=nsend.at[way, s], dst_ref=nrecv.at[way, s],
            send_sem=ring_send.at[way, s], recv_sem=ring_recv.at[way, s],
            device_id=(tm, to * 2 + c), device_id_type=MESH,
        )

    def chain_step(way, s):
        total = mine(chains[way][0][s])
        if s > 0:
            hop(way, s - 1).wait_recv()
            total = total + nrecv[way, s - 1].astype(F32)
        nsend[way, s] = total.astype(BF16)
        hop(way, s).start()

    def chain_steps(s):
        for way in range(4):
            if s < len(chains[way][0]):
                chain_step(way, s)

    def spread(i, carry):
        at = pl.ds(pl.multiple_of(i * 16, 16), 16)
        sc, wt = scp[at, :], wtp[at, :]
        for j in range(SLOTS):
            s0, s1 = sc[:, j : j + 1], sc[:, SLOTS + j : SLOTS + j + 1]
            w0, w1 = wt[:, j : j + 1], wt[:, SLOTS + j : SLOTS + j + 1]
            gkb[j, at, :] = (
                (s0 * qk[0, at, :] + s1 * qk[1, at, :]) + (w0 * gv[0, at, :] + w1 * gv[1, at, :])
            ).astype(BF16)
        return carry

    def version_sums(m):
        wanted = (lax.broadcasted_iota(jnp.int32, (256, 128), 0) + 256 * m).astype(F32)
        ids = []
        for k in range(READS // 128):
            vid = vids[k // 2 : k // 2 + 1, (k % 2) * 128 : (k % 2) * 128 + 128]
            ids.append((wanted == vid).astype(F32).astype(BF16))
        sums = nn(jnp.concatenate(ids, axis=1), gkb[...].reshape(READS, D)).astype(BF16)
        vpart[pl.ds(8 * m, 8)] = sums.reshape(8, OWN, D)
        for i in range(8):
            to = 8 * m + ((tm + i) & 7)

            @pl.when(to != tm)
            def _(to=to):
                pltpu.make_async_remote_copy(
                    src_ref=vpart.at[to], dst_ref=vbuf.at[(to - tm + 15) & 15],
                    send_sem=v_send, recv_sem=v_recv,
                    device_id=(to, node), device_id_type=MESH,
                ).start()

    lax.fori_loop(0, EV // 32, spread, 0)
    for g in range(3):
        part_copy(g).wait()
    chain_steps(0)
    lax.fori_loop(EV // 32, EV // 16, spread, 0)
    version_sums(0)
    part_copy(3).wait()
    chain_steps(1)
    version_sums(1)
    chain_steps(2)

    gdst = (nt(gin[:, 0:1024], wide(wb, 1536, 1024)) + nt(gcand[...], wide(wb, 2560, 512))) + gmem[...]
    hot = (lax.broadcasted_iota(jnp.int32, (OWN, EV), 0) == dst_loc[...]).astype(F32).astype(BF16)
    dpart[...] = mine(0) + nn(hot, gdst.astype(BF16))
    chain_steps(3)

    ends = [(way, len(chains[way][0]) - 1) for way in range(4)]
    for way, s in ends:
        hop(way, s).wait_recv()
    node_out[...] = dpart[...] + (
        (nrecv[0, 3].astype(F32) + nrecv[1, 2].astype(F32)) + (nrecv[2, 3].astype(F32) + nrecv[3, 3].astype(F32))
    )
    pltpu.make_async_copy(vbuf, vbuf, v_recv).wait()
    total = vpart[tm].astype(F32)
    for k in range(15):
        total = total + vbuf[k].astype(F32)
    ver_out[...] = total

    for way in range(4):
        for s in range(len(chains[way][0])):
            hop(way, s).wait_send()
    pltpu.make_async_copy(vbuf, vbuf, v_send).wait()
    for ph, (buf, _) in enumerate(bufs):
        ref = buf.at[:, :, :, c]
        pltpu.make_async_copy(ref, ref, sib_send.at[ph]).wait()
        ref = buf.at[0:3, :, 0, c]
        pltpu.make_async_copy(ref, ref, r1_send.at[ph]).wait()
        ref = buf.at[0:3, :, :, c]
        pltpu.make_async_copy(ref, ref, r2_send.at[ph]).wait()

    @pl.when(zy == kind)
    def _():
        ref = wb.at[0:3, :, 0, 0, :, 0:640]
        pltpu.make_async_copy(ref, ref, s1_send.at[0]).wait()
        ref = wb.at[0:3, 0:3, 0, :, :, 0:640]
        pltpu.make_async_copy(ref, ref, s1_send.at[1]).wait()


def hand_out(ver_in, node_in, ver_out, node_out):
    ver_out[...] = ver_in[...]
    node_out[...] = node_in[...]


def body(
    message, dest_mem, nbr_rows, emb_grad, event_time, nbr_time, nbr_count, source_id, dest_local,
    read_owner, read_row, w_in, w_hid, w_query, w_keyval, w_out,
):
    vmem = pl.BlockSpec(memory_space=pltpu.VMEM)
    hbm = pl.BlockSpec(memory_space=pl.ANY)
    dma = pltpu.SemaphoreType.DMA
    scratch = [
        pltpu.VMEM((EV, D), BF16),
        pltpu.VMEM((EV, D), BF16),
        pltpu.VMEM((READS, D), BF16),
        pltpu.VMEM((EV, D), BF16),
        pltpu.VMEM((1, EV), jnp.int32),
        pltpu.VMEM((SLOTS, EV), jnp.int32),
        pltpu.VMEM((1, EV), jnp.int32),
        pltpu.VMEM((1, EV), jnp.int32),
        pltpu.VMEM((1, EV), jnp.int32),
        pltpu.VMEM((1, READS), jnp.int32),
        pltpu.VMEM((READS // 128, 128), jnp.int32),
        pltpu.VMEM((4, 4, 4, 2, 16, CA), BF16),
        pltpu.VMEM((4, 4, 4, 2, 16, CB), BF16),
        pltpu.VMEM((4, READS, 128), F32),
        pltpu.VMEM((SLOTS, EV, D), F32),
        pltpu.VMEM((SLOTS, EV, D), BF16),
        pltpu.VMEM((2, EV, D), F32),
        pltpu.VMEM((2, EV, D), F32),
        pltpu.VMEM((2, EV, D), BF16),
        pltpu.VMEM((4, EV, D), F32),
        pltpu.VMEM((EV, D), BF16),
        pltpu.VMEM((EV, D), F32),
        pltpu.VMEM((EV, 3 * D), BF16),
        pltpu.VMEM((EV, D), BF16),
        pltpu.VMEM((EV, D), BF16),
        pltpu.VMEM((EV, 8), F32),
        pltpu.VMEM((8, EV), F32),
        pltpu.VMEM((EV, 128), F32),
        pltpu.VMEM((EV, 128), F32),
        pltpu.VMEM((EV, 128), F32),
        pltpu.VMEM((16, OWN, D), BF16),
        pltpu.VMEM((15, OWN, D), BF16),
        pltpu.VMEM((4, 2, 4, OWN, D), BF16),
        pltpu.VMEM((4, 4, OWN, D), BF16),
        pltpu.VMEM((4, 4, OWN, D), BF16),
        pltpu.VMEM((4, 4, OWN, D), BF16),
        pltpu.VMEM((OWN, D), F32),
        pltpu.VMEM((READS, 128), F32),
        pltpu.VMEM((8, EV), F32),
        pltpu.VMEM((16, 128), F32),
        dma((11,)),
        dma((2,)),
        dma((2,)),
        dma((2, 4)),
        dma((2,)),
        dma((2,)),
        dma((2, 16, 2)),
        dma((2,)),
        dma((2,)),
        dma,
        dma,
        dma((4,)),
        dma((4,)),
        dma((4, 4)),
        dma((4, 4)),
    ]
    version_grad, node_grad = pl.pallas_call(
        kernel,
        out_shape=(jax.ShapeDtypeStruct((OWN, D), F32), jax.ShapeDtypeStruct((OWN, D), F32)),
        in_specs=[hbm] * 16,
        out_specs=(vmem, vmem),
        scratch_shapes=scratch,
        compiler_params=pltpu.CompilerParams(
            collective_id=0, has_side_effects=True, vmem_limit_bytes=56 * 1024 * 1024
        ),
        cost_estimate=pl.CostEstimate(
            flops=4_000_000_000, bytes_accessed=8_000_000, transcendentals=1_000_000
        ),
    )(
        message, dest_mem, nbr_rows, emb_grad,
        event_time.reshape(1, EV), nbr_time.T, nbr_count.reshape(1, EV),
        source_id.reshape(1, EV), dest_local.reshape(1, EV),
        read_owner.reshape(1, READS), read_row.reshape(READS // 128, 128),
        w_in, w_hid, w_query, w_keyval, w_out,
    )
    version_grad, node_grad = pl.pallas_call(
        hand_out,
        out_shape=(jax.ShapeDtypeStruct((OWN, D), F32), jax.ShapeDtypeStruct((OWN, D), F32)),
        in_specs=[vmem] * 2,
        out_specs=(vmem, vmem),
        compiler_params=pltpu.CompilerParams(vmem_limit_bytes=60 * 1024 * 1024),
    )(version_grad, node_grad)
    return version_grad, node_grad[None]


def solution(mesh):
    both = P(("tm", "node"))
    in_specs = (
        (P(("tm", "node"), None),) * 4
        + (both, P(("tm", "node"), None), both, both, both, P(("tm", "node"), None), both)
        + (P("node", None),) * 5
    )
    out_specs = (P(("tm", "node"), None), P("tm", "node", None))
    return jax.shard_map(body, mesh=mesh, in_specs=in_specs, out_specs=out_specs, check_vma=False)
```

```python
import math

import jax
import jax.numpy as jnp
from jax import lax
from jax.experimental import pallas as pl
from jax.experimental.pallas import tpu as pltpu
from jax.sharding import PartitionSpec as P

D = 512
HEAD = 256
SLOTS = 6
EV = 256
READS = EV * SLOTS
OWN = 32
CA = 512
CB = 768
F32 = jnp.float32
BF16 = jnp.bfloat16
MESH = pl.DeviceIdType.MESH
FAR = ((5, 6, 7, 8), (9, 10, 11, 12), (1, 2, 3, 4), (13, 14, 15, 0))


def nn(a, b):
    return lax.dot_general(a, b, (((1,), (0,)), ((), ())), preferred_element_type=F32)


def nt(a, b):
    return lax.dot_general(a, b, (((1,), (1,)), ((), ())), preferred_element_type=F32)


def sigmoid(v):
    return 0.5 * jnp.tanh(0.5 * v) + 0.5


def cos_wide(angle):
    half = 0.5 * angle
    turns = jnp.floor(half * (1.0 / math.pi) + 0.5)
    s = (half - turns * 3.140625) - turns * (math.pi - 3.140625)
    q = s * s
    p = q * (-1.0 / 39916800.0) + (1.0 / 362880.0)
    p = p * q + (-1.0 / 5040.0)
    p = p * q + (1.0 / 120.0)
    p = p * q + (-1.0 / 6.0)
    p = p * q + 1.0
    sine = p * s
    return 1.0 - 2.0 * (sine * sine)


def cos_small(angle):
    q = angle * angle
    return 1.0 + q * (q * (1.0 / 24.0) - 0.5)


def kernel(
    msg_in, dst_in, nbr_in, emb_in, ev_in, nbt_in, cnt_in, src_in, dloc_in, own_in, vrow_in,
    w_in, w_hid, w_q, w_kv, w_out,
    ver_out, node_out,
    msg, dst, nbr, emb, ev_time, nb_time, nb_count, src_id, dst_loc, owner, vrow,
    wa, wb, rbuf, keys, gkb, qk, gv, ctx, gates, mem, gmem, gin, gcand, gmsg, tcol, tpack, gwp, scp, wtp,
    vpart, vbuf, npart, nsib, nsend, nrecv, dpart,
    vcol, vids, idp,
    in_sem, loc_sem, s1_send, s1_recv, r1_send, r2_send, piece_sem, sib_send, sib_recv,
    v_send, v_recv, nd_send, nd_recv, ring_send, ring_recv,
):
    tm = lax.axis_index("tm")
    node = lax.axis_index("node")
    x, y = tm >> 2, tm & 3
    z, c = node >> 1, node & 1
    other = 1 - c
    sibling = (tm, z * 2 + other)
    zq, zy = z >> 2, z & 3

    def pick(p, q):
        return jnp.where(c == 0, p, q)

    a, b = pick(x, y), pick(y, x)

    def tm_of(aa, bb):
        return pick(aa * 4 + bb, bb * 4 + aa)

    a_left, a_right, a_far = (a + 3) & 3, (a + 1) & 3, (a + 2) & 3
    b_left, b_right, b_far = (b + 3) & 3, (b + 1) & 3, (b + 2) & 3
    dev_a_left, dev_a_right = (tm_of(a_left, b), node), (tm_of(a_right, b), node)
    dev_b_left, dev_b_right = (tm_of(a, b_left), node), (tm_of(a, b_right), node)

    bufs = ((wa, CA), (wb, CB))

    kind = (y + 2 * c) & 3

    def share(ph, q):
        buf, _ = bufs[ph]
        return buf.at[x, q, kind, c]

    inputs = (
        (nbr_in, nbr), (ev_in, ev_time), (nbt_in, nb_time), (cnt_in, nb_count), (own_in, owner), (vrow_in, vrow),
        (msg_in, msg), (dst_in, dst), (emb_in, emb), (src_in, src_id), (dloc_in, dst_loc),
    )

    def copy_in(i):
        return pltpu.make_async_copy(inputs[i][0], inputs[i][1], in_sem.at[i])

    blocks = (((w_kv, 0), (w_in, 0)), ((w_kv, CA), (w_in, CB)), ((w_out, 0), (w_hid, 0)), ((w_q, 0), (w_hid, CB)))
    for k, pair in enumerate(blocks):
        @pl.when(jnp.logical_and(zy == kind, x == k))
        def _(pair=pair):
            for ph, (ref, at) in enumerate(pair):
                pltpu.make_async_copy(
                    ref.at[:, pl.ds(at, bufs[ph][1])], share(ph, zq), loc_sem.at[ph]
                ).start()

    barrier = pltpu.get_barrier_semaphore()

    def greet(k, carry):
        pl.semaphore_signal(barrier, inc=1, device_id=(tm, (node + 2 * k) & 31), device_id_type=MESH)
        pl.semaphore_signal(barrier, inc=1, device_id=((tm + k) & 15, node), device_id_type=MESH)
        return carry

    lax.fori_loop(1, 16, greet, 0)
    pl.semaphore_signal(barrier, inc=1, device_id=sibling, device_id_type=MESH)

    for i in range(11):
        copy_in(i).start()
    pl.semaphore_wait(barrier, 31)

    @pl.when(zy == kind)
    def _():
        for ph in range(2):
            def send(i, carry, ph=ph):
                k = jnp.where((i & 1) == 0, 8 - (i >> 1), 8 + ((i + 1) >> 1))
                pltpu.make_async_remote_copy(
                    src_ref=share(ph, zq), dst_ref=share(ph, zq),
                    send_sem=s1_send.at[ph], recv_sem=s1_recv.at[ph, zq],
                    device_id=(tm, ((z + k) & 15) * 2 + c), device_id_type=MESH,
                ).start()
                return carry
            pltpu.make_async_copy(share(ph, zq), share(ph, zq), loc_sem.at[ph]).wait()
            lax.fori_loop(0, 15, send, 0)

    def stage1_wait(ph):
        for q in range(4):
            @pl.when(4 * q + kind != z)
            def _(q=q):
                pltpu.make_async_copy(share(ph, q), share(ph, q), s1_recv.at[ph, q]).wait()

    def piece(ph, aa, bb, part=None):
        buf, _ = bufs[ph]
        xx, yy = pick(aa, bb), pick(bb, (aa + 2) & 3)
        rows = pl.ds(0, 4) if part is None else pl.ds(2 * part, 2)
        return buf.at[xx, rows, yy, c]

    def send_piece(ph, aa, bb, device, send_sem, part=None, slot=0):
        ref = piece(ph, aa, bb, part)
        pltpu.make_async_remote_copy(
            src_ref=ref, dst_ref=ref, send_sem=send_sem.at[ph],
            recv_sem=piece_sem.at[ph, aa * 4 + bb, slot],
            device_id=device, device_id_type=MESH,
        ).start()

    def wait_piece(ph, aa, bb, part=None, slot=0):
        ref = piece(ph, aa, bb, part)
        pltpu.make_async_copy(ref, ref, piece_sem.at[ph, aa * 4 + bb, slot]).wait()

    def to_sibling(ph, bb):
        buf, _ = bufs[ph]

        def send(ref):
            pltpu.make_async_remote_copy(
                src_ref=ref, dst_ref=ref, send_sem=sib_send.at[ph], recv_sem=sib_recv.at[ph],
                device_id=sibling, device_id_type=MESH,
            ).start()

        @pl.when(c == 0)
        def _():
            send(buf.at[:, :, bb, 0])

        @pl.when(c == 1)
        def _():
            send(buf.at[bb, :, :, 1])

    def second_ring(ph, aa):
        send_piece(ph, aa, b, dev_b_left, r2_send)
        send_piece(ph, aa, b, dev_b_right, r2_send)

    def step0(ph):
        stage1_wait(ph)
        send_piece(ph, a, b, dev_a_left, r1_send)
        send_piece(ph, a, b, dev_a_right, r1_send)
        second_ring(ph, a)

    def step1(ph):
        wait_piece(ph, a_left, b)
        send_piece(ph, a_left, b, dev_a_right, r1_send, 0, 0)
        second_ring(ph, a_left)
        wait_piece(ph, a_right, b)
        send_piece(ph, a_right, b, dev_a_left, r1_send, 1, 1)
        second_ring(ph, a_right)

    def step2(ph):
        wait_piece(ph, a_far, b, 0, 0)
        wait_piece(ph, a_far, b, 1, 1)
        second_ring(ph, a_far)
        to_sibling(ph, b)

    def step3(ph):
        for aa in (a, a_left, a_right, a_far):
            wait_piece(ph, aa, b_left)
            send_piece(ph, aa, b_left, dev_b_right, r2_send, 0, 0)
            wait_piece(ph, aa, b_right)
            send_piece(ph, aa, b_right, dev_b_left, r2_send, 1, 1)
        to_sibling(ph, b_left)
        to_sibling(ph, b_right)

    def step4(ph):
        for aa in (a, a_left, a_right, a_far):
            wait_piece(ph, aa, b_far, 0, 0)
            wait_piece(ph, aa, b_far, 1, 1)
        to_sibling(ph, b_far)

    def all_here(ph):
        ref = bufs[ph][0].at[:, :, :, other]
        pltpu.make_async_copy(ref, ref, sib_recv.at[ph]).wait()

    def widen(i, carry):
        at = pl.ds(pl.multiple_of(i * 64, 64), 64)
        for t in range(4):
            rbuf[t, at, :] = nbr[at, t * 128 : (t + 1) * 128].astype(F32)
        return carry

    for i in range(6):
        copy_in(i).wait()
    lax.fori_loop(0, READS // 64, widen, 0)
    tpack[0:6, :] = (ev_time[...] - nb_time[...]).astype(F32)
    tpack[6:7, :] = nb_count[...].astype(F32)
    tpack[7:8, :] = jnp.zeros((1, EV), F32)
    tcol[...] = jnp.transpose(tpack[...])
    lanes = lax.broadcasted_iota(jnp.int32, (1, D), 1).astype(F32)
    freq = jnp.exp(lanes * (-9.0 * math.log(10.0) / D))

    def make_keys(i, carry):
        at = pl.ds(pl.multiple_of(i * 16, 16), 16)
        gaps = tcol[at, :]
        for j in range(SLOTS):
            gap = gaps[:, j : j + 1]
            for t, cosine in enumerate((cos_wide, cos_wide, cos_small, cos_small)):
                cut = slice(t * 128, (t + 1) * 128)
                rows = rbuf[t, pl.ds(i * (16 * SLOTS) + j, 16, stride=SLOTS), :]
                keys[j, at, cut] = rows + cosine(gap * freq[:, cut])
        return carry

    lax.fori_loop(0, EV // 16, make_keys, 0)

    for i in range(6, 11):
        copy_in(i).wait()

    step0(1)
    step0(0)

    for k in range(READS // 128):
        idp[k : k + 1, :] = (owner[:, k * 128 : (k + 1) * 128] * OWN + vrow[k : k + 1, :]).astype(F32)
    idp[12:16, :] = jnp.zeros((4, 128), F32)
    columns = jnp.transpose(idp[...])
    for k in range(READS // 128):
        vcol[k * 128 : (k + 1) * 128, :] = jnp.broadcast_to(columns[:, k : k + 1], (128, 128))
    for j in range(SLOTS):
        vids[j : j + 1, :] = jnp.transpose(vcol[pl.ds(j, EV, stride=SLOTS), :])[0:1, :]

    step1(1)
    step1(0)
    step2(1)
    step2(0)
    step3(1)
    step3(0)
    step4(1)
    step4(0)

    def wide(ref, start, width):
        size = ref.shape[-1]
        out = []
        while width:
            block, at = divmod(start, size)
            take = min(width, size - at)
            out.append(ref[block, :, :, :, :, at : at + take].reshape(D, take))
            start, width = start + take, width - take
        return out[0] if len(out) == 1 else jnp.concatenate(out, axis=1)

    all_here(1)

    def gate(k):
        return (nn(msg[...], wide(wb, k * D, D)), nn(dst[...], wide(wb, 1536 + k * D, D)))

    gi, gh = gate(0)
    gates[0] = sigmoid(gi + gh)
    gi, gh = gate(2)
    gates[3] = gh
    gates[2] = jnp.tanh(gi + gates[0] * gh)
    gi, gh = gate(1)
    update = sigmoid(gi + gh)
    gates[1] = update
    mem[...] = ((1.0 - update) * gates[2] + update * dst[...].astype(F32)).astype(BF16)

    all_here(0)

    gatt = nt(emb[...], wide(wa, 1024, 512)).astype(BF16)
    for h in range(2):
        gv[h] = nt(gatt[:, h * HEAD : (h + 1) * HEAD], wide(wa, 512 + h * HEAD, HEAD))

    lane16 = lax.broadcasted_iota(jnp.int32, (16, 128), 1)

    def row_dots(vec, out):
        def block(i, carry):
            at = pl.ds(pl.multiple_of(i * 16, 16), 16)
            acc = jnp.zeros((16, 128), F32)
            v0, v1 = vec[0, at, :], vec[1, at, :]
            for j in range(SLOTS):
                key = keys[j, at, :]
                for h, v in enumerate((v0, v1)):
                    prod = key * v
                    part = (prod[:, 0:128] + prod[:, 128:256]) + (prod[:, 256:384] + prod[:, 384:512])
                    acc = jnp.where(lane16 == h * SLOTS + j, jnp.sum(part, axis=1, keepdims=True), acc)
            out[at, :] = acc
            return carry
        lax.fori_loop(0, EV // 16, block, 0)

    row_dots(gv, gwp)

    quer = nn(mem[...], wide(wa, 1536, 512)).astype(BF16)
    for h in range(2):
        qk[h] = nt(quer[:, h * HEAD : (h + 1) * HEAD], wide(wa, h * HEAD, HEAD))

    row_dots(qk, scp)

    lane = lax.broadcasted_iota(jnp.int32, (EV, 128), 1)
    slot = jnp.where(lane >= SLOTS, lane - SLOTS, lane).astype(F32)
    head0, head1 = lane < SLOTS, jnp.logical_and(lane >= SLOTS, lane < 2 * SLOTS)
    live = jnp.logical_and(lane < 2 * SLOTS, slot < tcol[:, 6:7])
    raw = jnp.where(live, jnp.exp(scp[...] * (1.0 / 16.0)), 0.0)

    def per_head(v):
        s0 = jnp.sum(jnp.where(head0, v, 0.0), axis=1, keepdims=True)
        s1 = jnp.sum(jnp.where(head1, v, 0.0), axis=1, keepdims=True)
        return jnp.where(head0, s0, s1)

    weight = raw / per_head(raw)
    gw = gwp[...]
    wtp[...] = weight
    scp[...] = weight * (gw - per_head(weight * gw)) * (1.0 / 16.0)

    def gather_slots(i, carry):
        at = pl.ds(pl.multiple_of(i * 16, 16), 16)
        sc = scp[at, :]
        c0 = jnp.zeros((16, D), F32)
        c1 = jnp.zeros((16, D), F32)
        for j in range(SLOTS):
            key = keys[j, at, :]
            c0 = c0 + sc[:, j : j + 1] * key
            c1 = c1 + sc[:, SLOTS + j : SLOTS + j + 1] * key
        ctx[0, at, :] = c0.astype(BF16)
        ctx[1, at, :] = c1.astype(BF16)
        return carry

    lax.fori_loop(0, EV // 16, gather_slots, 0)
    gq = [nn(ctx[h], wide(wa, h * HEAD, HEAD)).astype(BF16) for h in range(2)]
    gmem[...] = emb[...].astype(F32) + (
        nt(gq[0], wide(wa, 1536, HEAD)) + nt(gq[1], wide(wa, 1536 + HEAD, HEAD))
    )

    def gru(i, carry):
        at = pl.ds(pl.multiple_of(i * 16, 16), 16)
        gm = gmem[at, :]
        r, u, cand, hc = gates[0, at, :], gates[1, at, :], gates[2, at, :], gates[3, at, :]
        gu = gm * (dst[at, :].astype(F32) - cand)
        gc = gm * (1.0 - u) * (1.0 - cand * cand)
        gin[at, 0:512] = (gc * hc * (r * (1.0 - r))).astype(BF16)
        gin[at, 512:1024] = (gu * (u * (1.0 - u))).astype(BF16)
        gin[at, 1024:1536] = gc.astype(BF16)
        gcand[at, :] = (gc * r).astype(BF16)
        gmem[at, :] = gm * u
        return carry

    lax.fori_loop(0, EV // 16, gru, 0)

    gmsg[...] = nt(gin[...], wide(wb, 0, 1536)).astype(BF16)

    def part_copy(g):
        return pltpu.make_async_remote_copy(
            src_ref=npart.at[g, other], dst_ref=nsib.at[g], send_sem=nd_send.at[g], recv_sem=nd_recv.at[g],
            device_id=sibling, device_id_type=MESH,
        )

    for g, offsets in enumerate(FAR):
        base = ((z + offsets[0]) & 15) * 64
        wanted = (lax.broadcasted_iota(jnp.int32, (256, EV), 0) + base) & 1023
        hot = (wanted == src_id[...]).astype(F32).astype(BF16)
        sums = nn(hot, gmsg[...]).astype(BF16).reshape(4, 2, OWN, D)
        npart[g, 0] = sums[:, 0]
        npart[g, 1] = sums[:, 1]
        part_copy(g).start()

    def mine(rel):
        for g, offsets in enumerate(FAR):
            if rel in offsets:
                k = offsets.index(rel)
                return npart[g, c, k].astype(F32) + nsib[g, k].astype(F32)

    chains = (((8, 9, 10, 11), -1, -5), ((7, 6, 5), 1, 5), ((12, 13, 14, 15), -1, -1), ((4, 3, 2, 1), 1, 1))

    def hop(way, s):
        steps, near, last = chains[way]
        to = (z + (last if s == len(steps) - 1 else near) + 16) & 15
        return pltpu.make_async_remote_copy(
            src_ref=nsend.at[way, s], dst_ref=nrecv.at[way, s],
            send_sem=ring_send.at[way, s], recv_sem=ring_recv.at[way, s],
            device_id=(tm, to * 2 + c), device_id_type=MESH,
        )

    def chain_step(way, s):
        total = mine(chains[way][0][s])
        if s > 0:
            hop(way, s - 1).wait_recv()
            total = total + nrecv[way, s - 1].astype(F32)
        nsend[way, s] = total.astype(BF16)
        hop(way, s).start()

    def chain_steps(s):
        for way in range(4):
            if s < len(chains[way][0]):
                chain_step(way, s)

    def spread(i, carry):
        at = pl.ds(pl.multiple_of(i * 16, 16), 16)
        sc, wt = scp[at, :], wtp[at, :]
        for j in range(SLOTS):
            s0, s1 = sc[:, j : j + 1], sc[:, SLOTS + j : SLOTS + j + 1]
            w0, w1 = wt[:, j : j + 1], wt[:, SLOTS + j : SLOTS + j + 1]
            gkb[j, at, :] = (
                (s0 * qk[0, at, :] + s1 * qk[1, at, :]) + (w0 * gv[0, at, :] + w1 * gv[1, at, :])
            ).astype(BF16)
        return carry

    def version_sums(m):
        wanted = (lax.broadcasted_iota(jnp.int32, (256, 128), 0) + 256 * m).astype(F32)
        ids = []
        for k in range(READS // 128):
            vid = vids[k // 2 : k // 2 + 1, (k % 2) * 128 : (k % 2) * 128 + 128]
            ids.append((wanted == vid).astype(F32).astype(BF16))
        sums = nn(jnp.concatenate(ids, axis=1), gkb[...].reshape(READS, D)).astype(BF16)
        vpart[pl.ds(8 * m, 8)] = sums.reshape(8, OWN, D)
        for i in range(8):
            to = 8 * m + ((tm + i) & 7)

            @pl.when(to != tm)
            def _(to=to):
                pltpu.make_async_remote_copy(
                    src_ref=vpart.at[to], dst_ref=vbuf.at[(to - tm + 15) & 15],
                    send_sem=v_send, recv_sem=v_recv,
                    device_id=(to, node), device_id_type=MESH,
                ).start()

    lax.fori_loop(0, EV // 32, spread, 0)
    for g in range(3):
        part_copy(g).wait()
    chain_steps(0)
    lax.fori_loop(EV // 32, EV // 16, spread, 0)
    version_sums(0)
    part_copy(3).wait()
    chain_steps(1)
    version_sums(1)
    chain_steps(2)

    gdst = (nt(gin[:, 0:1024], wide(wb, 1536, 1024)) + nt(gcand[...], wide(wb, 2560, 512))) + gmem[...]
    hot = (lax.broadcasted_iota(jnp.int32, (OWN, EV), 0) == dst_loc[...]).astype(F32).astype(BF16)
    dpart[...] = mine(0) + nn(hot, gdst.astype(BF16))
    chain_steps(3)

    ends = [(way, len(chains[way][0]) - 1) for way in range(4)]
    for way, s in ends:
        hop(way, s).wait_recv()
    node_out[...] = dpart[...] + (
        (nrecv[0, 3].astype(F32) + nrecv[1, 2].astype(F32)) + (nrecv[2, 3].astype(F32) + nrecv[3, 3].astype(F32))
    )
    pltpu.make_async_copy(vbuf, vbuf, v_recv).wait()
    total = vpart[tm].astype(F32)
    for k in range(15):
        total = total + vbuf[k].astype(F32)
    ver_out[...] = total

    for way in range(4):
        for s in range(len(chains[way][0])):
            hop(way, s).wait_send()
    pltpu.make_async_copy(vbuf, vbuf, v_send).wait()
    for ph, (buf, _) in enumerate(bufs):
        ref = buf.at[:, :, :, c]
        pltpu.make_async_copy(ref, ref, sib_send.at[ph]).wait()
        ref = buf.at[0:3, :, 0, c]
        pltpu.make_async_copy(ref, ref, r1_send.at[ph]).wait()
        ref = buf.at[0:3, :, :, c]
        pltpu.make_async_copy(ref, ref, r2_send.at[ph]).wait()

    @pl.when(zy == kind)
    def _():
        ref = wb.at[0:3, :, 0, 0, :, 0:640]
        pltpu.make_async_copy(ref, ref, s1_send.at[0]).wait()
        ref = wb.at[0:3, 0:3, 0, :, :, 0:640]
        pltpu.make_async_copy(ref, ref, s1_send.at[1]).wait()


def hand_out(ver_in, node_in, ver_out, node_out):
    ver_out[...] = ver_in[...]
    node_out[...] = node_in[...]


def body(
    message, dest_mem, nbr_rows, emb_grad, event_time, nbr_time, nbr_count, source_id, dest_local,
    read_owner, read_row, w_in, w_hid, w_query, w_keyval, w_out,
):
    vmem = pl.BlockSpec(memory_space=pltpu.VMEM)
    hbm = pl.BlockSpec(memory_space=pl.ANY)
    dma = pltpu.SemaphoreType.DMA
    scratch = [
        pltpu.VMEM((EV, D), BF16),
        pltpu.VMEM((EV, D), BF16),
        pltpu.VMEM((READS, D), BF16),
        pltpu.VMEM((EV, D), BF16),
        pltpu.VMEM((1, EV), jnp.int32),
        pltpu.VMEM((SLOTS, EV), jnp.int32),
        pltpu.VMEM((1, EV), jnp.int32),
        pltpu.VMEM((1, EV), jnp.int32),
        pltpu.VMEM((1, EV), jnp.int32),
        pltpu.VMEM((1, READS), jnp.int32),
        pltpu.VMEM((READS // 128, 128), jnp.int32),
        pltpu.VMEM((4, 4, 4, 2, 16, CA), BF16),
        pltpu.VMEM((4, 4, 4, 2, 16, CB), BF16),
        pltpu.VMEM((4, READS, 128), F32),
        pltpu.VMEM((SLOTS, EV, D), F32),
        pltpu.VMEM((SLOTS, EV, D), BF16),
        pltpu.VMEM((2, EV, D), F32),
        pltpu.VMEM((2, EV, D), F32),
        pltpu.VMEM((2, EV, D), BF16),
        pltpu.VMEM((4, EV, D), F32),
        pltpu.VMEM((EV, D), BF16),
        pltpu.VMEM((EV, D), F32),
        pltpu.VMEM((EV, 3 * D), BF16),
        pltpu.VMEM((EV, D), BF16),
        pltpu.VMEM((EV, D), BF16),
        pltpu.VMEM((EV, 8), F32),
        pltpu.VMEM((8, EV), F32),
        pltpu.VMEM((EV, 128), F32),
        pltpu.VMEM((EV, 128), F32),
        pltpu.VMEM((EV, 128), F32),
        pltpu.VMEM((16, OWN, D), BF16),
        pltpu.VMEM((15, OWN, D), BF16),
        pltpu.VMEM((4, 2, 4, OWN, D), BF16),
        pltpu.VMEM((4, 4, OWN, D), BF16),
        pltpu.VMEM((4, 4, OWN, D), BF16),
        pltpu.VMEM((4, 4, OWN, D), BF16),
        pltpu.VMEM((OWN, D), F32),
        pltpu.VMEM((READS, 128), F32),
        pltpu.VMEM((8, EV), F32),
        pltpu.VMEM((16, 128), F32),
        dma((11,)),
        dma((2,)),
        dma((2,)),
        dma((2, 4)),
        dma((2,)),
        dma((2,)),
        dma((2, 16, 2)),
        dma((2,)),
        dma((2,)),
        dma,
        dma,
        dma((4,)),
        dma((4,)),
        dma((4, 4)),
        dma((4, 4)),
    ]
    version_grad, node_grad = pl.pallas_call(
        kernel,
        out_shape=(jax.ShapeDtypeStruct((OWN, D), F32), jax.ShapeDtypeStruct((OWN, D), F32)),
        in_specs=[hbm] * 16,
        out_specs=(vmem, vmem),
        scratch_shapes=scratch,
        compiler_params=pltpu.CompilerParams(
            collective_id=0, has_side_effects=True, vmem_limit_bytes=56 * 1024 * 1024
        ),
        cost_estimate=pl.CostEstimate(
            flops=4_000_000_000, bytes_accessed=8_000_000, transcendentals=1_000_000
        ),
    )(
        message, dest_mem, nbr_rows, emb_grad,
        event_time.reshape(1, EV), nbr_time.T, nbr_count.reshape(1, EV),
        source_id.reshape(1, EV), dest_local.reshape(1, EV),
        read_owner.reshape(1, READS), read_row.reshape(READS // 128, 128),
        w_in, w_hid, w_query, w_keyval, w_out,
    )
    version_grad, node_grad = pl.pallas_call(
        hand_out,
        out_shape=(jax.ShapeDtypeStruct((OWN, D), F32), jax.ShapeDtypeStruct((OWN, D), F32)),
        in_specs=[vmem] * 2,
        out_specs=(vmem, vmem),
        compiler_params=pltpu.CompilerParams(vmem_limit_bytes=60 * 1024 * 1024),
    )(version_grad, node_grad)
    return version_grad, node_grad[None]


def solution(mesh):
    both = P(("tm", "node"))
    in_specs = (
        (P(("tm", "node"), None),) * 4
        + (both, P(("tm", "node"), None), both, both, both, P(("tm", "node"), None), both)
        + (P("node", None),) * 5
    )
    out_specs = (P(("tm", "node"), None), P("tm", "node", None))
    return jax.shard_map(body, mesh=mesh, in_specs=in_specs, out_specs=out_specs, check_vma=False)
```
